128 devices in a mesh: bucket: 32 (over z, x_lo, y), seq: 4 (over x_hi, core).
Axes of the slice: x: 4 (x_hi: 2, x_lo: 2; x = x_hi * 2 + x_lo), y: 4, z: 4, core: 2. Of those that a mesh axis runs over, the one named last changes fastest.
Arguments:
- tokens: bfloat16 [32, 1024, 1024], P('bucket', 'seq'), may hold values from -6 to 6
- condition: bfloat16 [32, 1024], P('bucket'), may hold values from -6 to 6
- lengths: int32 [32, 2], P('bucket'), may hold values from 64 to 896, as said below
- head_mask: int32 [32, 16], P('bucket'), may hold values 0 or 1
- group_mask: int32 [32, 16], P('bucket'), may hold values 0 or 1
- token_mask: int32 [32, 1024], P('bucket', 'seq'), may hold values 0 or 1
- ada_weight: bfloat16 [1024, 6144], replicated, may hold values from -0.1875 to 0.1875
- ada_bias: bfloat16 [6144], replicated, may hold values from -3 to 3
- qkv_weight: bfloat16 [1024, 3072], replicated, may hold values from -0.1875 to 0.1875
- qv_bias: bfloat16 [2048], replicated, may hold values from -3 to 3
- proj_weight: bfloat16 [1024, 1024], replicated, may hold values from -0.75 to 0.75
- proj_bias: bfloat16 [1024], replicated, may hold values from -3 to 3
- fc1_weight: bfloat16 [1024, 4096], replicated, may hold values from -0.1875 to 0.1875
- fc1_bias: bfloat16 [4096], replicated, may hold values from -3 to 3
- fc2_weight: bfloat16 [4096, 1024], replicated, may hold values from -0.09375 to 0.09375
- fc2_bias: bfloat16 [1024], replicated, may hold values from -3 to 3
- out_grad: bfloat16 [32, 1024, 1024], P('bucket', 'seq'), may hold values from -6 to 6
Outputs:
- block_out: float32 [32, 1024, 1024], P('bucket', 'seq')
- input_grad: float32 [32, 1024, 1024], P('bucket', 'seq')
- cond_grad: float32 [32, 1024], P('bucket')
- ada_weight_grad: float32 [1024, 6144], P('bucket')
- ada_bias_grad: float32 [6144], P('bucket')
- qkv_weight_grad: float32 [1024, 3072], P('bucket')
- qv_bias_grad: float32 [2048], P('bucket')
- proj_weight_grad: float32 [1024, 1024], P('bucket')
- proj_bias_grad: float32 [1024], P('bucket')
- fc1_weight_grad: float32 [1024, 4096], P('bucket')
- fc1_bias_grad: float32 [4096], P('bucket')
- fc2_weight_grad: float32 [4096, 1024], P('bucket')
- fc2_bias_grad: float32 [1024], P('bucket')
The draws below stay inside these ranges and needn't reach their ends.
Inputs may be any that keep to these rules, and one draw needn't show every extreme that they name: `lengths`: lengths of a bucket's two items in the order in which they lie in its row from position 0; they sum to 960, so the last 64 positions of every row are padding.
All inputs are finite; a program needn't handle non-finite values. No bound on the sum of `head_mask` or of `group_mask` or of `token_mask` on one device may be relied on, other than what follows from the above.
Results may differ from the reference program's by a relative error of at most 0.025.
Values may be sent and summed in bfloat16 or wider, within the bound.
A program may use at most 256 MiB of HBM per device.

```python
import jax
import jax.numpy as jnp
from jax import lax

D = 1024
FF = 4096
HEADS = 16
GROUPS = 16
HEAD_DIM = 64
ROW = 1024
BUCKETS = 32


def draw_lengths(key, part):
    key = jax.random.fold_in(key, 11)
    key_short, key_rank, key_order = jax.random.split(key, 3)
    lowest = ROW // 16
    highest = ROW // 8
    short_len = jax.random.randint(key_short, (BUCKETS,), lowest, highest + 1)
    ranking = jax.random.permutation(key_rank, BUCKETS)
    short_len = jnp.where(ranking == 0, lowest, jnp.where(ranking == 1, highest, short_len))
    long_len = ROW - ROW // 16 - short_len
    order_bit = jax.random.randint(key_order, (BUCKETS,), 0, 2)
    first_len = jnp.where(order_bit == 0, long_len, short_len)
    second_len = long_len + short_len - first_len
    return jnp.stack([first_len, second_len], axis=1).astype(jnp.int32)


def touch_ends(result, stream_key, least, high):
    spot = [jax.random.randint(jax.random.fold_in(stream_key, axis), (), 0, length) for axis, length in enumerate(result.shape)]
    main_axis = result.shape.index(max(result.shape))
    next_to = spot[:main_axis] + [(spot[main_axis] + 1) % result.shape[main_axis]] + spot[main_axis + 1:]
    return result.at[tuple(spot)].set(least).at[tuple(next_to)].set(high)


def steps_of(stream_key, extent, cuts, low, high):
    loudness = 1.0
    for dim, blocks in cuts:
        draws = jax.random.uniform(jax.random.fold_in(jax.random.fold_in(stream_key, 6), dim), (blocks,), jnp.float32, low / len(cuts), high / len(cuts))
        loudness = loudness * jnp.repeat(jnp.exp(draws), extent[dim] // blocks).reshape((-1,) + (1,) * (len(extent) - 1 - dim))
    return loudness


def normal_values(key, extent, deviation, most, cuts=(), kind=jnp.bfloat16):
    array = deviation * jax.random.normal(key, extent, jnp.float32)
    if cuts:
        array = array * steps_of(key, extent, cuts, -0.22, 0.18)
    return jnp.clip(array, -most, most).astype(kind)


def setup_inputs(seed: int = 0) -> dict:
    streams_of = jax.random.split(jax.random.key(seed), 18)
    return {
        "tokens": normal_values(streams_of[0], (BUCKETS, ROW, D), 1.0, 6.0, ((0, 32), (1, 4))),
        "condition": normal_values(streams_of[1], (BUCKETS, D), 1.0, 6.0, ((0, 32),)),
        "lengths": draw_lengths(jax.random.fold_in(streams_of[17], 71), 0),
        "head_mask": touch_ends((jax.random.randint(streams_of[3], (BUCKETS, HEADS), 0, 4) < 3).astype(jnp.int32), jax.random.fold_in(streams_of[3], 1), 0, 1),
        "group_mask": touch_ends((jax.random.randint(streams_of[4], (BUCKETS, GROUPS), 0, 4) < 3).astype(jnp.int32), jax.random.fold_in(streams_of[4], 1), 0, 1),
        "token_mask": touch_ends((jax.random.randint(streams_of[5], (BUCKETS, ROW), 0, 4) < 3).astype(jnp.int32), jax.random.fold_in(streams_of[5], 1), 0, 1),
        "ada_weight": normal_values(streams_of[6], (D, 6 * D), D ** -0.5, 0.1875),
        "ada_bias": normal_values(streams_of[7], (6 * D,), 0.5, 3.0),
        "qkv_weight": normal_values(streams_of[8], (D, 3 * D), D ** -0.5, 0.1875),
        "qv_bias": normal_values(streams_of[9], (2 * D,), 0.5, 3.0),
        "proj_weight": normal_values(streams_of[10], (D, D), (D // 16) ** -0.5, 0.75),
        "proj_bias": normal_values(streams_of[11], (D,), 0.5, 3.0),
        "fc1_weight": normal_values(streams_of[12], (D, FF), D ** -0.5, 0.1875),
        "fc1_bias": normal_values(streams_of[13], (FF,), 0.5, 3.0),
        "fc2_weight": normal_values(streams_of[14], (FF, D), FF ** -0.5, 0.09375),
        "fc2_bias": normal_values(streams_of[15], (D,), 0.5, 3.0),
        "out_grad": normal_values(streams_of[16], (BUCKETS, ROW, D), 1.0, 6.0, ((0, 32), (1, 4))),
    }


@jax.custom_vjp
def low(v):
    return lax.optimization_barrier(v.astype(jnp.bfloat16)).astype(jnp.float32)

@jax.custom_vjp
def low_back(v):
    return v

def low_keep(v):
    return (low(v), None)

def low_pass(kept, grad):
    return (grad,)

def back_keep(v):
    return (v, None)

def back_low(kept, grad):
    return (low(grad),)
low.defvjp(low_keep, low_pass)
low_back.defvjp(back_keep, back_low)

def matmul(first_op, second_op):
    return jnp.dot(first_op, second_op, precision=lax.Precision.HIGHEST)

def normalize(values):
    centred = values - lax.optimization_barrier(jnp.mean(values, axis=-1, keepdims=True))
    return centred * lax.rsqrt(lax.optimization_barrier(jnp.mean(centred * centred, axis=-1, keepdims=True)) + 1e-06)

def gelu_tanh(values):
    return 0.5 * values * (1.0 + jnp.tanh(0.7978845608028654 * (values + 0.044715 * values * values * values)))

def one_bucket(weights, inputs):
    ada_weight, ada_bias, qkv_weight, qv_bias, proj_weight, proj_bias, fc1_weight, fc1_bias, fc2_weight, fc2_bias = weights
    tokens, condition, lengths, head_mask, group_mask, token_mask = inputs
    positions = jnp.arange(ROW, dtype=jnp.int32)
    first_end = lengths[0]
    both_end = lengths[0] + lengths[1]
    segment = (positions >= first_end).astype(jnp.int32) + (positions >= both_end).astype(jnp.int32)
    allowed = segment[:, None] == segment[None, :]
    valid_rows = (positions < both_end).astype(jnp.float32)[:, None]
    kept_rows = valid_rows * token_mask.astype(jnp.float32)[:, None]
    channel_mask = jnp.repeat(group_mask.astype(jnp.float32), FF // GROUPS)
    silu_low = low(jax.nn.silu(condition))
    modulation = low_back(matmul(silu_low[None, :], ada_weight))[0] + ada_bias
    shift_one, scale_one, gate_one, shift_two, scale_two, gate_two = jnp.split(modulation, 6)
    normed = low(normalize(tokens) * (1.0 + scale_one) + shift_one)
    projected = matmul(normed, qkv_weight)
    queries = low_back(low(projected[:, :D] + qv_bias[:D]))
    key_rows = low_back(low(projected[:, D:2 * D]))
    value_rows = low_back(low(projected[:, 2 * D:] + qv_bias[D:]))
    query_heads = queries.reshape(ROW, HEADS, HEAD_DIM)
    key_heads = key_rows.reshape(ROW, HEADS, HEAD_DIM)
    value_heads = value_rows.reshape(ROW, HEADS, HEAD_DIM)
    raw_scores = low_back(jnp.einsum('qhd,khd->hqk', query_heads, key_heads, precision=lax.Precision.HIGHEST))
    scores = jnp.where(allowed[None], raw_scores * HEAD_DIM ** (-0.5), -1e+30)
    largest = lax.optimization_barrier(jnp.max(scores, axis=-1, keepdims=True))
    log_total = largest + jnp.log(lax.optimization_barrier(jnp.sum(jnp.exp(scores - largest), axis=-1, keepdims=True)))
    probs_low = low(jnp.exp(scores - log_total))
    context = jnp.einsum('hqk,khd->qhd', probs_low, value_heads, precision=lax.Precision.HIGHEST)
    context = context * head_mask.astype(jnp.float32)[None, :, None]
    attended = low_back(low(context.reshape(ROW, D)))
    branch = low_back(matmul(attended, proj_weight) + proj_bias)
    middle = tokens + valid_rows * gate_one * branch
    normed_two = low(normalize(middle) * (1.0 + scale_two) + shift_two)
    hidden = low_back(matmul(normed_two, fc1_weight) + fc1_bias)
    activated = low(gelu_tanh(hidden) * channel_mask)
    mlp_out = low_back(matmul(activated, fc2_weight) + fc2_bias)
    return middle + kept_rows * gate_two * mlp_out

def reference(tokens, condition, lengths, head_mask, group_mask, token_mask, ada_weight, ada_bias, qkv_weight, qv_bias, proj_weight, proj_bias, fc1_weight, fc1_bias, fc2_weight, fc2_bias, out_grad):
    weights = (ada_weight.astype(jnp.float32), ada_bias.astype(jnp.float32), qkv_weight.astype(jnp.float32), qv_bias.astype(jnp.float32), proj_weight.astype(jnp.float32), proj_bias.astype(jnp.float32), fc1_weight.astype(jnp.float32), fc1_bias.astype(jnp.float32), fc2_weight.astype(jnp.float32), fc2_bias.astype(jnp.float32))

    def forward(weight_set, token_values, cond_values):

        def per_bucket(inputs):
            return one_bucket(weight_set, inputs)
        return lax.map(jax.checkpoint(per_bucket), (token_values, cond_values, lengths, head_mask, group_mask, token_mask))
    block_out, pullback = jax.vjp(forward, weights, tokens.astype(jnp.float32), condition.astype(jnp.float32))
    weight_grads, input_grad, cond_grad = pullback(out_grad.astype(jnp.float32))
    return (block_out, input_grad, cond_grad, weight_grads[0], weight_grads[1], weight_grads[2], weight_grads[3], weight_grads[4], weight_grads[5], weight_grads[6], weight_grads[7], weight_grads[8], weight_grads[9])
```

```python
import functools

import jax
import jax.numpy as jnp
from jax import lax
from jax.experimental import pallas as pl
from jax.experimental.pallas import tpu as pltpu
from jax.sharding import PartitionSpec as P


MESH_IDS = pl.DeviceIdType.MESH
AXES = {"x": 0, "y": 1, "z": 2}
ROUTES = ("zyx", "yxz", "xzy")


def place():
    bucket = lax.axis_index("bucket")
    seq = lax.axis_index("seq")
    return (
        (seq // 2) * 2 + (bucket // 4) % 2,
        bucket % 4,
        bucket // 8,
        seq % 2,
    )


def device(x, y, z, core):
    return (z * 8 + (x % 2) * 4 + y, (x // 2) * 2 + core)


def shifted(spot, axis, step):
    x, y, z, core = spot
    if axis == "x":
        x = (x + step) % 4
    elif axis == "y":
        y = (y + step) % 4
    elif axis == "z":
        z = (z + step) % 4
    else:
        core = 1 - core
    return device(x, y, z, core)


def greet(spot, moves):
    barrier = pltpu.get_barrier_semaphore()
    for axis, step in moves:
        pl.semaphore_signal(
            barrier, inc=1, device_id=shifted(spot, axis, step), device_id_type=MESH_IDS
        )
    pl.semaphore_wait(barrier, len(moves))


TORUS = [(axis, step) for axis in "xyz" for step in (1, -1)]


def cut(route, phase, target, spot):
    index = {"z": slice(None), "x": (slice(None), slice(None)), "y": slice(None)}
    axis = route[phase]
    index[axis] = (target % 2, target // 2) if axis == "x" else target
    done = route[:phase]
    parts = []
    if "z" not in done:
        parts.append(index["z"])
    if "x" not in done:
        parts.append(index["x"][0])
    if "y" not in done:
        parts.append(index["y"])
    if "x" not in done:
        parts.append(index["x"][1])
    return tuple(parts)


def left_over(route, phase):
    done = route[:phase]
    dims = []
    if "z" not in done:
        dims.append(4)
    if "x" not in done:
        dims.append(2)
    if "y" not in done:
        dims.append(4)
    if "x" not in done:
        dims.append(2)
    return tuple(dims)


class Piece:
    def __init__(self, source, columns, route, landing, sums, send_sem, recv_sem, spot):
        self.source, self.columns, self.route = source, columns, route
        self.landing, self.sums = landing, sums
        self.send_sem, self.recv_sem, self.spot = send_sem, recv_sem, spot
        self.copies = {}

    def block(self, phase, target, half):
        width = self.columns // 2
        index = cut(self.route, phase, target, self.spot)
        lanes = pl.ds(half * width, width)
        if phase == 0:
            return self.source(index, half * width, width)
        return self.sums[phase - 1].at[index + (slice(None), lanes)]

    def here(self, phase):
        return self.spot[AXES[self.route[phase]]]

    def send(self, phase, slot, ref, step):
        copy = pltpu.make_async_remote_copy(
            src_ref=ref,
            dst_ref=self.landing[phase].at[slot],
            send_sem=self.send_sem.at[phase, slot],
            recv_sem=self.recv_sem.at[phase, slot],
            device_id=shifted(self.spot, self.route[phase], step),
            device_id_type=MESH_IDS,
        )
        copy.start()
        self.copies[phase, slot] = copy

    def first(self, phase):
        a = self.here(phase)
        self.send(phase, 0, self.block(phase, (a + 2) % 4, 0), 1)
        self.send(phase, 1, self.block(phase, (a + 2) % 4, 1), -1)
        self.send(phase, 2, self.block(phase, (a + 1) % 4, 1), 1)
        self.send(phase, 3, self.block(phase, (a + 3) % 4, 0), -1)

    def second(self, phase):
        a = self.here(phase)
        landing = self.landing[phase]
        for slot, step, half in ((0, 1, 0), (1, -1, 1)):
            self.copies[phase, slot].wait_recv()
            add_into(landing.at[slot], [self.block(phase, (a + step) % 4, half)])
            self.send(phase, slot + 4, landing.at[slot], step)

    def third(self, phase):
        a = self.here(phase)
        landing = self.landing[phase]
        width = self.columns // 2
        for slot in (2, 3, 4, 5):
            self.copies[phase, slot].wait_recv()
        for half, slots in ((0, (3, 4)), (1, (2, 5))):
            target = self.sums[phase].at[..., pl.ds(half * width, width)]
            add_into(
                target,
                [landing.at[slots[0]], landing.at[slots[1]]],
                self.block(phase, a, half),
            )

    def finish(self):
        for copy in self.copies.values():
            copy.wait_send()


def add_into(target, others, start=None):
    total = (target if start is None else start)[...].astype(jnp.float32)
    for other in others:
        total = total + other[...].astype(jnp.float32)
    target[...] = total.astype(jnp.bfloat16)


def reduce_kernel(views, *refs):
    count = len(views)
    inputs = max(v[0] for v in views) + 1
    sources, outs = refs[:inputs], refs[inputs : inputs + count]
    scratch = list(refs[inputs + count :])
    send_sem, recv_sem, end_send, end_recv = scratch[-4:]
    spot = place()
    greet(spot, TORUS + [("core", 0), ("x", 2)])
    pieces = []
    for k, (which, kind, offset, columns) in enumerate(views):
        landing, sums = scratch[8 * k : 8 * k + 3], scratch[8 * k + 3 : 8 * k + 6]

        def source(index, start, width, ref=sources[which], kind=kind, offset=offset):
            if kind == "rows":
                return ref.at[index + (offset, slice(None), pl.ds(start, width))]
            return ref.at[index + (slice(None), pl.ds(offset + start, width))]

        pieces.append(
            Piece(
                source, columns, ROUTES[k % 3], landing, sums, send_sem.at[k], recv_sem.at[k], spot
            )
        )
    for piece in pieces:
        piece.first(0)
    for phase in range(3):
        for piece in pieces:
            piece.second(phase)
        for piece in pieces:
            piece.third(phase)
            if phase < 2:
                piece.first(phase + 1)

    def to(k, stage, src, dst, axis, step):
        copy = pltpu.make_async_remote_copy(
            src_ref=src,
            dst_ref=dst,
            send_sem=end_send.at[k, stage],
            recv_sem=end_recv.at[k, stage],
            device_id=shifted(spot, axis, step),
            device_id_type=MESH_IDS,
        )
        copy.start()
        return copy

    near, far = [], []
    for k, piece in enumerate(pieces):
        near.append(to(k, 0, piece.sums[2], scratch[8 * k + 6], "core", 0))
    high = spot[0] // 2
    for k, piece in enumerate(pieces):
        near[k].wait()
        both, there = scratch[8 * k + 6], scratch[8 * k + 7]
        add_into(both, [piece.sums[2]])
        far.append(to(k, 1, both, there, "x", 2))
        outs[k][high] = both[...].astype(jnp.float32)
    for k, piece in enumerate(pieces):
        far[k].wait()
        outs[k][1 - high] = scratch[8 * k + 7][...].astype(jnp.float32)
    for piece in pieces:
        piece.finish()


def reduce_weights(arrays, views, collective_id, name):
    scratch = []
    for k, (_, _, _, columns) in enumerate(views):
        route = ROUTES[k % 3]
        dims = [left_over(route, phase) + (16,) for phase in range(4)]
        for phase in range(3):
            scratch.append(pltpu.VMEM((6,) + dims[phase + 1] + (columns // 2,), jnp.bfloat16))
        for phase in range(3):
            scratch.append(pltpu.VMEM(dims[phase + 1] + (columns,), jnp.bfloat16))
        scratch.append(pltpu.VMEM((16, columns), jnp.bfloat16))
        scratch.append(pltpu.VMEM((16, columns), jnp.bfloat16))
    count = len(views)
    scratch += [pltpu.SemaphoreType.DMA((count, 3, 6))] * 2
    scratch += [pltpu.SemaphoreType.DMA((count, 2))] * 2
    return pl.pallas_call(
        functools.partial(reduce_kernel, views),
        out_shape=[jax.ShapeDtypeStruct((2, 16, v[3]), jnp.float32) for v in views],
        in_specs=[pl.BlockSpec(memory_space=pltpu.VMEM)] * len(arrays),
        out_specs=[pl.BlockSpec(memory_space=pltpu.VMEM)] * count,
        scratch_shapes=scratch,
        compiler_params=pltpu.CompilerParams(
            collective_id=collective_id, has_side_effects=True, vmem_limit_bytes=60 << 20
        ),
        name=name,
    )(*arrays)


def normalize(values):
    centred = values - jnp.mean(values, axis=-1, keepdims=True)
    return centred * lax.rsqrt(jnp.mean(centred * centred, axis=-1, keepdims=True) + 1e-06)


def gelu_tanh(values):
    return (
        0.5
        * values
        * (1.0 + jnp.tanh(0.7978845608028654 * (values + 0.044715 * values * values * values)))
    )


def product(first_op, second_op):
    return jnp.dot(first_op, second_op, preferred_element_type=jnp.float32)


def over_rows(first_op, second_op):
    return lax.dot_general(
        first_op, second_op, (((0,), (0,)), ((), ())), preferred_element_type=jnp.float32
    )


def against(first_op, second_op):
    return lax.dot_general(
        first_op, second_op, (((1,), (1,)), ((), ())), preferred_element_type=jnp.float32
    )


def segment_ids(positions, first_end, both_end):
    return (positions >= first_end).astype(jnp.int32) + (positions >= both_end).astype(jnp.int32)


def masked_scores(query_heads, key_heads, allowed, score_scale):
    raw_scores = jnp.einsum(
        "qhd,khd->hqk", query_heads, key_heads, preferred_element_type=jnp.float32
    )
    return jnp.where(allowed[None], raw_scores * score_scale, -1e30)


def local(
    tokens,
    condition,
    lengths,
    head_mask,
    group_mask,
    token_mask,
    ada_weight,
    ada_bias,
    qkv_weight,
    qv_bias,
    proj_weight,
    proj_bias,
    fc1_weight,
    fc1_bias,
    fc2_weight,
    fc2_bias,
    out_grad,
):
    model_width = tokens.shape[2]
    local_rows = tokens.shape[1]
    full_rows = local_rows * lax.axis_size("seq")
    heads_count = head_mask.shape[1]
    head_width = model_width // heads_count
    score_scale = head_width ** (-0.5)
    row_start = lax.axis_index("seq") * local_rows
    local_pos = row_start + jnp.arange(local_rows, dtype=jnp.int32)
    all_pos = jnp.arange(full_rows, dtype=jnp.int32)
    first_end = lengths[0, 0]
    both_end = lengths[0, 0] + lengths[0, 1]
    allowed = (
        segment_ids(local_pos, first_end, both_end)[:, None]
        == segment_ids(all_pos, first_end, both_end)[None, :]
    )
    valid_rows = (local_pos < both_end).astype(jnp.float32)[:, None]
    kept_rows = valid_rows * token_mask[0].astype(jnp.float32)[:, None]
    head_keep = head_mask[0].astype(jnp.bfloat16)[None, :, None]
    channel_mask = jnp.repeat(
        group_mask[0].astype(jnp.float32), fc1_weight.shape[1] // group_mask.shape[1]
    )
    inputs = tokens[0].astype(jnp.float32)
    upstream = out_grad[0].astype(jnp.float32)
    silu_value, silu_back = jax.vjp(jax.nn.silu, condition[0].astype(jnp.float32))
    silu_low = silu_value.astype(jnp.bfloat16)
    modulation = product(silu_low[None, :], ada_weight)[0] + ada_bias.astype(jnp.float32)
    shift_one, scale_one, gate_one, shift_two, scale_two, gate_two = jnp.split(modulation, 6)
    normed_one, norm_back_one = jax.vjp(normalize, inputs)
    normed = (normed_one * (1.0 + scale_one) + shift_one).astype(jnp.bfloat16)
    projected = product(normed, qkv_weight)
    bias_values = qv_bias.astype(jnp.float32)
    queries = (projected[:, :model_width] + bias_values[:model_width]).astype(jnp.bfloat16)
    key_rows = projected[:, model_width : 2 * model_width].astype(jnp.bfloat16)
    value_rows = (projected[:, 2 * model_width :] + bias_values[model_width:]).astype(jnp.bfloat16)
    key_all, value_all = (
        lax.all_gather(key_rows, "seq", axis=0, tiled=True),
        lax.all_gather(value_rows, "seq", axis=0, tiled=True),
    )
    query_heads = queries.reshape(local_rows, heads_count, head_width)
    key_heads = key_all.reshape(full_rows, heads_count, head_width)
    value_heads = value_all.reshape(full_rows, heads_count, head_width)
    scores = masked_scores(query_heads, key_heads, allowed, score_scale)
    largest = jnp.max(scores, axis=-1, keepdims=True)
    log_total = largest + jnp.log(jnp.sum(jnp.exp(scores - largest), axis=-1, keepdims=True))
    probs_low = jnp.exp(scores - log_total).astype(jnp.bfloat16)
    context = jnp.einsum("hqk,khd->qhd", probs_low, value_heads, preferred_element_type=jnp.float32)
    attended = (context * head_keep).reshape(local_rows, model_width).astype(jnp.bfloat16)
    branch = product(attended, proj_weight) + proj_bias.astype(jnp.float32)
    middle = inputs + valid_rows * gate_one * branch
    normed_mid, norm_back_two = jax.vjp(normalize, middle)
    normed_two = (normed_mid * (1.0 + scale_two) + shift_two).astype(jnp.bfloat16)
    hidden = product(normed_two, fc1_weight) + fc1_bias.astype(jnp.float32)
    gelu_value, gelu_back = jax.vjp(gelu_tanh, hidden)
    activated = (gelu_value * channel_mask).astype(jnp.bfloat16)
    mlp_out = product(activated, fc2_weight) + fc2_bias.astype(jnp.float32)
    block_out = middle + kept_rows * gate_two * mlp_out
    mlp_grad = (kept_rows * gate_two * upstream).astype(jnp.bfloat16)
    gate_two_grad = jnp.sum(kept_rows * mlp_out * upstream, axis=0)
    fc2_w_grad = over_rows(activated, mlp_grad)
    fc2_b_grad = jnp.sum(mlp_grad.astype(jnp.float32), axis=0)
    hidden_grad = gelu_back(against(mlp_grad, fc2_weight) * channel_mask)[0].astype(jnp.bfloat16)
    fc1_w_grad = over_rows(normed_two, hidden_grad)
    fc1_b_grad = jnp.sum(hidden_grad.astype(jnp.float32), axis=0)
    normed_two_grad = against(hidden_grad, fc1_weight)
    shift_two_grad = jnp.sum(normed_two_grad, axis=0)
    scale_two_grad = jnp.sum(normed_two_grad * normed_mid, axis=0)
    middle_grad = upstream + norm_back_two(normed_two_grad * (1.0 + scale_two))[0]
    branch_grad = (valid_rows * gate_one * middle_grad).astype(jnp.bfloat16)
    gate_one_grad = jnp.sum(valid_rows * branch * middle_grad, axis=0)
    proj_w_grad = over_rows(attended, branch_grad)
    proj_b_grad = jnp.sum(branch_grad.astype(jnp.float32), axis=0)
    context_grad = (
        against(branch_grad, proj_weight)
        .astype(jnp.bfloat16)
        .reshape(local_rows, heads_count, head_width)
        * head_keep
    )
    attn_probs = jnp.exp(masked_scores(query_heads, key_heads, allowed, score_scale) - log_total)
    prob_grad = jnp.einsum(
        "qhd,khd->hqk", context_grad, value_heads, preferred_element_type=jnp.float32
    )
    row_total = jnp.sum(attn_probs * prob_grad, axis=-1, keepdims=True)
    score_grad = (attn_probs * (prob_grad - row_total) * score_scale).astype(jnp.bfloat16)
    query_grad = (
        jnp.einsum("hqk,khd->qhd", score_grad, key_heads, preferred_element_type=jnp.float32)
        .reshape(local_rows, model_width)
        .astype(jnp.bfloat16)
    )
    key_part = jnp.einsum(
        "hqk,qhd->khd", score_grad, query_heads, preferred_element_type=jnp.float32
    ).reshape(full_rows, model_width)
    value_part = jnp.einsum(
        "hqk,qhd->khd",
        attn_probs.astype(jnp.bfloat16),
        context_grad,
        preferred_element_type=jnp.float32,
    ).reshape(full_rows, model_width)
    key_sum, value_sum = (
        lax.psum_scatter(
            key_part.astype(jnp.bfloat16), "seq", scatter_dimension=0, tiled=True
        ).astype(jnp.float32),
        lax.psum_scatter(
            value_part.astype(jnp.bfloat16), "seq", scatter_dimension=0, tiled=True
        ).astype(jnp.float32),
    )
    value_low = value_sum.astype(jnp.bfloat16)
    qkv_grad = jnp.concatenate([query_grad, key_sum.astype(jnp.bfloat16), value_low], axis=1)
    qkv_w_grad = over_rows(normed, qkv_grad)
    qv_b_grad = jnp.concatenate(
        [
            jnp.sum(query_grad.astype(jnp.float32), axis=0),
            jnp.sum(value_low.astype(jnp.float32), axis=0),
        ]
    )
    normed_grad = against(qkv_grad, qkv_weight)
    shift_one_grad = jnp.sum(normed_grad, axis=0)
    scale_one_grad = jnp.sum(normed_grad * normed_one, axis=0)
    input_grad = middle_grad + norm_back_one(normed_grad * (1.0 + scale_one))[0]
    mod_part = jnp.concatenate(
        [
            shift_one_grad,
            scale_one_grad,
            gate_one_grad,
            shift_two_grad,
            scale_two_grad,
            gate_two_grad,
        ]
    )
    mod_grad = lax.psum(mod_part, "seq")
    mod_low = mod_grad.astype(jnp.bfloat16)
    cond_grad = silu_back(against(mod_low[None, :], ada_weight)[0])[0]
    silu_all = lax.all_gather(silu_low, "bucket", axis=0)
    mod_all = lax.all_gather(mod_low, "bucket", axis=0)
    bucket = lax.axis_index("bucket")
    width = model_width // 32
    silu_mine = lax.dynamic_slice_in_dim(silu_all, bucket * width, width, axis=1)
    ada_w_shard = over_rows(silu_mine, mod_all)
    vectors = jnp.concatenate([qv_b_grad, proj_b_grad, fc1_b_grad, fc2_b_grad])
    vectors = lax.psum(vectors, ("bucket", "seq"))
    sizes = (2 * model_width, model_width, fc1_weight.shape[1], model_width)
    shards, start = [], 0
    for size in sizes:
        shards.append(lax.dynamic_slice_in_dim(vectors, start + bucket * (size // 32), size // 32))
        start += size
    qv_shard, proj_b_shard, fc1_b_shard, fc2_b_shard = shards
    ada_b_shard = lax.dynamic_slice_in_dim(
        jnp.sum(mod_all.astype(jnp.float32), axis=0), bucket * 6 * width, 6 * width
    )
    grid = (4, 2, 4, 2)
    fc2_pieces = reduce_weights(
        [
            fc2_w_grad.astype(jnp.bfloat16).reshape(grid + (4, 16, model_width)),
            proj_w_grad.astype(jnp.bfloat16).reshape(grid + (16, model_width)),
        ],
        [(0, "rows", q, model_width) for q in range(4)] + [(1, "columns", 0, model_width)],
        0,
        "reduce_fc2_proj",
    )
    fc1_pieces = reduce_weights(
        [
            fc1_w_grad.astype(jnp.bfloat16).reshape(grid + (16, 4 * model_width)),
            qkv_w_grad.astype(jnp.bfloat16).reshape(grid + (16, 3 * model_width)),
        ],
        [(0, "columns", q * model_width, model_width) for q in range(4)]
        + [(1, "columns", q * model_width, model_width) for q in range(3)],
        1,
        "reduce_fc1_qkv",
    )
    fc2_w_shard = jnp.stack(fc2_pieces[:4], axis=1).reshape(128, model_width)
    proj_w_shard = fc2_pieces[4].reshape(32, model_width)
    fc1_w_shard = jnp.concatenate(fc1_pieces[:4], axis=2).reshape(32, 4 * model_width)
    qkv_shard = jnp.concatenate(fc1_pieces[4:], axis=2).reshape(32, 3 * model_width)
    return (
        block_out[None],
        input_grad[None],
        cond_grad[None],
        ada_w_shard,
        ada_b_shard,
        qkv_shard,
        qv_shard,
        proj_w_shard,
        proj_b_shard,
        fc1_w_shard,
        fc1_b_shard,
        fc2_w_shard,
        fc2_b_shard,
    )


def solution(mesh):
    return jax.shard_map(
        local,
        mesh=mesh,
        in_specs=(
            P("bucket", "seq", None),
            P("bucket", None),
            P("bucket", None),
            P("bucket", None),
            P("bucket", None),
            P("bucket", "seq"),
            P(),
            P(),
            P(),
            P(),
            P(),
            P(),
            P(),
            P(),
            P(),
            P(),
            P("bucket", "seq", None),
        ),
        out_specs=(
            P("bucket", "seq", None),
            P("bucket", "seq", None),
            P("bucket", None),
            P("bucket", None),
            P("bucket"),
            P("bucket", None),
            P("bucket"),
            P("bucket", None),
            P("bucket"),
            P("bucket", None),
            P("bucket"),
            P("bucket", None),
            P("bucket"),
        ),
        check_vma=False,
    )
```

```python
import functools

import jax
import jax.numpy as jnp
from jax import lax
from jax.experimental import pallas as pl
from jax.experimental.pallas import tpu as pltpu
from jax.sharding import PartitionSpec as P


MESH_IDS = pl.DeviceIdType.MESH
AXES = {"x": 0, "y": 1, "z": 2}


def place():
    bucket = lax.axis_index("bucket")
    seq = lax.axis_index("seq")
    return (
        (seq // 2) * 2 + (bucket // 4) % 2,
        bucket % 4,
        bucket // 8,
        seq % 2,
    )


def device(x, y, z, core):
    return (z * 8 + (x % 2) * 4 + y, (x // 2) * 2 + core)


def shifted(spot, axis, step):
    x, y, z, core = spot
    if axis == "x":
        x = (x + step) % 4
    elif axis == "y":
        y = (y + step) % 4
    elif axis == "z":
        z = (z + step) % 4
    elif axis == "l":
        x = (x // 2) * 2 + 1 - x % 2
    return device(x, y, z, core)


TORUS = [(axis, step) for axis in "xyz" for step in (1, -1)]


def add_into(target, others):
    total = target[...].astype(jnp.float32)
    for other in others:
        total = total + other[...].astype(jnp.float32)
    target[...] = total.astype(jnp.bfloat16)


class Piece:
    def __init__(self, source, columns, route, landing, send_sem, recv_sem, spot):
        self.source, self.columns, self.route = source, columns, route
        self.landing = landing
        self.send_sem, self.recv_sem, self.spot = send_sem, recv_sem, spot
        self.copies, self.done = {}, []

    @staticmethod
    def dims(route, phase, columns):
        done = route[: phase + 1]
        out = []
        if "z" not in done:
            out.append(4)
        if "x" not in done and "l" not in done:
            out.append(2)
        if "y" not in done:
            out.append(4)
        if "l" in route:
            return tuple(out) + (16, columns)
        if "x" not in done:
            out.append(2)
        return tuple(out) + (16, columns // 2)

    def block(self, phase, target, half):
        done, axis = self.route[:phase], self.route[phase]
        split = "l" in self.route
        index = []
        if "z" not in done:
            index.append(target if axis == "z" else slice(None))
        if "x" not in done and "l" not in done:
            index.append(
                target % 2 if axis == "x" else target if axis == "l" else slice(None)
            )
        if "y" not in done:
            index.append(target if axis == "y" else slice(None))
        if phase == 0:
            if split:
                return self.source.at[tuple(index) + (half,)]
            index.append(target // 2 if axis == "x" else slice(None))
            width = self.columns // 2
            lanes = pl.ds(half * width, width)
            return self.source.at[tuple(index) + (slice(None), lanes)]
        if not split and "x" not in done:
            index.append(target // 2 if axis == "x" else slice(None))
        return self.landing[phase - 1].at[(3 - half,) + tuple(index)]

    def here(self, phase):
        if self.route[phase] == "l":
            return self.spot[0] % 2
        return self.spot[AXES[self.route[phase]]]

    def send(self, phase, slot, ref, step):
        copy = pltpu.make_async_remote_copy(
            src_ref=ref,
            dst_ref=self.landing[phase].at[slot],
            send_sem=self.send_sem.at[phase, slot],
            recv_sem=self.recv_sem.at[phase, slot],
            device_id=shifted(self.spot, self.route[phase], step),
            device_id_type=MESH_IDS,
        )
        copy.start()
        self.copies[phase, slot] = copy

    def first(self, phase):
        a = self.here(phase)
        if self.route[phase] == "l":
            self.send(phase, 2, self.block(phase, 1 - a, 1), 1)
            self.send(phase, 3, self.block(phase, 1 - a, 0), 1)
            return
        self.send(phase, 0, self.block(phase, (a + 2) % 4, 0), 1)
        self.send(phase, 1, self.block(phase, (a + 2) % 4, 1), -1)
        self.send(phase, 2, self.block(phase, (a + 1) % 4, 1), 1)
        self.send(phase, 3, self.block(phase, (a + 3) % 4, 0), -1)

    def second(self, phase):
        if self.route[phase] == "l":
            return
        a = self.here(phase)
        landing = self.landing[phase]
        for slot, step, half in ((0, 1, 0), (1, -1, 1)):
            self.copies[phase, slot].wait_recv()
            add_into(landing.at[slot], [self.block(phase, (a + step) % 4, half)])
            self.send(phase, slot + 4, landing.at[slot], step)

    def third(self, phase):
        a = self.here(phase)
        landing = self.landing[phase]
        for half, slot, other in ((0, 3, 4), (1, 2, 5)):
            self.copies[phase, slot].wait_recv()
            terms = [self.block(phase, a, half)]
            if self.route[phase] != "l":
                self.copies[phase, other].wait_recv()
                terms.append(landing.at[other])
            add_into(landing.at[slot], terms)

    def result(self, half):
        return self.landing[-1].at[3 - half]

    def sent(self, phase):
        for slot in range(4):
            self.copies[phase, slot].wait_send()
            self.done.append((phase, slot))

    def finish(self):
        for key, copy in self.copies.items():
            if key not in self.done:
                copy.wait_send()


BF = jnp.bfloat16
F32 = jnp.float32
VMEM = pl.BlockSpec(memory_space=pltpu.VMEM)
SMEM = pl.BlockSpec(memory_space=pltpu.SMEM)
ANY = pl.BlockSpec(memory_space=pl.ANY)
NT = (((1,), (1,)), ((), ()))
TN = (((0,), (0,)), ((), ()))
WIDTH = 1024
ROWS = 256
HEAD = 64
MINE = 256


def dot(a, b):
    return jnp.dot(a, b, preferred_element_type=F32)


def dot_nt(a, b):
    return lax.dot_general(a, b, NT, preferred_element_type=F32)


def dot_tn(a, b):
    return lax.dot_general(a, b, TN, preferred_element_type=F32)


def norm_parts(values):
    centred = values - jnp.mean(values, axis=-1, keepdims=True)
    rate = lax.rsqrt(jnp.mean(centred * centred, axis=-1, keepdims=True) + 1e-06)
    return centred * rate, rate


def norm_back(normed, rate, grad):
    inner = jnp.mean(grad * normed, axis=-1, keepdims=True)
    return (grad - jnp.mean(grad, axis=-1, keepdims=True) - normed * inner) * rate


def segment(positions, lengths):
    first = lengths[0, 0]
    both = lengths[0, 0] + lengths[0, 1]
    return (positions >= first).astype(jnp.int32) + (positions >= both).astype(jnp.int32)


def quad(spot):
    x, _, _, core = spot
    high = x // 2
    own = high * 2 + core
    pair = high * 2 + (1 - core)
    far = (1 - high) * 2 + core
    cross = (1 - high) * 2 + (1 - core)
    return own, pair, far, cross


def partner(spot, which):
    x, y, z, core = spot
    if which == "pair":
        return device(x, y, z, 1 - core)
    if which == "far":
        return device((x + 2) % 4, y, z, core)
    return device((x + 2) % 4, y, z, 1 - core)


def greet_all(spot, moves, partners):
    barrier = pltpu.get_barrier_semaphore()
    for axis, step in moves:
        pl.semaphore_signal(
            barrier, inc=1, device_id=shifted(spot, axis, step), device_id_type=MESH_IDS
        )
    for which in partners:
        pl.semaphore_signal(barrier, inc=1, device_id=partner(spot, which), device_id_type=MESH_IDS)
    pl.semaphore_wait(barrier, len(moves) + len(partners))


class Mail:
    def __init__(self, spot, send_sem, recv_sem):
        self.spot, self.send_sem, self.recv_sem = spot, send_sem, recv_sem
        self.copies, self.done = [], []

    def send(self, src, dst, which):
        return self.send_to(src, dst, partner(self.spot, which))

    def send_ring(self, src, dst, axis, step):
        return self.send_to(src, dst, shifted(self.spot, axis, step))

    def send_to(self, src, dst, target):
        k = len(self.copies)
        copy = pltpu.make_async_remote_copy(
            src_ref=src,
            dst_ref=dst,
            send_sem=self.send_sem.at[k],
            recv_sem=self.recv_sem.at[k],
            device_id=target,
            device_id_type=MESH_IDS,
        )
        copy.start()
        self.copies.append(copy)
        return copy

    def sent(self, copy):
        copy.wait_send()
        self.done.append(copy)

    def finish(self):
        for copy in self.copies:
            if not any(copy is other for other in self.done):
                copy.wait_send()


def attend_kernel(
    tokens,
    condition,
    lengths,
    head_mask,
    ada_weight,
    ada_bias,
    qkv_weight,
    qv_bias,
    mods,
    attended,
    q_out,
    v_out,
    kt_out,
    ot_out,
    inv_out,
    normed_out,
    e_out,
    ada,
    weight,
    everyone,
    k_aug,
    vt,
    ctx_t,
    ctx_send,
    ctx_recv,
    e_all,
    load_sem,
    out_sem,
    send_sem,
    recv_sem,
):
    spot = place()
    own, pair, far, cross = quad(spot)
    loads = []
    for j in range(6):
        loads.append(
            pltpu.make_async_copy(
                ada_weight.at[:, pl.ds(j * WIDTH, WIDTH)], ada.at[j], load_sem.at[j]
            )
        )
    for j in range(3):
        start = pl.multiple_of(j * WIDTH + own * MINE, MINE)
        loads.append(
            pltpu.make_async_copy(
                qkv_weight.at[:, pl.ds(start, MINE)],
                weight.at[:, pl.ds(j * MINE, MINE)],
                load_sem.at[6 + j],
            )
        )
    for copy in loads:
        copy.start()
    greet_all(spot, [], ("pair", "far", "cross"))
    mail = Mail(spot, send_sem, recv_sem)
    half = ROWS // 2
    to_far = [
        mail.send(
            tokens.at[pl.ds(i * half, half)], everyone.at[own, pl.ds(i * half, half)], "far"
        )
        for i in range(2)
    ]
    to_pair = mail.send(tokens, everyone.at[own], "pair")

    value = condition[...].astype(F32)
    silu_low = (value / (1.0 + jnp.exp(-value))).astype(BF)
    silu_rows = jnp.broadcast_to(silu_low, (16, WIDTH))
    for j in range(6):
        loads[j].wait()
        row = dot(silu_rows, ada[j])[0:1]
        mods[pl.ds(j, 1), :] = row + ada_bias[:, pl.ds(j * WIDTH, WIDTH)].astype(F32)
    for copy in loads[6:]:
        copy.wait()

    shift, scale = mods[0:1, :], 1.0 + mods[1:2, :]
    mine = pl.multiple_of(own * MINE, MINE)
    q_bias = qv_bias[:, pl.ds(mine, MINE)].astype(F32)
    v_bias = qv_bias[:, pl.ds(WIDTH + mine, MINE)].astype(F32)
    lane = lax.broadcasted_iota(jnp.int32, (ROWS, 128), 1)

    def project(block, rows):
        normed = (norm_parts(rows[...].astype(F32))[0] * scale + shift).astype(BF)
        here = pl.ds(pl.multiple_of(block * ROWS, ROWS), ROWS)
        normed_out[here, :] = normed
        projected = dot(normed, weight[...])
        q_out[here, :] = ((projected[:, :MINE] + q_bias).astype(BF) * 0.125).astype(BF)
        keys = projected[:, MINE : 2 * MINE].astype(BF)
        values = (projected[:, 2 * MINE :] + v_bias).astype(BF)
        spots = segment(block * ROWS + lax.broadcasted_iota(jnp.int32, (ROWS, 128), 0), lengths)
        marks = jnp.where(spots == lane, 1.0, 0.0).astype(BF)
        for p in range(2):
            k_aug[p, here, pl.ds(0, 128)] = keys[:, p * 128 : (p + 1) * 128]
            k_aug[p, here, pl.ds(128, 128)] = marks
        v_out[here, :] = values
        kt_out[:, here] = keys.T
        vt[:, here] = values.T

    project(own, tokens)
    to_pair.wait_recv()
    project(pair, everyone.at[pair])
    forwards = []
    for i in range(2):
        to_far[i].wait_recv()
        piece = everyone.at[far, pl.ds(i * half, half)]
        forwards.append(mail.send(piece, piece, "pair"))
    project(far, everyone.at[far])
    for copy in forwards:
        copy.wait_recv()
    project(cross, everyone.at[cross])

    lanes = lax.broadcasted_iota(jnp.int32, (ROWS, 256), 1)
    out_copies = []
    sends = []
    for n, (block, which) in enumerate(
        ((cross, "cross"), (far, "far"), (pair, "pair"), (own, None))
    ):
        here = pl.ds(pl.multiple_of(block * ROWS, ROWS), ROWS)
        spots = segment(block * ROWS + lax.broadcasted_iota(jnp.int32, (ROWS, 128), 0), lengths)
        marks = jnp.where((spots != lane) & (lane < 3), -1e30, 0.0).astype(BF)

        def head(h, carry, block=block, here=here, marks=marks):
            p = h // 2
            queries = q_out[here, pl.ds(pl.multiple_of(p * 128, 128), 128)]
            both = jnp.concatenate([queries, marks], axis=1)
            keep = (lanes // HEAD == h % 2) | (lanes >= 128)
            both = jnp.where(keep, both, jnp.zeros_like(both))
            scores = dot_nt(k_aug[p], both)
            top = jnp.max(scores, axis=0, keepdims=True)
            powers = jnp.exp(scores - top)
            inverse = 1.0 / jnp.sum(powers, axis=0, keepdims=True)
            low = powers.astype(BF)
            e_all[:, pl.ds(pl.multiple_of((block * 4 + h) * ROWS, ROWS), ROWS)] = low
            inv_out[h, :, here] = inverse
            part = pl.ds(pl.multiple_of(h * HEAD, HEAD), HEAD)
            out = dot(vt[part, :], low) * inverse
            ot_out[part, here] = out.astype(BF)
            ctx_t[part, :] = out * head_mask[0, own * 4 + h].astype(F32)
            return carry

        lax.fori_loop(0, 4, head, 0)
        ctx = ctx_t[...].T.astype(BF)
        if which is None:
            ctx_recv[own] = ctx
        else:
            ctx_send[n] = ctx
            sends.append(mail.send(ctx_send.at[n], ctx_recv.at[own], which))
        wide = pl.ds(pl.multiple_of(block * 4 * ROWS, ROWS), 4 * ROWS)
        copy = pltpu.make_async_copy(e_all.at[:, wide], e_out.at[:, wide], out_sem.at[n])
        copy.start()
        out_copies.append(copy)
    for copy in sends:
        copy.wait_recv()
    for s in range(4):
        attended[:, pl.ds(s * MINE, MINE)] = ctx_recv[s]
    for copy in out_copies:
        copy.wait()
    mail.finish()


def attend(
    tokens, condition, lengths, head_mask, ada_weight, ada_bias, qkv_weight, qv_bias
):
    shape = jax.ShapeDtypeStruct
    row = 4 * ROWS
    return pl.pallas_call(
        attend_kernel,
        out_shape=[
            shape((8, WIDTH), F32),
            shape((ROWS, WIDTH), BF),
            shape((row, MINE), BF),
            shape((row, MINE), BF),
            shape((MINE, row), BF),
            shape((MINE, row), BF),
            shape((4, 1, row), F32),
            shape((row, WIDTH), BF),
            shape((row, 4 * row), BF),
        ],
        in_specs=[VMEM, VMEM, SMEM, SMEM, ANY, VMEM, ANY, VMEM],
        out_specs=[VMEM] * 8 + [ANY],
        scratch_shapes=[
            pltpu.VMEM((6, WIDTH, WIDTH), BF),
            pltpu.VMEM((WIDTH, 3 * MINE), BF),
            pltpu.VMEM((4, ROWS, WIDTH), BF),
            pltpu.VMEM((2, row, 256), BF),
            pltpu.VMEM((MINE, row), BF),
            pltpu.VMEM((MINE, ROWS), F32),
            pltpu.VMEM((3, ROWS, MINE), BF),
            pltpu.VMEM((4, ROWS, MINE), BF),
            pltpu.VMEM((row, 4 * row), BF),
            pltpu.SemaphoreType.DMA((9,)),
            pltpu.SemaphoreType.DMA((4,)),
            pltpu.SemaphoreType.DMA((8,)),
            pltpu.SemaphoreType.DMA((8,)),
        ],
        compiler_params=pltpu.CompilerParams(
            collective_id=2, has_side_effects=True, vmem_limit_bytes=60 << 20
        ),
        name="attend",
    )(tokens, condition, lengths, head_mask, ada_weight, ada_bias, qkv_weight, qv_bias)


ROUTE_OF = ("zyx", "yxz", "xzy", "zyx", "yxz", "xzy", "yxz", "xzy", "zyl", "yzl")
COLUMNS_OF = (768, 768, 512, 768, 512, 768, 256, 256, 384, 384)
FC_COLUMNS = sum(COLUMNS_OF[:8])
FC2_UNITS = ((0, 0), (0, 1), (1, 0), (1, 1), (2, 0), (2, 1), (3, 0), (3, 1))


def lanes_at(start, size):
    return pl.ds(pl.multiple_of(start, 128), size)


def block_rows(index):
    return pl.ds(pl.multiple_of(index * ROWS, ROWS), ROWS)


def middle_kernel(
    tokens,
    out_grad,
    mods,
    lengths,
    head_mask,
    group_mask,
    token_mask,
    proj_bias,
    fc1_bias,
    fc2_bias,
    attended,
    proj_weight,
    fc1_weight,
    fc2_weight,
    qkv_weight,
    q_in,
    v_in,
    kt_in,
    ot_in,
    inv_in,
    normed_in,
    e_in,
    block_out,
    input_grad,
    vec,
    qkv_out,
    proj_out,
    fc1_out,
    fc2_out,
    proj_w,
    fc1_w,
    fc2_w,
    att,
    normed_two,
    big,
    mlp_grad,
    branch_cols,
    middle,
    branch,
    part_send,
    part_recv,
    channel,
    kt,
    ot,
    inv,
    do_recv,
    dq_t,
    dk,
    dv,
    n_recv,
    fin,
    fin_q,
    load_sem,
    out_sem,
    mail_send,
    mail_recv,
    piece_send,
    piece_recv,
    *piece_refs,
):
    spot = place()
    core, high = spot[3], spot[0] // 2
    own, pair, far, cross = quad(spot)
    half_ff = 2 * WIDTH

    def load(k, src, dst):
        copy = pltpu.make_async_copy(src, dst, load_sem.at[k])
        copy.start()
        return copy

    here, there = block_rows(core), block_rows(1 - core)
    load_att = load(0, attended, att.at[here])
    load_proj = load(1, proj_weight, proj_w)
    load_fc1 = load(2, fc1_weight.at[:, lanes_at(core * half_ff, half_ff)], fc1_w)
    load_fc2 = load(
        3, fc2_weight.at[pl.ds(pl.multiple_of(core * half_ff, 256), half_ff), :], fc2_w
    )
    load_heads = [load(4, kt_in, kt), load(5, ot_in, ot), load(6, inv_in, inv)]
    greet_all(spot, TORUS, ("pair", "far", "cross"))
    mail = Mail(spot, mail_send, mail_recv)
    pieces = []
    for k in range(10):
        refs = piece_refs[3 * k : 3 * k + 3]
        if k < 8:
            source = piece_refs[30 + k]
        else:
            source = pieces[0].source.at[..., (k - 8) * 384 : (k - 7) * 384]
        pieces.append(
            Piece(
                source,
                COLUMNS_OF[k],
                ROUTE_OF[k],
                refs,
                piece_send.at[k],
                piece_recv.at[k],
                spot,
            )
        )
    fc2_p, fc1_p, proj_p, qkv_p = pieces[0:3], pieces[3:6], pieces[6:8], pieces[8:10]

    def first(group, phase):
        for piece in group:
            piece.first(phase)

    def second(group, phase):
        for piece in group:
            piece.second(phase)

    def third(group, phase):
        for piece in group:
            piece.third(phase)
            if phase < 2:
                piece.first(phase + 1)

    shift_two, scale_two = mods[3:4, :], 1.0 + mods[4:5, :]
    gate_one, gate_two = mods[2:3, :], mods[5:6, :]
    position = own * ROWS + lax.broadcasted_iota(jnp.int32, (ROWS, 1), 0)
    valid = (position < lengths[0, 0] + lengths[0, 1]).astype(F32)
    kept = valid * token_mask[...].astype(F32)
    for g in range(8):
        channel[:, pl.ds(g * 256, 256)] = jnp.full(
            (1, 256), group_mask[0, core * 8 + g].astype(F32), F32
        )
    vec[...] = jnp.zeros_like(vec)

    upstream = out_grad[...].astype(F32)
    low_grad = (kept * gate_two * upstream).astype(BF)
    mlp_grad[here, :] = low_grad
    vec[13:14, :] = jnp.sum(low_grad.astype(F32), axis=0, keepdims=True)
    got_grad = mail.send(mlp_grad.at[here], mlp_grad.at[here], "pair")
    load_att.wait()
    got_att = mail.send(att.at[here], att.at[here], "pair")
    load_proj.wait()
    branch[...] = dot(att[here, :], proj_w[...]) + proj_bias[...].astype(F32)
    mid = tokens[...].astype(F32) + valid * gate_one * branch[...]
    middle[...] = mid
    normed_two[here, :] = (norm_parts(mid)[0] * scale_two + shift_two).astype(BF)
    got_normed = mail.send(normed_two.at[here], normed_two.at[here], "pair")
    load_fc1.wait()
    mine = lanes_at(core * half_ff, half_ff)
    TILE = 512

    def hidden(rows):
        def body(i, carry):
            cols = lanes_at(i * TILE, TILE)
            wide = lanes_at(core * half_ff + i * TILE, TILE)
            u = dot(normed_two[rows, :], fc1_w[:, cols]) + fc1_bias[:, wide].astype(F32)
            square = u * u
            t = jnp.tanh(0.7978845608028654 * u * (1.0 + 0.044715 * square))
            up = 0.5 * (1.0 + t)
            mask = channel[:, cols]
            big[rows, wide] = (u * up * mask).astype(BF)
            slope = up + 0.5 * u * (1.0 - t * t) * (
                0.7978845608028654 + (3 * 0.7978845608028654 * 0.044715) * square
            )
            low = pl.ds(pl.multiple_of(2 * ROWS + rows.start, ROWS), ROWS)
            big[low, cols] = (slope * mask).astype(BF)
            return carry

        lax.fori_loop(0, half_ff // TILE, body, 0)

    hidden(here)
    got_act = [mail.send(big.at[here, mine], big.at[here, mine], "pair")]
    got_normed.wait_recv()
    hidden(there)
    got_act.append(mail.send(big.at[there, mine], big.at[there, mine], "pair"))
    load_fc2.wait()
    part_send[0] = dot(big[there, mine], fc2_w[...]).astype(BF)
    got_part = mail.send(part_send.at[0], part_recv.at[0], "pair")
    mlp_out = dot(big[here, mine], fc2_w[...]) + fc2_bias[...].astype(F32)
    got_part.wait_recv()
    mlp_out = mlp_out + part_recv[0].astype(F32)
    result = middle[...] + kept * gate_two * mlp_out
    out_copies = []
    for s in range(4):
        cols = slice(s * MINE, (s + 1) * MINE)
        dk[s * ROWS : (s + 1) * ROWS, :] = result[:, cols]
        out_copies.append(
            pltpu.make_async_copy(
                dk.at[pl.ds(s * ROWS, ROWS)], block_out.at[:, pl.ds(s * MINE, MINE)], out_sem.at[s]
            )
        )
        out_copies[s].start()
    vec[5:6, :] = jnp.sum(kept * mlp_out * upstream, axis=0, keepdims=True)

    got_grad.wait_recv()
    for copy in got_act:
        copy.wait_recv()
    half_cols = lanes_at(core * 512, 512)

    def fc2_tile(i, carry):
        t = dot_tn(big[0 : 2 * ROWS, lanes_at(i * 512, 512)], mlp_grad[:, half_cols])
        t = t.astype(BF).reshape(4, 2, 4, 16, 512)
        z, x_lo = i // 2, i % 2
        fc2_p[0].source[z, x_lo, :, :, :, 0:512] = t[:, :, 0]
        fc2_p[0].source[z, x_lo, :, :, :, 512:768] = t[:, :, 1, :, 0:256]
        fc2_p[1].source[z, x_lo, :, :, :, 0:256] = t[:, :, 1, :, 256:512]
        fc2_p[1].source[z, x_lo, :, :, :, 256:768] = t[:, :, 2]
        fc2_p[2].source[z, x_lo] = t[:, :, 3]
        return carry

    lax.fori_loop(0, 8, fc2_tile, 0)
    first(fc2_p, 0)

    def hidden_grad(i, carry):
        cols = lanes_at(i * TILE, TILE)
        low = pl.ds(pl.multiple_of(i * TILE, TILE), TILE)
        grad = dot_nt(mlp_grad[...], fc2_w[low, :])
        grad = (grad * big[2 * ROWS : 4 * ROWS, cols].astype(F32)).astype(BF)
        big[2 * ROWS : 4 * ROWS, lanes_at(half_ff + i * TILE, TILE)] = grad
        total = jnp.sum(grad.astype(F32), axis=0, keepdims=True)
        row = 9 + 2 * core + i // 2
        vec[pl.ds(row, 1), lanes_at((i % 2) * TILE, TILE)] = total
        return carry

    lax.fori_loop(0, half_ff // TILE, hidden_grad, 0)
    low_rows, low_cols = pl.ds(2 * ROWS, 2 * ROWS), pl.ds(half_ff, half_ff)
    load_qkv = [
        load(
            7 + j,
            qkv_weight.at[:, lanes_at(j * WIDTH + own * MINE, MINE)],
            fc2_w.at[pl.ds(0, WIDTH), pl.ds(j * MINE, MINE)],
        )
        for j in range(3)
    ]
    load_heads.append(load(10, q_in, fc2_w.at[pl.ds(0, WIDTH), pl.ds(768, 256)]))
    load_heads.append(load(11, v_in, fc2_w.at[pl.ds(WIDTH, WIDTH), pl.ds(768, 256)]))
    second(fc2_p, 0)

    start = half_ff
    for piece in fc1_p:
        width = piece.columns

        def fc1_tile(i, carry, start=start, width=width, piece=piece):
            t = dot_tn(
                normed_two[:, lanes_at(i * 512, 512)],
                big[2 * ROWS : 4 * ROWS, start : start + width],
            )
            piece.source[pl.ds(i * 2, 2)] = t.astype(BF).reshape(2, 2, 4, 2, 16, width)
            return carry

        lax.fori_loop(0, 2, fc1_tile, 0)
        piece.first(0)
        start += width

    def back(rows):
        low = pl.ds(pl.multiple_of(2 * ROWS + rows.start, ROWS), ROWS)
        return dot_nt(big[low, low_cols], fc1_w[...])

    part_send[1] = back(there).astype(BF)
    got_back = mail.send(part_send.at[1], part_recv.at[1], "pair")
    normed_two_grad = back(here)
    for copy in got_act:
        mail.sent(copy)
    load_e = load(12, e_in, big)
    load_normed = load(13, normed_in, fc1_w.at[:, pl.ds(0, WIDTH)])
    third(fc2_p, 0)
    got_back.wait_recv()
    normed_two_grad = normed_two_grad + part_recv[1].astype(F32)
    normed_mid, rate = norm_parts(middle[...])
    vec[3:4, :] = jnp.sum(normed_two_grad, axis=0, keepdims=True)
    vec[4:5, :] = jnp.sum(normed_two_grad * normed_mid, axis=0, keepdims=True)
    mid_grad = upstream + norm_back(normed_mid, rate, normed_two_grad * scale_two)
    middle[...] = mid_grad
    vec[2:3, :] = jnp.sum(valid * branch[...] * mid_grad, axis=0, keepdims=True)
    branch_grad = (valid * gate_one * mid_grad).astype(BF)
    vec[8:9, :] = jnp.sum(branch_grad.astype(F32), axis=0, keepdims=True)
    mail.sent(got_normed)
    normed_two[here, :] = branch_grad
    branch_cols[here, :] = normed_two[here, half_cols]
    other_cols = lanes_at((1 - core) * 512, 512)
    got_cols = mail.send(normed_two.at[here, other_cols], branch_cols.at[here], "pair")
    context_grad = dot_nt(branch_grad, proj_w[...]).astype(BF)
    mail.sent(got_part)
    part_send[0] = context_grad
    got_do = [
        mail.send(
            part_send.at[0, :, lanes_at(block * MINE, MINE)], do_recv.at[own], which
        )
        for block, which in ((cross, "cross"), (far, "far"), (pair, "pair"))
    ]
    do_recv[own] = part_send[0, :, lanes_at(own * MINE, MINE)]

    got_att.wait_recv()
    got_cols.wait_recv()
    second(fc1_p, 0)

    def proj_tile(i, carry):
        t = dot_tn(att[:, lanes_at(i * 512, 512)], branch_cols[...])
        t = t.astype(BF).reshape(2, 2, 4, 2, 16, 512)
        proj_p[0].source[pl.ds(i * 2, 2)] = t[..., 0:256]
        proj_p[1].source[pl.ds(i * 2, 2)] = t[..., 256:512]
        return carry

    lax.fori_loop(0, 2, proj_tile, 0)
    first(proj_p, 0)
    second(fc2_p, 1)

    for copy in out_copies:
        copy.wait()
    q_wide, do_wide = proj_w.at[:, 0:MINE], proj_w.at[:, MINE : 2 * MINE]
    for copy in load_heads:
        copy.wait()
    load_e.wait()
    load_normed.wait()
    for copy in load_qkv:
        copy.wait()
    for n, block in enumerate((own, pair, far, cross)):
        if n > 0:
            got_do[3 - n].wait_recv()
        rows = block_rows(block)
        lane = lax.broadcasted_iota(jnp.int32, (ROWS, MINE), 1)
        grad_t = do_recv[block].astype(F32).T
        parts, rests = [], []
        for h in range(4):
            factor = inv[h, :, rows] * head_mask[0, own * 4 + h].astype(F32)
            part = (grad_t[h * HEAD : (h + 1) * HEAD] * factor).astype(BF)
            parts.append(part)
            rests.append(
                jnp.sum(
                    part.astype(F32) * ot[h * HEAD : (h + 1) * HEAD, rows].astype(F32),
                    axis=0,
                    keepdims=True,
                )
            )
        grad_low = jnp.concatenate(parts, axis=0)
        grad_rows = grad_low.astype(F32).T.astype(BF)
        queries = fc2_w[rows, 768:1024]
        zero = jnp.zeros((), BF)
        for h in range(4):
            keep = lane // HEAD == h
            q_wide[h * ROWS : (h + 1) * ROWS, :] = jnp.where(keep, queries, zero)
            do_wide[h * ROWS : (h + 1) * ROWS, :] = jnp.where(keep, grad_rows, zero)
        for h in range(4):
            below = lax.broadcasted_iota(jnp.int32, (MINE, ROWS), 0) // HEAD == h
            masked = jnp.where(below, grad_low, zero)
            prob_grad = dot(fc2_w[WIDTH : 2 * WIDTH, 768:1024], masked)
            powers = big[:, lanes_at((block * 4 + h) * ROWS, ROWS)].astype(F32)
            score_grad = (powers * (prob_grad - rests[h])).astype(BF)
            fc1_w[:, WIDTH + h * ROWS : WIDTH + (h + 1) * ROWS] = score_grad
            dq_t[h * HEAD : (h + 1) * HEAD, :] = dot(
                kt[h * HEAD : (h + 1) * HEAD, :], score_grad
            )
        more_k = dot(fc1_w[:, WIDTH : 2 * WIDTH], q_wide[...])
        more_v = dot(big[:, lanes_at(block * 4 * ROWS, 4 * ROWS)], do_wide[...])
        if n == 0:
            dk[...] = more_k
            dv[...] = more_v
        else:
            dk[...] += more_k
            dv[...] += more_v
        row_of = pl.ds(pl.multiple_of(WIDTH + block * ROWS, ROWS), ROWS)
        fc2_w[row_of, 0:MINE] = (dq_t[...].T * 0.125).astype(BF)
        if n == 0:
            third(fc2_p, 1)
            third(fc1_p, 0)
        elif n == 1:
            second(proj_p, 0)
            second(fc2_p, 2)
            second(fc1_p, 1)
        elif n == 2:
            third(proj_p, 0)
            third(fc2_p, 2)
            third(fc1_p, 1)
    low = slice(WIDTH, 2 * WIDTH)
    fc2_w[low, MINE : 2 * MINE] = dk[...].astype(BF)
    fc2_w[low, 2 * MINE : 3 * MINE] = dv[...].astype(BF)
    for j, row in ((0, 6), (2, 7)):
        total = jnp.sum(fc2_w[low, j * MINE : (j + 1) * MINE].astype(F32), axis=0, keepdims=True)
        vec[row : row + 1, lanes_at(own * MINE, MINE)] = total

    fc2_p[0].sent(0)

    def qkv_tile(i, carry):
        t = dot_tn(fc1_w[:, lanes_at(i * 512, 512)], fc2_w[WIDTH : 2 * WIDTH, 0:768])
        t = t.astype(BF).reshape(2, 2, 4, 2, 16, 768)
        qkv_p[0].source[pl.ds(i * 2, 2)] = t[..., 0:384]
        qkv_p[1].source[pl.ds(i * 2, 2)] = t[..., 384:768]
        return carry

    lax.fori_loop(0, 2, qkv_tile, 0)
    first(qkv_p, 0)
    second(proj_p, 1)
    second(fc1_p, 2)

    def normed_back(block):
        row_of = pl.ds(pl.multiple_of(WIDTH + block * ROWS, ROWS), ROWS)
        return dot_nt(fc2_w[row_of, 0:768], fc2_w[0:WIDTH, 0:768])

    mail.sent(got_cols)
    normed_two[0:ROWS, :] = normed_back(cross).astype(BF)
    got_cross = mail.send(normed_two.at[pl.ds(0, ROWS)], part_recv.at[0], "pair")
    far_part = normed_back(far)
    got_cross.wait_recv()
    normed_two[ROWS : 2 * ROWS, :] = (far_part + part_recv[0].astype(F32)).astype(BF)
    got_far = mail.send(normed_two.at[pl.ds(ROWS, ROWS)], n_recv, "far")
    mail.sent(got_grad)
    mlp_grad[0:ROWS, :] = normed_back(pair).astype(BF)
    got_pair = mail.send(mlp_grad.at[pl.ds(0, ROWS)], part_recv.at[1], "pair")
    second(qkv_p, 0)
    third(proj_p, 1)
    third(fc1_p, 2)
    normed_grad = normed_back(own)
    got_pair.wait_recv()
    second(proj_p, 2)
    third(qkv_p, 0)
    got_far.wait_recv()
    normed_grad = normed_grad + n_recv[...].astype(F32) + part_recv[1].astype(F32)
    normed_one, rate = norm_parts(tokens[...].astype(F32))
    vec[0:1, :] = jnp.sum(normed_grad, axis=0, keepdims=True)
    vec[1:2, :] = jnp.sum(normed_grad * normed_one, axis=0, keepdims=True)
    branch[...] = middle[...] + norm_back(
        normed_one, rate, normed_grad * (1.0 + mods[1:2, :])
    )
    out_copy = pltpu.make_async_copy(branch, input_grad, out_sem.at[4])
    out_copy.start()
    second(qkv_p, 1)
    third(proj_p, 2)

    start = 0
    for piece in pieces[:8]:
        width = piece.columns // 2
        for half in range(2):
            fin[high, core, :, start : start + width] = piece.result(half)[...]
            start += width
    to_far = mail.send(fin.at[high, core], fin.at[high, core], "far")
    to_pair = mail.send(fin.at[high, core], fin.at[high, core], "pair")
    third(qkv_p, 1)
    third(qkv_p, 2)
    for k, piece in enumerate(qkv_p):
        for half in range(2):
            fin_q[own, half, :, k * 384 : (k + 1) * 384] = piece.result(half)[...]
    q_far = mail.send(fin_q.at[own], fin_q.at[own], "far")
    q_pair = mail.send(fin_q.at[own], fin_q.at[own], "pair")
    to_far.wait_recv()
    to_pair_two = mail.send(fin.at[1 - high, core], fin.at[1 - high, core], "pair")
    q_far.wait_recv()
    q_pair_two = mail.send(fin_q.at[far], fin_q.at[far], "pair")
    for copy in (to_pair, q_pair, to_pair_two, q_pair_two):
        copy.wait_recv()
    for h in range(2):
        for c in range(2):
            start = 0
            for unit in range(8):
                q, half = FC2_UNITS[unit]
                col = c * 512 + half * 256
                fc2_out[h, q, :, col : col + 256] = fin[h, c, :, start : start + 256]
                start += 256
            fc1_out[h, :, c * half_ff : (c + 1) * half_ff] = fin[
                h, c, :, start : start + half_ff
            ]
            start += half_ff
            proj_out[h, :, c * 512 : (c + 1) * 512] = fin[h, c, :, start : start + 512]
    for s in range(4):
        for h in range(2):
            for j in range(3):
                col = j * WIDTH + s * MINE
                qkv_out[h, :, col : col + MINE] = fin_q[s, h, :, j * MINE : (j + 1) * MINE]
    out_copy.wait()
    mail.finish()
    for piece in pieces:
        piece.finish()


def middle_call(*args):
    shape = jax.ShapeDtypeStruct
    row = 4 * ROWS
    piece_scratch = []
    for k in range(10):
        for phase in range(3):
            dims = Piece.dims(ROUTE_OF[k], phase, COLUMNS_OF[k])
            slots = 4 if ROUTE_OF[k][phase] == "l" else 6
            piece_scratch.append(pltpu.VMEM((slots,) + dims, BF))
    for k in range(8):
        piece_scratch.append(pltpu.VMEM((4, 2, 4, 2, 16, COLUMNS_OF[k]), BF))
    scratch = [
        pltpu.VMEM((WIDTH, WIDTH), BF),
        pltpu.VMEM((WIDTH, 2 * WIDTH), BF),
        pltpu.VMEM((2 * WIDTH, WIDTH), BF),
        pltpu.VMEM((2 * ROWS, WIDTH), BF),
        pltpu.VMEM((2 * ROWS, WIDTH), BF),
        pltpu.VMEM((row, 4 * row), BF),
        pltpu.VMEM((2 * ROWS, WIDTH), BF),
        pltpu.VMEM((2 * ROWS, WIDTH // 2), BF),
        pltpu.VMEM((ROWS, WIDTH), F32),
        pltpu.VMEM((ROWS, WIDTH), F32),
        pltpu.VMEM((2, ROWS, WIDTH), BF),
        pltpu.VMEM((2, ROWS, WIDTH), BF),
        pltpu.VMEM((1, 2 * WIDTH), F32),
        pltpu.VMEM((MINE, row), BF),
        pltpu.VMEM((MINE, row), BF),
        pltpu.VMEM((4, 1, row), F32),
        pltpu.VMEM((4, ROWS, MINE), BF),
        pltpu.VMEM((MINE, ROWS), F32),
        pltpu.VMEM((row, MINE), F32),
        pltpu.VMEM((row, MINE), F32),
        pltpu.VMEM((ROWS, WIDTH), BF),
        pltpu.VMEM((2, 2, 16, FC_COLUMNS), BF),
        pltpu.VMEM((4, 2, 16, 768), BF),
        pltpu.SemaphoreType.DMA((14,)),
        pltpu.SemaphoreType.DMA((5,)),
        pltpu.SemaphoreType.DMA((24,)),
        pltpu.SemaphoreType.DMA((24,)),
        pltpu.SemaphoreType.DMA((10, 3, 6)),
        pltpu.SemaphoreType.DMA((10, 3, 6)),
    ] + piece_scratch
    return pl.pallas_call(
        middle_kernel,
        out_shape=[
            shape((ROWS, WIDTH), F32),
            shape((ROWS, WIDTH), F32),
            shape((16, WIDTH), F32),
            shape((2, 16, 3 * WIDTH), BF),
            shape((2, 16, WIDTH), BF),
            shape((2, 16, 4 * WIDTH), BF),
            shape((2, 4, 16, WIDTH), BF),
        ],
        in_specs=[VMEM, VMEM, VMEM, SMEM, SMEM, SMEM, VMEM, VMEM, VMEM, VMEM] + [ANY] * 12,
        out_specs=[ANY, ANY] + [VMEM] * 5,
        scratch_shapes=scratch,
        compiler_params=pltpu.CompilerParams(
            collective_id=3, has_side_effects=True, vmem_limit_bytes=62 << 20
        ),
        name="middle",
    )(*args)


def tail_kernel(
    vec,
    condition,
    ada_weight,
    cond_grad,
    ada_out,
    sums_out,
    ada,
    share,
    mine_low,
    everyone,
    turned,
    left,
    load_sem,
    send_sem,
    recv_sem,
):
    spot = place()
    x, y, z, core = spot
    bucket = lax.axis_index("bucket")
    x_lo = x % 2
    loads = []
    for j in range(6):
        copy = pltpu.make_async_copy(
            ada_weight.at[:, pl.ds(j * WIDTH, WIDTH)], ada.at[j], load_sem.at[j]
        )
        copy.start()
        loads.append(copy)
    ring = [("y", 1), ("y", -1), ("y", 2), ("l", 0), ("z", 1), ("z", -1), ("z", 2)]
    greet_all(spot, ring, ("pair", "far"))
    mail = Mail(spot, send_sem, recv_sem)

    share[0] = vec[...]
    mail.send(share.at[0], share.at[1], "pair").wait_recv()
    share[2] = share[0] + share[1]
    mail.send(share.at[2], share.at[3], "far").wait_recv()
    total = share[2] + share[3]
    value = condition[...].astype(F32)
    sigma = 1.0 / (1.0 + jnp.exp(-value))
    row = lax.broadcasted_iota(jnp.int32, (16, WIDTH), 0)
    low = jnp.where(row == 14, value * sigma, total).astype(BF)
    mine_low[...] = low

    half = lanes_at(core * 512, 512)
    everyone[z, x_lo, y, :, half] = mine_low[:, half]
    mine = everyone.at[z, x_lo, y, :, half]
    copies = [mail.send_ring(mine, mine, "y", step) for step in (1, -1, 2)]
    for copy in loads:
        copy.wait()
    back = jnp.zeros((1, WIDTH), F32)
    for j in range(6):
        back = back + dot_nt(low, ada[j])[j : j + 1]
    cond_grad[...] = back * (sigma * (1.0 + value * (1.0 - sigma)))
    for copy in copies:
        copy.wait_recv()
    mine = everyone.at[z, x_lo, :, :, half]
    mail.send_ring(mine, mine, "l", 0).wait_recv()
    mine = everyone.at[z, :, :, :, half]
    copies = [mail.send_ring(mine, mine, "z", step) for step in (1, -1, 2)]
    near = [mail.send(mine, mine, "pair")]
    for step, copy in zip((1, -1, 2), copies, strict=True):
        copy.wait_recv()
        mine = everyone.at[(z + 4 - step) % 4, :, :, :, half]
        near.append(mail.send(mine, mine, "pair"))
    for copy in near:
        copy.wait_recv()

    window = everyone[:, :, :, :, lanes_at((bucket // 4) * 128, 128)]
    turned[...] = window.reshape(512, 128).astype(F32).T
    silu = turned[pl.ds(pl.multiple_of((bucket % 4) * 32, 32), 32), :]
    lane = lax.broadcasted_iota(jnp.int32, (32, 512), 1)
    silu = jnp.where(lane % 16 == 14, silu, 0.0)
    for j in range(6):
        left[pl.ds(j * 32, 32), :] = pltpu.roll(silu, 512 + j - 14, 1).astype(BF)
    pick = lax.broadcasted_iota(jnp.int32, (16, 512), 0)
    lane = lax.broadcasted_iota(jnp.int32, (16, 512), 1)
    left[pl.ds(192, 16), :] = jnp.where(lane % 16 == pick, 1.0, 0.0).astype(BF)
    result = dot(left[...], everyone[...].reshape(512, WIDTH))
    for j in range(6):
        ada_out[:, pl.ds(j * WIDTH, WIDTH)] = result[j * 32 : (j + 1) * 32]
    sums_out[...] = result[192:208]
    mail.finish()


def tail_call(vec, condition, ada_weight):
    shape = jax.ShapeDtypeStruct
    return pl.pallas_call(
        tail_kernel,
        out_shape=[
            shape((1, WIDTH), F32),
            shape((32, 6 * WIDTH), F32),
            shape((16, WIDTH), F32),
        ],
        in_specs=[VMEM, VMEM, ANY],
        out_specs=[VMEM] * 3,
        scratch_shapes=[
            pltpu.VMEM((6, WIDTH, WIDTH), BF),
            pltpu.VMEM((4, 16, WIDTH), F32),
            pltpu.VMEM((16, WIDTH), BF),
            pltpu.VMEM((4, 2, 4, 16, WIDTH), BF),
            pltpu.VMEM((128, 512), F32),
            pltpu.VMEM((208, 512), BF),
            pltpu.SemaphoreType.DMA((6,)),
            pltpu.SemaphoreType.DMA((16,)),
            pltpu.SemaphoreType.DMA((16,)),
        ],
        compiler_params=pltpu.CompilerParams(
            collective_id=4, has_side_effects=True, vmem_limit_bytes=60 << 20
        ),
        name="tail",
    )(vec, condition, ada_weight)


def local(
    tokens,
    condition,
    lengths,
    head_mask,
    group_mask,
    token_mask,
    ada_weight,
    ada_bias,
    qkv_weight,
    qv_bias,
    proj_weight,
    proj_bias,
    fc1_weight,
    fc1_bias,
    fc2_weight,
    fc2_bias,
    out_grad,
):
    mods, attended, queries, values, kt, ot, inv, normed, powers = attend(
        tokens[0],
        condition,
        lengths,
        head_mask,
        ada_weight,
        ada_bias[None],
        qkv_weight,
        qv_bias[None],
    )
    block_out, input_grad, vec, qkv_grad, proj_grad, fc1_grad, fc2_grad = middle_call(
        tokens[0],
        out_grad[0],
        mods,
        lengths,
        head_mask,
        group_mask,
        token_mask.reshape(ROWS, 1),
        proj_bias[None],
        fc1_bias[None],
        fc2_bias[None],
        attended,
        proj_weight,
        fc1_weight,
        fc2_weight,
        qkv_weight,
        queries,
        values,
        kt,
        ot,
        inv,
        normed,
        powers,
    )
    cond_grad, ada_grad, sums = tail_call(vec, condition, ada_weight)
    bucket = lax.axis_index("bucket")
    sums = sums.reshape(-1)

    def shard(start, size):
        return lax.dynamic_slice_in_dim(sums, start + bucket * (size // 32), size // 32)

    return (
        block_out[None],
        input_grad[None],
        cond_grad,
        ada_grad,
        shard(0, 6 * WIDTH),
        qkv_grad.reshape(32, 3 * WIDTH).astype(F32),
        shard(6 * WIDTH, 2 * WIDTH),
        proj_grad.reshape(32, WIDTH).astype(F32),
        shard(8 * WIDTH, WIDTH),
        fc1_grad.reshape(32, 4 * WIDTH).astype(F32),
        shard(9 * WIDTH, 4 * WIDTH),
        fc2_grad.reshape(128, WIDTH).astype(F32),
        shard(13 * WIDTH, WIDTH),
    )


def solution(mesh):
    return jax.shard_map(
        local,
        mesh=mesh,
        in_specs=(
            P("bucket", "seq", None),
            P("bucket", None),
            P("bucket", None),
            P("bucket", None),
            P("bucket", None),
            P("bucket", "seq"),
            P(),
            P(),
            P(),
            P(),
            P(),
            P(),
            P(),
            P(),
            P(),
            P(),
            P("bucket", "seq", None),
        ),
        out_specs=(
            P("bucket", "seq", None),
            P("bucket", "seq", None),
            P("bucket", None),
            P("bucket", None),
            P("bucket"),
            P("bucket", None),
            P("bucket"),
            P("bucket", None),
            P("bucket"),
            P("bucket", None),
            P("bucket"),
            P("bucket", None),
            P("bucket"),
        ),
        check_vma=False,
    )
```

```python
import functools

import jax
import jax.numpy as jnp
from jax import lax
from jax.experimental import pallas as pl
from jax.experimental.pallas import tpu as pltpu
from jax.sharding import PartitionSpec as P


MESH_IDS = pl.DeviceIdType.MESH
AXES = {"x": 0, "y": 1, "z": 2}


def place():
    bucket = lax.axis_index("bucket")
    seq = lax.axis_index("seq")
    return (
        (seq // 2) * 2 + (bucket // 4) % 2,
        bucket % 4,
        bucket // 8,
        seq % 2,
    )


def device(x, y, z, core):
    return (z * 8 + (x % 2) * 4 + y, (x // 2) * 2 + core)


def shifted(spot, axis, step):
    x, y, z, core = spot
    if axis == "x":
        x = (x + step) % 4
    elif axis == "y":
        y = (y + step) % 4
    elif axis == "z":
        z = (z + step) % 4
    elif axis == "l":
        x = (x // 2) * 2 + 1 - x % 2
    return device(x, y, z, core)


TORUS = [(axis, step) for axis in "xyz" for step in (1, -1)]


def add_into(target, others):
    total = target[...].astype(jnp.float32)
    for other in others:
        total = total + other[...].astype(jnp.float32)
    target[...] = total.astype(jnp.bfloat16)


class Piece:
    def __init__(self, source, columns, route, landing, send_sem, recv_sem, spot):
        self.source, self.columns, self.route = source, columns, route
        self.landing = landing
        self.send_sem, self.recv_sem, self.spot = send_sem, recv_sem, spot
        self.copies, self.done = {}, []

    @staticmethod
    def dims(route, phase, columns):
        done = route[: phase + 1]
        out = []
        if "z" not in done:
            out.append(4)
        if "x" not in done and "l" not in done:
            out.append(2)
        if "y" not in done:
            out.append(4)
        if "l" in route:
            return tuple(out) + (16, columns)
        if "x" not in done:
            out.append(2)
        return tuple(out) + (16, columns // 2)

    def block(self, phase, target, half):
        done, axis = self.route[:phase], self.route[phase]
        split = "l" in self.route
        index = []
        if "z" not in done:
            index.append(target if axis == "z" else slice(None))
        if "x" not in done and "l" not in done:
            index.append(
                target % 2 if axis == "x" else target if axis == "l" else slice(None)
            )
        if "y" not in done:
            index.append(target if axis == "y" else slice(None))
        if phase == 0:
            if split:
                return self.source.at[tuple(index) + (half,)]
            index.append(target // 2 if axis == "x" else slice(None))
            width = self.columns // 2
            lanes = pl.ds(half * width, width)
            return self.source.at[tuple(index) + (slice(None), lanes)]
        if not split and "x" not in done:
            index.append(target // 2 if axis == "x" else slice(None))
        return self.landing[phase - 1].at[(3 - half,) + tuple(index)]

    def here(self, phase):
        if self.route[phase] == "l":
            return self.spot[0] % 2
        return self.spot[AXES[self.route[phase]]]

    def send(self, phase, slot, ref, step):
        copy = pltpu.make_async_remote_copy(
            src_ref=ref,
            dst_ref=self.landing[phase].at[slot],
            send_sem=self.send_sem.at[phase, slot],
            recv_sem=self.recv_sem.at[phase, slot],
            device_id=shifted(self.spot, self.route[phase], step),
            device_id_type=MESH_IDS,
        )
        copy.start()
        self.copies[phase, slot] = copy

    def first(self, phase):
        a = self.here(phase)
        if self.route[phase] == "l":
            self.send(phase, 2, self.block(phase, 1 - a, 1), 1)
            self.send(phase, 3, self.block(phase, 1 - a, 0), 1)
            return
        self.send(phase, 0, self.block(phase, (a + 2) % 4, 0), 1)
        self.send(phase, 1, self.block(phase, (a + 2) % 4, 1), -1)
        self.send(phase, 2, self.block(phase, (a + 1) % 4, 1), 1)
        self.send(phase, 3, self.block(phase, (a + 3) % 4, 0), -1)

    def second(self, phase):
        if self.route[phase] == "l":
            return
        a = self.here(phase)
        landing = self.landing[phase]
        for slot, step, half in ((0, 1, 0), (1, -1, 1)):
            self.copies[phase, slot].wait_recv()
            add_into(landing.at[slot], [self.block(phase, (a + step) % 4, half)])
            self.send(phase, slot + 4, landing.at[slot], step)

    def third(self, phase):
        a = self.here(phase)
        landing = self.landing[phase]
        for half, slot, other in ((0, 3, 4), (1, 2, 5)):
            self.copies[phase, slot].wait_recv()
            terms = [self.block(phase, a, half)]
            if self.route[phase] != "l":
                self.copies[phase, other].wait_recv()
                terms.append(landing.at[other])
            add_into(landing.at[slot], terms)

    def result(self, half):
        return self.landing[-1].at[3 - half]

    def sent(self, phase):
        for slot in range(4):
            self.copies[phase, slot].wait_send()
            self.done.append((phase, slot))

    def finish(self):
        for key, copy in self.copies.items():
            if key not in self.done:
                copy.wait_send()


BF = jnp.bfloat16
F32 = jnp.float32
VMEM = pl.BlockSpec(memory_space=pltpu.VMEM)
SMEM = pl.BlockSpec(memory_space=pltpu.SMEM)
ANY = pl.BlockSpec(memory_space=pl.ANY)
NT = (((1,), (1,)), ((), ()))
TN = (((0,), (0,)), ((), ()))
WIDTH = 1024
ROWS = 256
HEAD = 64
MINE = 256


def dot(a, b):
    return jnp.dot(a, b, preferred_element_type=F32)


def dot_nt(a, b):
    return lax.dot_general(a, b, NT, preferred_element_type=F32)


def dot_tn(a, b):
    return lax.dot_general(a, b, TN, preferred_element_type=F32)


def norm_parts(values):
    centred = values - jnp.mean(values, axis=-1, keepdims=True)
    rate = lax.rsqrt(jnp.mean(centred * centred, axis=-1, keepdims=True) + 1e-06)
    return centred * rate, rate


def norm_back(normed, rate, grad):
    inner = jnp.mean(grad * normed, axis=-1, keepdims=True)
    return (grad - jnp.mean(grad, axis=-1, keepdims=True) - normed * inner) * rate


def segment(positions, lengths):
    first = lengths[0, 0]
    both = lengths[0, 0] + lengths[0, 1]
    return (positions >= first).astype(jnp.int32) + (positions >= both).astype(jnp.int32)


def quad(spot):
    x, _, _, core = spot
    high = x // 2
    own = high * 2 + core
    pair = high * 2 + (1 - core)
    far = (1 - high) * 2 + core
    cross = (1 - high) * 2 + (1 - core)
    return own, pair, far, cross


def partner(spot, which):
    x, y, z, core = spot
    if which == "pair":
        return device(x, y, z, 1 - core)
    if which == "far":
        return device((x + 2) % 4, y, z, core)
    return device((x + 2) % 4, y, z, 1 - core)


def greet_all(spot, moves, partners):
    barrier = pltpu.get_barrier_semaphore()
    for axis, step in moves:
        pl.semaphore_signal(
            barrier, inc=1, device_id=shifted(spot, axis, step), device_id_type=MESH_IDS
        )
    for which in partners:
        pl.semaphore_signal(barrier, inc=1, device_id=partner(spot, which), device_id_type=MESH_IDS)
    pl.semaphore_wait(barrier, len(moves) + len(partners))


class Mail:
    def __init__(self, spot, send_sem, recv_sem):
        self.spot, self.send_sem, self.recv_sem = spot, send_sem, recv_sem
        self.copies, self.done = [], []

    def send(self, src, dst, which):
        return self.send_to(src, dst, partner(self.spot, which))

    def send_ring(self, src, dst, axis, step):
        return self.send_to(src, dst, shifted(self.spot, axis, step))

    def send_to(self, src, dst, target):
        k = len(self.copies)
        copy = pltpu.make_async_remote_copy(
            src_ref=src,
            dst_ref=dst,
            send_sem=self.send_sem.at[k],
            recv_sem=self.recv_sem.at[k],
            device_id=target,
            device_id_type=MESH_IDS,
        )
        copy.start()
        self.copies.append(copy)
        return copy

    def sent(self, copy):
        copy.wait_send()
        self.done.append(copy)

    def finish(self):
        for copy in self.copies:
            if not any(copy is other for other in self.done):
                copy.wait_send()


def attend_kernel(
    tokens,
    condition,
    lengths,
    head_mask,
    ada_weight,
    ada_bias,
    qkv_weight,
    qv_bias,
    mods,
    attended,
    q_out,
    v_out,
    kt_out,
    ot_out,
    inv_out,
    normed_out,
    plain_out,
    e_out,
    ada,
    weight,
    everyone,
    k_aug,
    vt,
    ctx_t,
    ctx_send,
    ctx_recv,
    e_all,
    load_sem,
    out_sem,
    send_sem,
    recv_sem,
):
    spot = place()
    own, pair, far, cross = quad(spot)
    loads = []
    for j in range(6):
        loads.append(
            pltpu.make_async_copy(
                ada_weight.at[:, pl.ds(j * WIDTH, WIDTH)], ada.at[j], load_sem.at[j]
            )
        )
    for j in range(3):
        start = pl.multiple_of(j * WIDTH + own * MINE, MINE)
        loads.append(
            pltpu.make_async_copy(
                qkv_weight.at[:, pl.ds(start, MINE)],
                weight.at[:, pl.ds(j * MINE, MINE)],
                load_sem.at[6 + j],
            )
        )
    for copy in loads:
        copy.start()
    greet_all(spot, [], ("pair", "far", "cross"))
    mail = Mail(spot, send_sem, recv_sem)
    half = ROWS // 2
    to_far = [
        mail.send(
            tokens.at[pl.ds(i * half, half)], everyone.at[own, pl.ds(i * half, half)], "far"
        )
        for i in range(2)
    ]
    to_pair = mail.send(tokens, everyone.at[own], "pair")

    value = condition[...].astype(F32)
    silu_low = (value / (1.0 + jnp.exp(-value))).astype(BF)
    silu_rows = jnp.broadcast_to(silu_low, (16, WIDTH))
    for j in range(6):
        loads[j].wait()
        row = dot(silu_rows, ada[j])[0:1]
        mods[pl.ds(j, 1), :] = row + ada_bias[pl.ds(j * WIDTH, WIDTH)].astype(F32).reshape(1, WIDTH)
    for copy in loads[6:]:
        copy.wait()

    shift, scale = mods[0:1, :], 1.0 + mods[1:2, :]
    mine = pl.multiple_of(own * MINE, MINE)
    q_bias = qv_bias[pl.ds(mine, MINE)].astype(F32).reshape(1, MINE)
    v_bias = qv_bias[pl.ds(WIDTH + mine, MINE)].astype(F32).reshape(1, MINE)
    lane = lax.broadcasted_iota(jnp.int32, (ROWS, 128), 1)

    def project(block, rows):
        plain = norm_parts(rows[...].astype(F32))[0]
        normed = (plain * scale + shift).astype(BF)
        here = pl.ds(pl.multiple_of(block * ROWS, ROWS), ROWS)
        plain_out[here, :] = plain.astype(BF)
        normed_out[here, :] = normed
        projected = dot(normed, weight[...])
        q_out[here, :] = ((projected[:, :MINE] + q_bias).astype(BF) * 0.125).astype(BF)
        keys = projected[:, MINE : 2 * MINE].astype(BF)
        values = (projected[:, 2 * MINE :] + v_bias).astype(BF)
        spots = segment(block * ROWS + lax.broadcasted_iota(jnp.int32, (ROWS, 128), 0), lengths)
        marks = jnp.where(spots == lane, 1.0, 0.0).astype(BF)
        for p in range(2):
            k_aug[p, here, pl.ds(0, 128)] = keys[:, p * 128 : (p + 1) * 128]
            k_aug[p, here, pl.ds(128, 128)] = marks
        v_out[here, :] = values
        kt_out[:, here] = keys.T
        vt[:, here] = values.T

    project(own, tokens)
    to_pair.wait_recv()
    project(pair, everyone.at[pair])
    forwards = []
    for i in range(2):
        to_far[i].wait_recv()
        piece = everyone.at[far, pl.ds(i * half, half)]
        forwards.append(mail.send(piece, piece, "pair"))
    project(far, everyone.at[far])
    for copy in forwards:
        copy.wait_recv()
    project(cross, everyone.at[cross])

    lanes = lax.broadcasted_iota(jnp.int32, (ROWS, 256), 1)
    out_copies = []
    sends = []
    for n, (block, which) in enumerate(
        ((cross, "cross"), (far, "far"), (pair, "pair"), (own, None))
    ):
        here = pl.ds(pl.multiple_of(block * ROWS, ROWS), ROWS)
        spots = segment(block * ROWS + lax.broadcasted_iota(jnp.int32, (ROWS, 128), 0), lengths)
        marks = jnp.where((spots != lane) & (lane < 3), -1e30, 0.0).astype(BF)

        for h in range(4):
            p = h // 2
            both = jnp.concatenate([q_out[here, p * 128 : (p + 1) * 128], marks], axis=1)
            keep = (lanes // HEAD == h % 2) | (lanes >= 128)
            both = jnp.where(keep, both, jnp.zeros_like(both))
            scores = dot_nt(k_aug[p], both)
            top = jnp.max(scores, axis=0, keepdims=True)
            powers = jnp.exp(scores - top)
            inverse = 1.0 / jnp.sum(powers, axis=0, keepdims=True)
            low = powers.astype(BF)
            e_all[:, pl.ds(pl.multiple_of((block * 4 + h) * ROWS, ROWS), ROWS)] = low
            inv_out[h, :, here] = inverse
            part = slice(h * HEAD, (h + 1) * HEAD)
            out = dot(vt[part, :], low) * inverse
            ot_out[part, here] = out.astype(BF)
            ctx_t[part, :] = out * head_mask[0, own * 4 + h].astype(F32)
        ctx = ctx_t[...].T.astype(BF)
        if which is None:
            ctx_recv[own] = ctx
        else:
            ctx_send[n] = ctx
            sends.append(mail.send(ctx_send.at[n], ctx_recv.at[own], which))
        wide = pl.ds(pl.multiple_of(block * 4 * ROWS, ROWS), 4 * ROWS)
        copy = pltpu.make_async_copy(e_all.at[:, wide], e_out.at[:, wide], out_sem.at[n])
        copy.start()
        out_copies.append(copy)
    for copy in sends:
        copy.wait_recv()
    for s in range(4):
        attended[:, pl.ds(s * MINE, MINE)] = ctx_recv[s]
    for copy in out_copies:
        copy.wait()
    mail.finish()


def attend(
    tokens, condition, lengths, head_mask, ada_weight, ada_bias, qkv_weight, qv_bias
):
    shape = jax.ShapeDtypeStruct
    row = 4 * ROWS
    return pl.pallas_call(
        attend_kernel,
        out_shape=[
            shape((8, WIDTH), F32),
            shape((ROWS, WIDTH), BF),
            shape((row, MINE), BF),
            shape((row, MINE), BF),
            shape((MINE, row), BF),
            shape((MINE, row), BF),
            shape((4, 1, row), F32),
            shape((row, WIDTH), BF),
            shape((row, WIDTH), BF),
            shape((row, 4 * row), BF),
        ],
        in_specs=[VMEM, VMEM, SMEM, SMEM, ANY, VMEM, ANY, VMEM],
        out_specs=[VMEM] * 9 + [ANY],
        scratch_shapes=[
            pltpu.VMEM((6, WIDTH, WIDTH), BF),
            pltpu.VMEM((WIDTH, 3 * MINE), BF),
            pltpu.VMEM((4, ROWS, WIDTH), BF),
            pltpu.VMEM((2, row, 256), BF),
            pltpu.VMEM((MINE, row), BF),
            pltpu.VMEM((MINE, ROWS), F32),
            pltpu.VMEM((3, ROWS, MINE), BF),
            pltpu.VMEM((4, ROWS, MINE), BF),
            pltpu.VMEM((row, 4 * row), BF),
            pltpu.SemaphoreType.DMA((9,)),
            pltpu.SemaphoreType.DMA((4,)),
            pltpu.SemaphoreType.DMA((8,)),
            pltpu.SemaphoreType.DMA((8,)),
        ],
        compiler_params=pltpu.CompilerParams(
            collective_id=2, has_side_effects=True, vmem_limit_bytes=60 << 20
        ),
        name="attend",
    )(tokens, condition, lengths, head_mask, ada_weight, ada_bias, qkv_weight, qv_bias)


ROUTE_OF = ("zyx", "yxz", "xzy", "zyx", "yxz", "xzy", "yxz", "xzy", "zyl", "yzl")
COLUMNS_OF = (768, 768, 512, 768, 512, 768, 256, 256, 384, 384)
FC_COLUMNS = sum(COLUMNS_OF[:8])
FC2_UNITS = ((0, 0), (0, 1), (1, 0), (1, 1), (2, 0), (2, 1), (3, 0), (3, 1))


def lanes_at(start, size):
    return pl.ds(pl.multiple_of(start, 128), size)


def block_rows(index):
    return pl.ds(pl.multiple_of(index * ROWS, ROWS), ROWS)


def middle_kernel(
    tokens,
    out_grad,
    condition,
    mods,
    lengths,
    head_mask,
    group_mask,
    token_mask,
    proj_bias,
    fc1_bias,
    fc2_bias,
    attended,
    proj_weight,
    fc1_weight,
    fc2_weight,
    qkv_weight,
    q_in,
    v_in,
    kt_in,
    ot_in,
    inv_in,
    normed_in,
    plain_in,
    ada_weight,
    e_in,
    block_out,
    input_grad,
    cond_grad,
    ada_out,
    sums_out,
    fin_out,
    fin_q_out,
    proj_w,
    fc1_w,
    fc2_w,
    att,
    normed_two,
    big,
    mlp_grad,
    branch_cols,
    middle,
    branch,
    part_send,
    part_recv,
    channel,
    ot,
    inv,
    do_recv,
    dq_t,
    dk,
    dv,
    n_recv,
    fin,
    fin_q,
    vec,
    share,
    low_vec,
    everyone,
    load_sem,
    out_sem,
    mail_send,
    mail_recv,
    piece_send,
    piece_recv,
    *piece_refs,
):
    spot = place()
    core, high = spot[3], spot[0] // 2
    own, pair, far, cross = quad(spot)
    half_ff = 2 * WIDTH

    def load(k, src, dst):
        copy = pltpu.make_async_copy(src, dst, load_sem.at[k])
        copy.start()
        return copy

    here, there = block_rows(core), block_rows(1 - core)
    load_att = load(0, attended, att.at[here])
    load_proj = load(1, proj_weight, proj_w)
    load_fc1 = load(2, fc1_weight.at[:, lanes_at(core * half_ff, half_ff)], fc1_w)
    load_fc2 = load(
        3, fc2_weight.at[pl.ds(pl.multiple_of(core * half_ff, 256), half_ff), :], fc2_w
    )
    load_heads = [load(5, ot_in, ot), load(6, inv_in, inv)]
    greet_all(spot, TORUS + [("y", 2), ("z", 2)], ("pair", "far", "cross"))
    mail = Mail(spot, mail_send, mail_recv)
    pieces = []
    for k in range(10):
        refs = piece_refs[3 * k : 3 * k + 3]
        if k < 8:
            source = piece_refs[30 + k]
        else:
            source = pieces[0].source.at[..., (k - 8) * 384 : (k - 7) * 384]
        pieces.append(
            Piece(
                source,
                COLUMNS_OF[k],
                ROUTE_OF[k],
                refs,
                piece_send.at[k],
                piece_recv.at[k],
                spot,
            )
        )
    fc2_p, fc1_p, proj_p, qkv_p = pieces[0:3], pieces[3:6], pieces[6:8], pieces[8:10]

    def first(group, phase):
        for piece in group:
            piece.first(phase)

    def second(group, phase):
        for piece in group:
            piece.second(phase)

    def third(group, phase):
        for piece in group:
            piece.third(phase)
            if phase < 2:
                piece.first(phase + 1)

    shift_two, scale_two = mods[3:4, :], 1.0 + mods[4:5, :]
    gate_one, gate_two = mods[2:3, :], mods[5:6, :]
    position = own * ROWS + lax.broadcasted_iota(jnp.int32, (ROWS, 1), 0)
    valid = (position < lengths[0, 0] + lengths[0, 1]).astype(F32)
    kept = valid * jnp.broadcast_to(token_mask[...].astype(F32), (8, ROWS)).T[:, 0:1]
    for g in range(8):
        channel[:, pl.ds(g * 256, 256)] = jnp.full(
            (1, 256), group_mask[0, core * 8 + g].astype(F32), F32
        )
    vec[...] = jnp.zeros_like(vec)

    upstream = out_grad[...].astype(F32)
    low_grad = (kept * gate_two * upstream).astype(BF)
    mlp_grad[here, :] = low_grad
    vec[13:14, :] = jnp.sum(low_grad.astype(F32), axis=0, keepdims=True)
    got_grad = mail.send(mlp_grad.at[here], mlp_grad.at[here], "pair")
    load_att.wait()
    got_att = mail.send(att.at[here], att.at[here], "pair")
    load_proj.wait()
    fresh = dot(att[here, :], proj_w[...]) + proj_bias[...].astype(F32).reshape(1, WIDTH)
    branch[...] = fresh.astype(BF)
    mid = tokens[...].astype(F32) + valid * gate_one * fresh
    middle[...] = mid
    normed_two[here, :] = (norm_parts(mid)[0] * scale_two + shift_two).astype(BF)
    got_normed = mail.send(normed_two.at[here], normed_two.at[here], "pair")
    load_fc1.wait()
    mine = lanes_at(core * half_ff, half_ff)
    TILE = 512

    def hidden(rows):
        def body(i, carry):
            cols = lanes_at(i * TILE, TILE)
            wide = lanes_at(core * half_ff + i * TILE, TILE)
            u = dot(normed_two[rows, :], fc1_w[:, cols]) + fc1_bias[wide].astype(F32).reshape(1, TILE)
            square = u * u
            t = jnp.tanh(0.7978845608028654 * u * (1.0 + 0.044715 * square))
            up = 0.5 * (1.0 + t)
            mask = channel[:, cols]
            big[rows, wide] = (u * up * mask).astype(BF)
            slope = up + 0.5 * u * (1.0 - t * t) * (
                0.7978845608028654 + (3 * 0.7978845608028654 * 0.044715) * square
            )
            low = pl.ds(pl.multiple_of(2 * ROWS + rows.start, ROWS), ROWS)
            big[low, cols] = (slope * mask).astype(BF)
            return carry

        lax.fori_loop(0, half_ff // TILE, body, 0)

    hidden(here)
    got_act = [mail.send(big.at[here, mine], big.at[here, mine], "pair")]
    got_normed.wait_recv()
    hidden(there)
    got_act.append(mail.send(big.at[there, mine], big.at[there, mine], "pair"))
    load_fc2.wait()
    part_send[0] = dot(big[there, mine], fc2_w[...]).astype(BF)
    got_part = mail.send(part_send.at[0], part_recv.at[0], "pair")
    mlp_out = dot(big[here, mine], fc2_w[...]) + fc2_bias[...].astype(F32).reshape(1, WIDTH)
    got_part.wait_recv()
    mlp_out = mlp_out + part_recv[0].astype(F32)

    def stage(result, target):
        copies = []
        for s in range(4):
            cols = pl.ds(s * MINE, MINE)
            dk[s * ROWS : (s + 1) * ROWS, :] = result[:, s * MINE : (s + 1) * MINE]
            copies.append(
                pltpu.make_async_copy(
                    dk.at[pl.ds(s * ROWS, ROWS)], target.at[:, cols], out_sem.at[s]
                )
            )
            copies[s].start()
        return copies

    out_copies = stage(middle[...] + kept * gate_two * mlp_out, block_out)
    vec[5:6, :] = jnp.sum(kept * mlp_out * upstream, axis=0, keepdims=True)

    got_grad.wait_recv()
    for copy in got_act:
        copy.wait_recv()
    half_cols = lanes_at(core * 512, 512)

    def fc2_tile(i, carry):
        t = dot_tn(big[0 : 2 * ROWS, lanes_at(i * 512, 512)], mlp_grad[:, half_cols])
        t = t.astype(BF).reshape(4, 2, 4, 16, 512)
        z, x_lo = i // 2, i % 2
        fc2_p[0].source[z, x_lo, :, :, :, 0:512] = t[:, :, 0]
        fc2_p[0].source[z, x_lo, :, :, :, 512:768] = t[:, :, 1, :, 0:256]
        fc2_p[1].source[z, x_lo, :, :, :, 0:256] = t[:, :, 1, :, 256:512]
        fc2_p[1].source[z, x_lo, :, :, :, 256:768] = t[:, :, 2]
        fc2_p[2].source[z, x_lo] = t[:, :, 3]
        return carry

    lax.fori_loop(0, 8, fc2_tile, 0)
    first(fc2_p, 0)

    def hidden_grad(i, carry):
        cols = lanes_at(i * TILE, TILE)
        low = pl.ds(pl.multiple_of(i * TILE, TILE), TILE)
        grad = dot_nt(mlp_grad[...], fc2_w[low, :])
        grad = (grad * big[2 * ROWS : 4 * ROWS, cols].astype(F32)).astype(BF)
        big[2 * ROWS : 4 * ROWS, lanes_at(half_ff + i * TILE, TILE)] = grad
        total = jnp.sum(grad.astype(F32), axis=0, keepdims=True)
        row = 9 + 2 * core + i // 2
        vec[pl.ds(row, 1), lanes_at((i % 2) * TILE, TILE)] = total
        return carry

    lax.fori_loop(0, half_ff // TILE, hidden_grad, 0)
    low_rows, low_cols = pl.ds(2 * ROWS, 2 * ROWS), pl.ds(half_ff, half_ff)
    load_qkv = [
        load(
            7 + j,
            qkv_weight.at[:, lanes_at(j * WIDTH + own * MINE, MINE)],
            fc2_w.at[pl.ds(0, WIDTH), pl.ds(j * MINE, MINE)],
        )
        for j in range(3)
    ]
    load_heads.append(load(10, q_in, fc2_w.at[pl.ds(0, WIDTH), pl.ds(768, 256)]))
    load_heads.append(load(11, v_in, fc2_w.at[pl.ds(WIDTH, WIDTH), pl.ds(768, 256)]))
    second(fc2_p, 0)

    start = half_ff
    for piece in fc1_p:
        width = piece.columns

        def fc1_tile(i, carry, start=start, width=width, piece=piece):
            t = dot_tn(
                normed_two[:, lanes_at(i * 512, 512)],
                big[2 * ROWS : 4 * ROWS, start : start + width],
            )
            piece.source[pl.ds(i * 2, 2)] = t.astype(BF).reshape(2, 2, 4, 2, 16, width)
            return carry

        lax.fori_loop(0, 2, fc1_tile, 0)
        piece.first(0)
        start += width

    def back(rows):
        low = pl.ds(pl.multiple_of(2 * ROWS + rows.start, ROWS), ROWS)
        return dot_nt(big[low, low_cols], fc1_w[...])

    part_send[1] = back(there).astype(BF)
    got_back = mail.send(part_send.at[1], part_recv.at[1], "pair")
    normed_two_grad = back(here)
    for copy in got_act:
        mail.sent(copy)
    load_e = load(12, e_in, big)
    load_normed = load(13, normed_in, fc1_w.at[:, pl.ds(0, WIDTH)])
    third(fc2_p, 0)
    got_back.wait_recv()
    normed_two_grad = normed_two_grad + part_recv[1].astype(F32)
    normed_mid, rate = norm_parts(middle[...])
    vec[3:4, :] = jnp.sum(normed_two_grad, axis=0, keepdims=True)
    vec[4:5, :] = jnp.sum(normed_two_grad * normed_mid, axis=0, keepdims=True)
    mid_grad = upstream + norm_back(normed_mid, rate, normed_two_grad * scale_two)
    middle[...] = mid_grad
    vec[2:3, :] = jnp.sum(valid * branch[...].astype(F32) * mid_grad, axis=0, keepdims=True)
    branch_grad = (valid * gate_one * mid_grad).astype(BF)
    vec[8:9, :] = jnp.sum(branch_grad.astype(F32), axis=0, keepdims=True)
    mail.sent(got_normed)
    normed_two[here, :] = branch_grad
    branch_cols[here, :] = normed_two[here, half_cols]
    other_cols = lanes_at((1 - core) * 512, 512)
    got_cols = mail.send(normed_two.at[here, other_cols], branch_cols.at[here], "pair")
    context_grad = dot_nt(branch_grad, proj_w[...]).astype(BF)
    mail.sent(got_part)
    part_send[0] = context_grad
    got_do = [
        mail.send(
            part_send.at[0, :, lanes_at(block * MINE, MINE)], do_recv.at[own], which
        )
        for block, which in ((cross, "cross"), (far, "far"), (pair, "pair"))
    ]
    do_recv[own] = part_send[0, :, lanes_at(own * MINE, MINE)]

    got_att.wait_recv()
    got_cols.wait_recv()
    second(fc1_p, 0)

    def proj_tile(i, carry):
        t = dot_tn(att[:, lanes_at(i * 512, 512)], branch_cols[...])
        t = t.astype(BF).reshape(2, 2, 4, 2, 16, 512)
        proj_p[0].source[pl.ds(i * 2, 2)] = t[..., 0:256]
        proj_p[1].source[pl.ds(i * 2, 2)] = t[..., 256:512]
        return carry

    lax.fori_loop(0, 2, proj_tile, 0)
    first(proj_p, 0)
    second(fc2_p, 1)

    mail.sent(got_att)
    mail.sent(got_back)
    load_plain = [
        load(14, plain_in.at[block_rows(cross)], att.at[pl.ds(0, ROWS)]),
        load(16, plain_in.at[block_rows(pair)], part_send.at[1]),
    ]
    load_heads.append(load(4, kt_in, att.at[pl.ds(ROWS, ROWS)]))
    for copy in out_copies:
        copy.wait()
    q_wide, do_wide = proj_w.at[:, 0:MINE], proj_w.at[:, MINE : 2 * MINE]
    for copy in load_heads:
        copy.wait()
    load_e.wait()
    load_normed.wait()
    for copy in load_qkv:
        copy.wait()
    for n, block in enumerate((own, pair, far, cross)):
        if n > 0:
            got_do[3 - n].wait_recv()
        rows = block_rows(block)
        lane = lax.broadcasted_iota(jnp.int32, (ROWS, MINE), 1)
        grad_t = do_recv[block].astype(F32).T
        parts, rests = [], []
        for h in range(4):
            factor = inv[h, :, rows] * head_mask[0, own * 4 + h].astype(F32)
            part = (grad_t[h * HEAD : (h + 1) * HEAD] * factor).astype(BF)
            parts.append(part)
            rests.append(
                jnp.sum(
                    part.astype(F32) * ot[h * HEAD : (h + 1) * HEAD, rows].astype(F32),
                    axis=0,
                    keepdims=True,
                )
            )
        grad_low = jnp.concatenate(parts, axis=0)
        grad_rows = grad_low.astype(F32).T.astype(BF)
        queries = fc2_w[rows, 768:1024]
        zero = jnp.zeros((), BF)
        for h in range(4):
            keep = lane // HEAD == h
            q_wide[h * ROWS : (h + 1) * ROWS, :] = jnp.where(keep, queries, zero)
            do_wide[h * ROWS : (h + 1) * ROWS, :] = jnp.where(keep, grad_rows, zero)
        for h in range(4):
            below = lax.broadcasted_iota(jnp.int32, (MINE, ROWS), 0) // HEAD == h
            masked = jnp.where(below, grad_low, zero)
            prob_grad = dot(fc2_w[WIDTH : 2 * WIDTH, 768:1024], masked)
            powers = big[:, lanes_at((block * 4 + h) * ROWS, ROWS)].astype(F32)
            score_grad = (powers * (prob_grad - rests[h])).astype(BF)
            fc1_w[:, WIDTH + h * ROWS : WIDTH + (h + 1) * ROWS] = score_grad
            dq_t[h * HEAD : (h + 1) * HEAD, :] = dot(
                att[ROWS + h * HEAD : ROWS + (h + 1) * HEAD, :], score_grad
            )
        more_k = dot(fc1_w[:, WIDTH : 2 * WIDTH], q_wide[...])
        more_v = dot(big[:, lanes_at(block * 4 * ROWS, 4 * ROWS)], do_wide[...])
        if n == 0:
            dk[...] = more_k
            dv[...] = more_v
        else:
            dk[...] += more_k
            dv[...] += more_v
        row_of = pl.ds(pl.multiple_of(WIDTH + block * ROWS, ROWS), ROWS)
        fc2_w[row_of, 0:MINE] = (dq_t[...].T * 0.125).astype(BF)
        if n == 0:
            third(fc2_p, 1)
            third(fc1_p, 0)
        elif n == 1:
            for copy in got_do:
                mail.sent(copy)
            load_plain.append(load(15, plain_in.at[block_rows(far)], part_send.at[0]))
            second(proj_p, 0)
            second(fc2_p, 2)
            second(fc1_p, 1)
        elif n == 2:
            third(proj_p, 0)
            third(fc2_p, 2)
            third(fc1_p, 1)
    low = slice(WIDTH, 2 * WIDTH)
    fc2_w[low, MINE : 2 * MINE] = dk[...].astype(BF)
    fc2_w[low, 2 * MINE : 3 * MINE] = dv[...].astype(BF)
    for j, row in ((0, 6), (2, 7)):
        total = jnp.sum(fc2_w[low, j * MINE : (j + 1) * MINE].astype(F32), axis=0, keepdims=True)
        vec[row : row + 1, lanes_at(own * MINE, MINE)] = total

    places = [big.at[:, pl.ds(j * WIDTH, WIDTH)] for j in range(4)]
    places += [proj_w, fc1_w.at[:, pl.ds(WIDTH, WIDTH)]]
    load_ada = [
        load(17 + j, ada_weight.at[:, pl.ds(j * WIDTH, WIDTH)], places[j]) for j in range(6)
    ]
    for copy in load_plain:
        copy.wait()

    def normed_back(block, plain):
        row_of = pl.ds(pl.multiple_of(WIDTH + block * ROWS, ROWS), ROWS)
        grad = dot_nt(fc2_w[row_of, 0:768], fc2_w[0:WIDTH, 0:768])
        vec[0:1, :] += jnp.sum(grad, axis=0, keepdims=True)
        vec[1:2, :] += jnp.sum(grad * plain.astype(F32), axis=0, keepdims=True)
        return grad

    mail.sent(got_cols)
    normed_two[0:ROWS, :] = normed_back(cross, att[0:ROWS, :]).astype(BF)
    got_cross = mail.send(normed_two.at[pl.ds(0, ROWS)], part_recv.at[0], "pair")
    far_part = normed_back(far, part_send[0])
    mail.sent(got_grad)
    mlp_grad[0:ROWS, :] = normed_back(pair, part_send[1]).astype(BF)
    got_pair = mail.send(mlp_grad.at[pl.ds(0, ROWS)], part_recv.at[1], "pair")
    own_part = normed_back(own, norm_parts(tokens[...].astype(F32))[0])
    for s in range(4):
        dv[s * ROWS : (s + 1) * ROWS, :] = own_part[:, s * MINE : (s + 1) * MINE]
    got_vec = mail.send(vec, share.at[0], "pair")
    got_cross.wait_recv()
    normed_two[ROWS : 2 * ROWS, :] = (far_part + part_recv[0].astype(F32)).astype(BF)
    got_vec.wait_recv()
    share[1] = vec[...] + share[0]
    got_vec = mail.send(share.at[1], share.at[2], "far")
    got_far = mail.send(normed_two.at[pl.ds(ROWS, ROWS)], n_recv, "far")

    fc2_p[0].sent(0)

    def qkv_tile(i, carry):
        t = dot_tn(fc1_w[:, lanes_at(i * 512, 512)], fc2_w[WIDTH : 2 * WIDTH, 0:768])
        t = t.astype(BF).reshape(2, 2, 4, 2, 16, 768)
        qkv_p[0].source[pl.ds(i * 2, 2)] = t[..., 0:384]
        qkv_p[1].source[pl.ds(i * 2, 2)] = t[..., 384:768]
        return carry

    lax.fori_loop(0, 2, qkv_tile, 0)
    first(qkv_p, 0)
    second(proj_p, 1)
    second(fc1_p, 2)
    got_vec.wait_recv()
    total = share[1] + share[2]
    value = condition[...].astype(F32)
    sigma = 1.0 / (1.0 + jnp.exp(-value))
    row = lax.broadcasted_iota(jnp.int32, (16, WIDTH), 0)
    low = jnp.where(row == 14, value * sigma, total).astype(BF)
    low_vec[...] = low
    x, y, z = spot[0], spot[1], spot[2]
    x_lo = x % 2
    ring_cols = lanes_at(core * 512, 512)
    everyone[z, x_lo, y, :, ring_cols] = low_vec[:, ring_cols]
    mine = everyone.at[z, x_lo, y, :, ring_cols]
    got_y = [mail.send_ring(mine, mine, "y", step) for step in (1, -1, 2)]
    second(qkv_p, 0)
    third(proj_p, 1)
    third(fc1_p, 2)
    for copy in load_ada:
        copy.wait()
    back_cond = jnp.zeros((1, WIDTH), F32)
    for j in range(6):
        back_cond = back_cond + dot_nt(low, places[j][...])[j : j + 1]
    cond_grad[...] = back_cond * (sigma * (1.0 + value * (1.0 - sigma)))
    for copy in got_y:
        copy.wait_recv()
    mine = everyone.at[z, x_lo, :, :, ring_cols]
    got_l = mail.send_ring(mine, mine, "l", 0)
    second(proj_p, 2)
    third(qkv_p, 0)
    got_l.wait_recv()
    mine = everyone.at[z, :, :, :, ring_cols]
    got_z = [mail.send_ring(mine, mine, "z", step) for step in (1, -1, 2)]
    got_near = [mail.send(mine, mine, "pair")]
    third(proj_p, 2)

    start = 0
    for piece in pieces[:8]:
        width = piece.columns // 2
        for half in range(2):
            fin[high, core, :, start : start + width] = piece.result(half)[...]
            start += width
    to_far = mail.send(fin.at[high, core], fin.at[high, core], "far")
    to_pair = mail.send(fin.at[high, core], fin.at[high, core], "pair")
    second(qkv_p, 1)
    got_pair.wait_recv()
    got_far.wait_recv()
    own_part = jnp.concatenate([dv[s * ROWS : (s + 1) * ROWS, :] for s in range(4)], axis=1)
    normed_grad = own_part + n_recv[...].astype(F32) + part_recv[1].astype(F32)
    normed_one, rate_one = norm_parts(tokens[...].astype(F32))
    result = middle[...] + norm_back(normed_one, rate_one, normed_grad * (1.0 + mods[1:2, :]))
    out_copies = stage(result, input_grad)
    third(qkv_p, 1)
    for step, copy in zip((1, -1, 2), got_z, strict=True):
        copy.wait_recv()
        mine = everyone.at[(z + 4 - step) % 4, :, :, :, ring_cols]
        got_near.append(mail.send(mine, mine, "pair"))
    third(qkv_p, 2)
    for k, piece in enumerate(qkv_p):
        for half in range(2):
            fin_q[own, half, :, k * 384 : (k + 1) * 384] = piece.result(half)[...]
    q_far = mail.send(fin_q.at[own], fin_q.at[own], "far")
    q_pair = mail.send(fin_q.at[own], fin_q.at[own], "pair")
    to_far.wait_recv()
    to_pair_two = mail.send(fin.at[1 - high, core], fin.at[1 - high, core], "pair")
    q_far.wait_recv()
    q_pair_two = mail.send(fin_q.at[far], fin_q.at[far], "pair")
    for copy in got_near:
        copy.wait_recv()

    bucket = lax.axis_index("bucket")
    window = everyone[:, :, :, :, lanes_at((bucket // 4) * 128, 128)]
    turned = window.reshape(512, 128).astype(F32).T
    quarter = pl.multiple_of((bucket % 4) * 32, 32)
    dv[0:128, :] = turned[:, 0:256]
    dv[128:256, :] = turned[:, 256:512]
    silu = jnp.concatenate([dv[pl.ds(quarter, 32), :], dv[pl.ds(quarter + 128, 32), :]], axis=1)
    lane = lax.broadcasted_iota(jnp.int32, (32, 512), 1)
    silu = jnp.where(lane % 16 == 14, silu, 0.0)
    left = [pltpu.roll(silu, 512 + j - 14, 1) for j in range(6)]
    pick = lax.broadcasted_iota(jnp.int32, (16, 512), 0)
    lane = lax.broadcasted_iota(jnp.int32, (16, 512), 1)
    left.append(jnp.where(lane % 16 == pick, 1.0, 0.0))
    product = dot(jnp.concatenate(left, axis=0).astype(BF), everyone[...].reshape(512, WIDTH))
    ada_copies = []
    for j in range(6):
        middle[j * 32 : (j + 1) * 32, :] = product[j * 32 : (j + 1) * 32]
        ada_copies.append(
            pltpu.make_async_copy(
                middle.at[pl.ds(j * 32, 32)],
                ada_out.at[:, pl.ds(j * WIDTH, WIDTH)],
                out_sem.at[7 + j],
            )
        )
        ada_copies[j].start()
    sums_out[...] = product[192:208]
    for copy in (to_pair, q_pair, to_pair_two, q_pair_two):
        copy.wait_recv()
    last_copies = [
        pltpu.make_async_copy(fin, fin_out, out_sem.at[5]),
        pltpu.make_async_copy(fin_q, fin_q_out, out_sem.at[6]),
    ]
    for copy in last_copies:
        copy.start()
    for copy in last_copies + out_copies + ada_copies:
        copy.wait()
    mail.finish()
    for piece in pieces:
        piece.finish()


def middle_call(*args):
    shape = jax.ShapeDtypeStruct
    row = 4 * ROWS
    piece_scratch = []
    for k in range(10):
        for phase in range(3):
            dims = Piece.dims(ROUTE_OF[k], phase, COLUMNS_OF[k])
            slots = 4 if ROUTE_OF[k][phase] == "l" else 6
            piece_scratch.append(pltpu.VMEM((slots,) + dims, BF))
    for k in range(8):
        piece_scratch.append(pltpu.VMEM((4, 2, 4, 2, 16, COLUMNS_OF[k]), BF))
    scratch = [
        pltpu.VMEM((WIDTH, WIDTH), BF),
        pltpu.VMEM((WIDTH, 2 * WIDTH), BF),
        pltpu.VMEM((2 * WIDTH, WIDTH), BF),
        pltpu.VMEM((2 * ROWS, WIDTH), BF),
        pltpu.VMEM((2 * ROWS, WIDTH), BF),
        pltpu.VMEM((row, 4 * row), BF),
        pltpu.VMEM((2 * ROWS, WIDTH), BF),
        pltpu.VMEM((2 * ROWS, WIDTH // 2), BF),
        pltpu.VMEM((ROWS, WIDTH), F32),
        pltpu.VMEM((ROWS, WIDTH), BF),
        pltpu.VMEM((2, ROWS, WIDTH), BF),
        pltpu.VMEM((2, ROWS, WIDTH), BF),
        pltpu.VMEM((1, 2 * WIDTH), F32),
        pltpu.VMEM((MINE, row), BF),
        pltpu.VMEM((4, 1, row), F32),
        pltpu.VMEM((4, ROWS, MINE), BF),
        pltpu.VMEM((MINE, ROWS), F32),
        pltpu.VMEM((row, MINE), F32),
        pltpu.VMEM((row, MINE), F32),
        pltpu.VMEM((ROWS, WIDTH), BF),
        pltpu.VMEM((2, 2, 16, FC_COLUMNS), BF),
        pltpu.VMEM((4, 2, 16, 768), BF),
        pltpu.VMEM((16, WIDTH), F32),
        pltpu.VMEM((3, 16, WIDTH), F32),
        pltpu.VMEM((16, WIDTH), BF),
        pltpu.VMEM((4, 2, 4, 16, WIDTH), BF),
        pltpu.SemaphoreType.DMA((23,)),
        pltpu.SemaphoreType.DMA((13,)),
        pltpu.SemaphoreType.DMA((40,)),
        pltpu.SemaphoreType.DMA((40,)),
        pltpu.SemaphoreType.DMA((10, 3, 6)),
        pltpu.SemaphoreType.DMA((10, 3, 6)),
    ] + piece_scratch
    return pl.pallas_call(
        middle_kernel,
        out_shape=[
            shape((ROWS, WIDTH), F32),
            shape((ROWS, WIDTH), F32),
            shape((1, WIDTH), F32),
            shape((32, 6 * WIDTH), F32),
            shape((16, WIDTH), F32),
            shape((2, 2, 16, FC_COLUMNS), BF),
            shape((4, 2, 16, 768), BF),
        ],
        in_specs=[VMEM] * 4 + [SMEM] * 3 + [VMEM] * 4 + [ANY] * 14,
        out_specs=[ANY, ANY, VMEM, ANY, VMEM, ANY, ANY],
        scratch_shapes=scratch,
        compiler_params=pltpu.CompilerParams(
            collective_id=3, has_side_effects=True, vmem_limit_bytes=63 << 20
        ),
        name="middle",
    )(*args)


def finish_kernel(
    block_in,
    input_in,
    cond_in,
    ada_in,
    sums,
    fin,
    fin_q,
    block_out,
    input_out,
    cond_out,
    ada_out,
    ada_b_out,
    qkv_out,
    qv_out,
    proj_out,
    proj_b_out,
    fc1_out,
    fc1_b_out,
    fc2_out,
    fc2_b_out,
    sem,
):
    copies = [
        pltpu.make_async_copy(src, dst, sem.at[k])
        for k, (src, dst) in enumerate(
            ((block_in, block_out), (input_in, input_out), (ada_in, ada_out))
        )
    ]
    for copy in copies:
        copy.start()
    cond_out[...] = cond_in[...]
    for h in range(2):
        rows = slice(h * 16, (h + 1) * 16)
        for c in range(2):
            start = 0
            for q, half in FC2_UNITS:
                row = h * 64 + q * 16
                col = c * 512 + half * 256
                fc2_out[row : row + 16, col : col + 256] = fin[h, c, :, start : start + 256].astype(
                    F32
                )
                start += 256
            fc1_out[rows, c * 2 * WIDTH : (c + 1) * 2 * WIDTH] = fin[
                h, c, :, start : start + 2 * WIDTH
            ].astype(F32)
            start += 2 * WIDTH
            proj_out[rows, c * 512 : (c + 1) * 512] = fin[h, c, :, start : start + 512].astype(F32)
        for s in range(4):
            for j in range(3):
                col = j * WIDTH + s * MINE
                qkv_out[rows, col : col + MINE] = fin_q[s, h, :, j * MINE : (j + 1) * MINE].astype(
                    F32
                )
    bucket = lax.axis_index("bucket")
    for row, size, dst in (
        (0, 6 * WIDTH, ada_b_out),
        (6, 2 * WIDTH, qv_out),
        (8, WIDTH, proj_b_out),
        (9, 4 * WIDTH, fc1_b_out),
        (13, WIDTH, fc2_b_out),
    ):
        width = size // 32
        line = jnp.concatenate([sums[row + r : row + r + 1, :] for r in range(size // WIDTH)], 1)
        line = jnp.broadcast_to(line, (8, size))
        line = pltpu.roll(line, (size - bucket * width) % size, 1)
        dst[...] = line[0, 0:width]
    for copy in copies:
        copy.wait()


def finish_call(*args):
    shape = jax.ShapeDtypeStruct
    sizes = [
        (ROWS, WIDTH),
        (ROWS, WIDTH),
        (1, WIDTH),
        (32, 6 * WIDTH),
        (6 * WIDTH // 32,),
        (32, 3 * WIDTH),
        (2 * WIDTH // 32,),
        (32, WIDTH),
        (WIDTH // 32,),
        (32, 4 * WIDTH),
        (4 * WIDTH // 32,),
        (128, WIDTH),
        (WIDTH // 32,),
    ]
    spread = (0, 1, 3)
    return pl.pallas_call(
        finish_kernel,
        out_shape=[shape(size, F32) for size in sizes],
        in_specs=[ANY, ANY, VMEM, ANY] + [VMEM] * 3,
        out_specs=[ANY if k in spread else VMEM for k in range(len(sizes))],
        scratch_shapes=[pltpu.SemaphoreType.DMA((3,))],
        compiler_params=pltpu.CompilerParams(vmem_limit_bytes=62 << 20),
        name="finish",
    )(*args)


def run_attend(tokens, condition, lengths, head_mask, ada_weight, ada_bias, qkv_weight, qv_bias):
    return attend(
        tokens[0],
        condition,
        lengths,
        head_mask,
        ada_weight,
        ada_bias,
        qkv_weight,
        qv_bias,
    )


def local(
    tokens,
    condition,
    lengths,
    head_mask,
    group_mask,
    token_mask,
    ada_weight,
    ada_bias,
    qkv_weight,
    qv_bias,
    proj_weight,
    proj_bias,
    fc1_weight,
    fc1_bias,
    fc2_weight,
    fc2_bias,
    out_grad,
):
    mods, attended, queries, values, kt, ot, inv, normed, plain, powers = run_attend(
        tokens, condition, lengths, head_mask, ada_weight, ada_bias, qkv_weight, qv_bias
    )
    block_out, input_grad, cond, ada, sums, fin, fin_q = middle_call(
        tokens[0],
        out_grad[0],
        condition,
        mods,
        lengths,
        head_mask,
        group_mask,
        token_mask,
        proj_bias,
        fc1_bias,
        fc2_bias,
        attended,
        proj_weight,
        fc1_weight,
        fc2_weight,
        qkv_weight,
        queries,
        values,
        kt,
        ot,
        inv,
        normed,
        plain,
        ada_weight,
        powers,
    )
    results = finish_call(block_out, input_grad, cond, ada, sums, fin, fin_q)
    return (results[0][None], results[1][None]) + tuple(results[2:])


def solution(mesh):
    return jax.shard_map(
        local,
        mesh=mesh,
        in_specs=(
            P("bucket", "seq", None),
            P("bucket", None),
            P("bucket", None),
            P("bucket", None),
            P("bucket", None),
            P("bucket", "seq"),
            P(),
            P(),
            P(),
            P(),
            P(),
            P(),
            P(),
            P(),
            P(),
            P(),
            P("bucket", "seq", None),
        ),
        out_specs=(
            P("bucket", "seq", None),
            P("bucket", "seq", None),
            P("bucket", None),
            P("bucket", None),
            P("bucket"),
            P("bucket", None),
            P("bucket"),
            P("bucket", None),
            P("bucket"),
            P("bucket", None),
            P("bucket"),
            P("bucket", None),
            P("bucket"),
        ),
        check_vma=False,
    )
```

```python
import functools

import jax
import jax.numpy as jnp
from jax import lax
from jax.experimental import pallas as pl
from jax.experimental.pallas import tpu as pltpu
from jax.sharding import PartitionSpec as P


MESH_IDS = pl.DeviceIdType.MESH
AXES = {"x": 0, "y": 1, "z": 2}


def place():
    bucket = lax.axis_index("bucket")
    seq = lax.axis_index("seq")
    return (
        (seq // 2) * 2 + (bucket // 4) % 2,
        bucket % 4,
        bucket // 8,
        seq % 2,
    )


def device(x, y, z, core):
    return (z * 8 + (x % 2) * 4 + y, (x // 2) * 2 + core)


def shifted(spot, axis, step):
    x, y, z, core = spot
    if axis == "x":
        x = (x + step) % 4
    elif axis == "y":
        y = (y + step) % 4
    elif axis == "z":
        z = (z + step) % 4
    elif axis == "l":
        x = (x // 2) * 2 + 1 - x % 2
    return device(x, y, z, core)


TORUS = [(axis, step) for axis in "xyz" for step in (1, -1)]


def add_into(target, others):
    total = target[...].astype(jnp.float32)
    for other in others:
        total = total + other[...].astype(jnp.float32)
    target[...] = total.astype(jnp.bfloat16)


class Piece:
    def __init__(self, source, columns, route, landing, send_sem, recv_sem, spot):
        self.source, self.columns, self.route = source, columns, route
        self.landing = landing
        self.send_sem, self.recv_sem, self.spot = send_sem, recv_sem, spot
        self.copies, self.done = {}, []

    @staticmethod
    def dims(route, phase, columns):
        done = route[: phase + 1]
        out = []
        if "z" not in done:
            out.append(4)
        if "x" not in done and "l" not in done:
            out.append(2)
        if "y" not in done:
            out.append(4)
        if "l" in route:
            return tuple(out) + (16, columns)
        if "x" not in done:
            out.append(2)
        return tuple(out) + (16, columns // 2)

    def block(self, phase, target, half):
        done, axis = self.route[:phase], self.route[phase]
        split = "l" in self.route
        index = []
        if "z" not in done:
            index.append(target if axis == "z" else slice(None))
        if "x" not in done and "l" not in done:
            index.append(
                target % 2 if axis == "x" else target if axis == "l" else slice(None)
            )
        if "y" not in done:
            index.append(target if axis == "y" else slice(None))
        if phase == 0:
            if split:
                return self.source.at[tuple(index) + (half,)]
            index.append(target // 2 if axis == "x" else slice(None))
            width = self.columns // 2
            lanes = pl.ds(half * width, width)
            return self.source.at[tuple(index) + (slice(None), lanes)]
        if not split and "x" not in done:
            index.append(target // 2 if axis == "x" else slice(None))
        return self.landing[phase - 1].at[(3 - half,) + tuple(index)]

    def here(self, phase):
        if self.route[phase] == "l":
            return self.spot[0] % 2
        return self.spot[AXES[self.route[phase]]]

    def send(self, phase, slot, ref, step):
        copy = pltpu.make_async_remote_copy(
            src_ref=ref,
            dst_ref=self.landing[phase].at[slot],
            send_sem=self.send_sem.at[phase, slot],
            recv_sem=self.recv_sem.at[phase, slot],
            device_id=shifted(self.spot, self.route[phase], step),
            device_id_type=MESH_IDS,
        )
        copy.start()
        self.copies[phase, slot] = copy

    def first(self, phase):
        a = self.here(phase)
        if self.route[phase] == "l":
            self.send(phase, 2, self.block(phase, 1 - a, 1), 1)
            self.send(phase, 3, self.block(phase, 1 - a, 0), 1)
            return
        self.send(phase, 0, self.block(phase, (a + 2) % 4, 0), 1)
        self.send(phase, 1, self.block(phase, (a + 2) % 4, 1), -1)
        self.send(phase, 2, self.block(phase, (a + 1) % 4, 1), 1)
        self.send(phase, 3, self.block(phase, (a + 3) % 4, 0), -1)

    def second(self, phase):
        if self.route[phase] == "l":
            return
        a = self.here(phase)
        landing = self.landing[phase]
        for slot, step, half in ((0, 1, 0), (1, -1, 1)):
            self.copies[phase, slot].wait_recv()
            add_into(landing.at[slot], [self.block(phase, (a + step) % 4, half)])
            self.send(phase, slot + 4, landing.at[slot], step)

    def third(self, phase):
        a = self.here(phase)
        landing = self.landing[phase]
        for half, slot, other in ((0, 3, 4), (1, 2, 5)):
            self.copies[phase, slot].wait_recv()
            terms = [self.block(phase, a, half)]
            if self.route[phase] != "l":
                self.copies[phase, other].wait_recv()
                terms.append(landing.at[other])
            add_into(landing.at[slot], terms)

    def result(self, half):
        return self.landing[-1].at[3 - half]

    def sent(self, phase):
        for slot in range(4):
            self.copies[phase, slot].wait_send()
            self.done.append((phase, slot))

    def finish(self):
        for key, copy in self.copies.items():
            if key not in self.done:
                copy.wait_send()


BF = jnp.bfloat16
F32 = jnp.float32
VMEM = pl.BlockSpec(memory_space=pltpu.VMEM)
SMEM = pl.BlockSpec(memory_space=pltpu.SMEM)
ANY = pl.BlockSpec(memory_space=pl.ANY)
NT = (((1,), (1,)), ((), ()))
TN = (((0,), (0,)), ((), ()))
WIDTH = 1024
ROWS = 256
HEAD = 64
MINE = 256


def dot(a, b):
    return jnp.dot(a, b, preferred_element_type=F32)


def dot_nt(a, b):
    return lax.dot_general(a, b, NT, preferred_element_type=F32)


def dot_tn(a, b):
    return lax.dot_general(a, b, TN, preferred_element_type=F32)


def down(op, values):
    while values.shape[0] > 8:
        size = values.shape[0] // 2
        values = op(values[:size], values[size:])
    return values


def norm_parts(values):
    centred = values - jnp.mean(values, axis=-1, keepdims=True)
    rate = lax.rsqrt(jnp.mean(centred * centred, axis=-1, keepdims=True) + 1e-06)
    return centred * rate, rate


def norm_back(normed, rate, grad):
    inner = jnp.mean(grad * normed, axis=-1, keepdims=True)
    return (grad - jnp.mean(grad, axis=-1, keepdims=True) - normed * inner) * rate


def segment(positions, lengths):
    first = lengths[0, 0]
    both = lengths[0, 0] + lengths[0, 1]
    return (positions >= first).astype(jnp.int32) + (positions >= both).astype(jnp.int32)


def quad(spot):
    x, _, _, core = spot
    high = x // 2
    own = high * 2 + core
    pair = high * 2 + (1 - core)
    far = (1 - high) * 2 + core
    cross = (1 - high) * 2 + (1 - core)
    return own, pair, far, cross


def partner(spot, which):
    x, y, z, core = spot
    if which == "pair":
        return device(x, y, z, 1 - core)
    if which == "far":
        return device((x + 2) % 4, y, z, core)
    return device((x + 2) % 4, y, z, 1 - core)


def greet_all(spot, moves, partners):
    barrier = pltpu.get_barrier_semaphore()
    for axis, step in moves:
        pl.semaphore_signal(
            barrier, inc=1, device_id=shifted(spot, axis, step), device_id_type=MESH_IDS
        )
    for which in partners:
        pl.semaphore_signal(barrier, inc=1, device_id=partner(spot, which), device_id_type=MESH_IDS)
    pl.semaphore_wait(barrier, len(moves) + len(partners))


class Mail:
    def __init__(self, spot, send_sem, recv_sem):
        self.spot, self.send_sem, self.recv_sem = spot, send_sem, recv_sem
        self.copies, self.done = [], []

    def send(self, src, dst, which):
        return self.send_to(src, dst, partner(self.spot, which))

    def send_ring(self, src, dst, axis, step):
        return self.send_to(src, dst, shifted(self.spot, axis, step))

    def send_to(self, src, dst, target):
        k = len(self.copies)
        copy = pltpu.make_async_remote_copy(
            src_ref=src,
            dst_ref=dst,
            send_sem=self.send_sem.at[k],
            recv_sem=self.recv_sem.at[k],
            device_id=target,
            device_id_type=MESH_IDS,
        )
        copy.start()
        self.copies.append(copy)
        return copy

    def sent(self, copy):
        copy.wait_send()
        self.done.append(copy)

    def finish(self):
        for copy in self.copies:
            if not any(copy is other for other in self.done):
                copy.wait_send()


def attend_kernel(
    tokens,
    condition,
    lengths,
    head_mask,
    ada_weight,
    ada_bias,
    qkv_weight,
    qv_bias,
    mods,
    attended,
    q_out,
    v_out,
    kt_out,
    ot_out,
    inv_out,
    normed_out,
    plain_out,
    e_out,
    ada,
    weight,
    everyone,
    k_aug,
    vt,
    ctx_t,
    ctx_send,
    ctx_recv,
    e_all,
    load_sem,
    out_sem,
    send_sem,
    recv_sem,
):
    spot = place()
    own, pair, far, cross = quad(spot)
    loads = []
    for j in range(6):
        loads.append(
            pltpu.make_async_copy(
                ada_weight.at[:, pl.ds(j * WIDTH, WIDTH)], ada.at[j], load_sem.at[j]
            )
        )
    for j in range(3):
        start = pl.multiple_of(j * WIDTH + own * MINE, MINE)
        loads.append(
            pltpu.make_async_copy(
                qkv_weight.at[:, pl.ds(start, MINE)],
                weight.at[:, pl.ds(j * MINE, MINE)],
                load_sem.at[6 + j],
            )
        )
    for copy in loads:
        copy.start()
    greet_all(spot, [], ("pair", "far", "cross"))
    mail = Mail(spot, send_sem, recv_sem)
    half = ROWS // 2
    to_far = [
        mail.send(
            tokens.at[pl.ds(i * half, half)], everyone.at[own, pl.ds(i * half, half)], "far"
        )
        for i in range(2)
    ]
    to_pair = mail.send(tokens, everyone.at[own], "pair")

    value = condition[...].astype(F32)
    silu_low = (value / (1.0 + jnp.exp(-value))).astype(BF)
    silu_rows = jnp.broadcast_to(silu_low, (16, WIDTH))
    for j in range(6):
        loads[j].wait()
        row = dot(silu_rows, ada[j])[0:1]
        mods[pl.ds(j, 1), :] = row + ada_bias[pl.ds(j * WIDTH, WIDTH)].astype(F32).reshape(1, WIDTH)
    for copy in loads[6:]:
        copy.wait()

    shift, scale = mods[0:1, :], 1.0 + mods[1:2, :]
    mine = pl.multiple_of(own * MINE, MINE)
    q_bias = qv_bias[pl.ds(mine, MINE)].astype(F32).reshape(1, MINE)
    v_bias = qv_bias[pl.ds(WIDTH + mine, MINE)].astype(F32).reshape(1, MINE)
    lane = lax.broadcasted_iota(jnp.int32, (ROWS, 128), 1)

    def project(block, rows):
        plain = norm_parts(rows[...].astype(F32))[0]
        normed = (plain * scale + shift).astype(BF)
        here = pl.ds(pl.multiple_of(block * ROWS, ROWS), ROWS)
        plain_out[here, :] = plain.astype(BF)
        normed_out[here, :] = normed
        projected = dot(normed, weight[...])
        q_out[here, :] = ((projected[:, :MINE] + q_bias).astype(BF) * 0.125).astype(BF)
        keys = projected[:, MINE : 2 * MINE].astype(BF)
        values = (projected[:, 2 * MINE :] + v_bias).astype(BF)
        spots = segment(block * ROWS + lax.broadcasted_iota(jnp.int32, (ROWS, 128), 0), lengths)
        marks = jnp.where(spots == lane, 1.0, 0.0).astype(BF)
        for p in range(2):
            k_aug[p, here, pl.ds(0, 128)] = keys[:, p * 128 : (p + 1) * 128]
            k_aug[p, here, pl.ds(128, 128)] = marks
        v_out[here, :] = values
        kt_out[:, here] = keys.T
        vt[:, here] = values.T

    project(own, tokens)
    to_pair.wait_recv()
    project(pair, everyone.at[pair])
    forwards = []
    for i in range(2):
        to_far[i].wait_recv()
        piece = everyone.at[far, pl.ds(i * half, half)]
        forwards.append(mail.send(piece, piece, "pair"))
    project(far, everyone.at[far])
    for copy in forwards:
        copy.wait_recv()
    project(cross, everyone.at[cross])

    lanes = lax.broadcasted_iota(jnp.int32, (ROWS, 256), 1)
    out_copies = []
    sends = []
    for n, (block, which) in enumerate(
        ((cross, "cross"), (far, "far"), (pair, "pair"), (own, None))
    ):
        here = pl.ds(pl.multiple_of(block * ROWS, ROWS), ROWS)
        spots = segment(block * ROWS + lax.broadcasted_iota(jnp.int32, (ROWS, 128), 0), lengths)
        marks = jnp.where((spots != lane) & (lane < 3), -1e30, 0.0).astype(BF)

        for h in range(4):
            p = h // 2
            both = jnp.concatenate([q_out[here, p * 128 : (p + 1) * 128], marks], axis=1)
            keep = (lanes // HEAD == h % 2) | (lanes >= 128)
            both = jnp.where(keep, both, jnp.zeros_like(both))
            scores = dot_nt(k_aug[p], both)
            top = jnp.max(down(jnp.maximum, scores), axis=0, keepdims=True)
            powers = jnp.exp(scores - top)
            inverse = 1.0 / jnp.sum(down(jnp.add, powers), axis=0, keepdims=True)
            low = powers.astype(BF)
            e_all[:, pl.ds(pl.multiple_of((block * 4 + h) * ROWS, ROWS), ROWS)] = low
            inv_out[h, :, here] = inverse
            part = slice(h * HEAD, (h + 1) * HEAD)
            out = dot(vt[part, :], low) * inverse
            ot_out[part, here] = out.astype(BF)
            ctx_t[part, :] = out * head_mask[0, own * 4 + h].astype(F32)
        ctx = ctx_t[...].T.astype(BF)
        if which is None:
            ctx_recv[own] = ctx
        else:
            ctx_send[n] = ctx
            sends.append(mail.send(ctx_send.at[n], ctx_recv.at[own], which))
        wide = pl.ds(pl.multiple_of(block * 4 * ROWS, ROWS), 4 * ROWS)
        copy = pltpu.make_async_copy(e_all.at[:, wide], e_out.at[:, wide], out_sem.at[n])
        copy.start()
        out_copies.append(copy)
    for copy in sends:
        copy.wait_recv()
    for s in range(4):
        attended[:, pl.ds(s * MINE, MINE)] = ctx_recv[s]
    for copy in out_copies:
        copy.wait()
    mail.finish()


def attend(
    tokens, condition, lengths, head_mask, ada_weight, ada_bias, qkv_weight, qv_bias
):
    shape = jax.ShapeDtypeStruct
    row = 4 * ROWS
    return pl.pallas_call(
        attend_kernel,
        out_shape=[
            shape((8, WIDTH), F32),
            shape((ROWS, WIDTH), BF),
            shape((row, MINE), BF),
            shape((row, MINE), BF),
            shape((MINE, row), BF),
            shape((MINE, row), BF),
            shape((4, 1, row), F32),
            shape((row, WIDTH), BF),
            shape((row, WIDTH), BF),
            shape((row, 4 * row), BF),
        ],
        in_specs=[VMEM, VMEM, SMEM, SMEM, ANY, VMEM, ANY, VMEM],
        out_specs=[VMEM] * 9 + [ANY],
        scratch_shapes=[
            pltpu.VMEM((6, WIDTH, WIDTH), BF),
            pltpu.VMEM((WIDTH, 3 * MINE), BF),
            pltpu.VMEM((4, ROWS, WIDTH), BF),
            pltpu.VMEM((2, row, 256), BF),
            pltpu.VMEM((MINE, row), BF),
            pltpu.VMEM((MINE, ROWS), F32),
            pltpu.VMEM((3, ROWS, MINE), BF),
            pltpu.VMEM((4, ROWS, MINE), BF),
            pltpu.VMEM((row, 4 * row), BF),
            pltpu.SemaphoreType.DMA((9,)),
            pltpu.SemaphoreType.DMA((4,)),
            pltpu.SemaphoreType.DMA((8,)),
            pltpu.SemaphoreType.DMA((8,)),
        ],
        compiler_params=pltpu.CompilerParams(
            collective_id=2, has_side_effects=True, vmem_limit_bytes=60 << 20
        ),
        name="attend",
    )(tokens, condition, lengths, head_mask, ada_weight, ada_bias, qkv_weight, qv_bias)


ROUTE_OF = ("zyx", "yxz", "zyx", "yxz", "xzy", "zyx", "yxz", "zyl", "yzl")
COLUMNS_OF = (1024, 1024, 512, 512, 1024, 256, 256, 384, 384)
PIECES = len(COLUMNS_OF)
FC_PIECES = PIECES - 2
FC_COLUMNS = sum(COLUMNS_OF[:FC_PIECES])
FC2_UNITS = ((0, 0), (0, 1), (1, 0), (1, 1), (2, 0), (2, 1), (3, 0), (3, 1))


def lanes_at(start, size):
    return pl.ds(pl.multiple_of(start, 128), size)


def block_rows(index):
    return pl.ds(pl.multiple_of(index * ROWS, ROWS), ROWS)


def middle_kernel(
    tokens,
    out_grad,
    condition,
    mods,
    lengths,
    head_mask,
    group_mask,
    token_mask,
    proj_bias,
    fc1_bias,
    fc2_bias,
    attended,
    proj_weight,
    fc1_weight,
    fc2_weight,
    qkv_weight,
    q_in,
    v_in,
    kt_in,
    ot_in,
    inv_in,
    normed_in,
    plain_in,
    ada_weight,
    e_in,
    block_out,
    input_grad,
    cond_grad,
    ada_out,
    sums_out,
    fin_out,
    fin_q_out,
    proj_w,
    fc1_w,
    fc2_w,
    att,
    normed_two,
    big,
    mlp_grad,
    branch_cols,
    middle,
    branch,
    part_send,
    part_recv,
    channel,
    ot,
    inv,
    do_recv,
    dq_t,
    dk,
    dv,
    n_recv,
    fin,
    fin_q,
    vec,
    share,
    low_vec,
    everyone,
    load_sem,
    out_sem,
    mail_send,
    mail_recv,
    piece_send,
    piece_recv,
    *piece_refs,
):
    spot = place()
    core, high = spot[3], spot[0] // 2
    own, pair, far, cross = quad(spot)
    half_ff = 2 * WIDTH

    def load(k, src, dst):
        copy = pltpu.make_async_copy(src, dst, load_sem.at[k])
        copy.start()
        return copy

    here, there = block_rows(core), block_rows(1 - core)
    load_att = load(0, attended, att.at[here])
    load_proj = load(1, proj_weight, proj_w)
    load_fc1 = load(2, fc1_weight.at[:, lanes_at(core * half_ff, half_ff)], fc1_w)
    load_fc2 = load(
        3, fc2_weight.at[pl.ds(pl.multiple_of(core * half_ff, 256), half_ff), :], fc2_w
    )
    load_heads = [load(5, ot_in, ot), load(6, inv_in, inv)]
    greet_all(spot, TORUS + [("y", 2), ("z", 2)], ("pair", "far", "cross"))
    mail = Mail(spot, mail_send, mail_recv)
    pieces = []
    for k in range(PIECES):
        refs = piece_refs[3 * k : 3 * k + 3]
        if k < FC_PIECES:
            source = piece_refs[3 * PIECES + k]
        else:
            source = pieces[0].source.at[..., pl.ds((k - FC_PIECES) * 384, 384)]
        pieces.append(
            Piece(
                source,
                COLUMNS_OF[k],
                ROUTE_OF[k],
                refs,
                piece_send.at[k],
                piece_recv.at[k],
                spot,
            )
        )
    fc2_p, fc1_p, proj_p, qkv_p = pieces[0:2], pieces[2:5], pieces[5:7], pieces[7:9]

    def first(group, phase):
        for piece in group:
            piece.first(phase)

    def second(group, phase):
        for piece in group:
            piece.second(phase)

    def third(group, phase):
        for piece in group:
            piece.third(phase)
            if phase < 2:
                piece.first(phase + 1)

    shift_two, scale_two = mods[3:4, :], 1.0 + mods[4:5, :]
    gate_one, gate_two = mods[2:3, :], mods[5:6, :]
    position = own * ROWS + lax.broadcasted_iota(jnp.int32, (ROWS, 1), 0)
    valid = (position < lengths[0, 0] + lengths[0, 1]).astype(F32)
    kept = valid * jnp.broadcast_to(token_mask[...].astype(F32), (8, ROWS)).T[:, 0:1]
    for g in range(8):
        channel[:, pl.ds(g * 256, 256)] = jnp.full(
            (1, 256), group_mask[0, core * 8 + g].astype(F32), F32
        )
    vec[...] = jnp.zeros_like(vec)

    upstream = out_grad[...].astype(F32)
    low_grad = (kept * gate_two * upstream).astype(BF)
    mlp_grad[here, :] = low_grad
    vec[13:14, :] = jnp.sum(low_grad.astype(F32), axis=0, keepdims=True)
    got_grad = mail.send(mlp_grad.at[here], mlp_grad.at[here], "pair")
    load_att.wait()
    got_att = mail.send(att.at[here], att.at[here], "pair")
    load_proj.wait()
    fresh = dot(att[here, :], proj_w[...]) + proj_bias[...].astype(F32).reshape(1, WIDTH)
    branch[...] = fresh.astype(BF)
    mid = tokens[...].astype(F32) + valid * gate_one * fresh
    middle[...] = mid
    normed_two[here, :] = (norm_parts(mid)[0] * scale_two + shift_two).astype(BF)
    got_normed = mail.send(normed_two.at[here], normed_two.at[here], "pair")
    load_fc1.wait()
    mine = lanes_at(core * half_ff, half_ff)
    TILE = 512

    def hidden(rows):
        def body(i, carry):
            cols = lanes_at(i * TILE, TILE)
            wide = lanes_at(core * half_ff + i * TILE, TILE)
            u = dot(normed_two[rows, :], fc1_w[:, cols]) + fc1_bias[wide].astype(F32).reshape(1, TILE)
            square = u * u
            t = jnp.tanh(0.7978845608028654 * u * (1.0 + 0.044715 * square))
            up = 0.5 * (1.0 + t)
            mask = channel[:, cols]
            big[rows, wide] = (u * up * mask).astype(BF)
            slope = up + 0.5 * u * (1.0 - t * t) * (
                0.7978845608028654 + (3 * 0.7978845608028654 * 0.044715) * square
            )
            low = pl.ds(pl.multiple_of(2 * ROWS + rows.start, ROWS), ROWS)
            big[low, cols] = (slope * mask).astype(BF)
            return carry

        lax.fori_loop(0, half_ff // TILE, body, 0)

    hidden(here)
    got_act = [mail.send(big.at[here, mine], big.at[here, mine], "pair")]
    got_normed.wait_recv()
    hidden(there)
    got_act.append(mail.send(big.at[there, mine], big.at[there, mine], "pair"))
    load_fc2.wait()
    part_send[0] = dot(big[there, mine], fc2_w[...]).astype(BF)
    got_part = mail.send(part_send.at[0], part_recv.at[0], "pair")
    mlp_out = dot(big[here, mine], fc2_w[...]) + fc2_bias[...].astype(F32).reshape(1, WIDTH)
    got_part.wait_recv()
    mlp_out = mlp_out + part_recv[0].astype(F32)

    def stage(result, target):
        copies = []
        for s in range(4):
            cols = pl.ds(s * MINE, MINE)
            dk[s * ROWS : (s + 1) * ROWS, :] = result[:, s * MINE : (s + 1) * MINE]
            copies.append(
                pltpu.make_async_copy(
                    dk.at[pl.ds(s * ROWS, ROWS)], target.at[:, cols], out_sem.at[s]
                )
            )
            copies[s].start()
        return copies

    out_copies = stage(middle[...] + kept * gate_two * mlp_out, block_out)
    vec[5:6, :] = jnp.sum(kept * mlp_out * upstream, axis=0, keepdims=True)

    got_grad.wait_recv()
    for copy in got_act:
        copy.wait_recv()
    half_cols = lanes_at(core * 512, 512)

    def fc2_tile(i, carry):
        t = dot_tn(big[0 : 2 * ROWS, lanes_at(i * 512, 512)], mlp_grad[:, half_cols])
        t = t.astype(BF).reshape(4, 2, 4, 16, 512)
        z, x_lo = i // 2, i % 2
        for q in range(4):
            cols = slice((q % 2) * 512, (q % 2 + 1) * 512)
            fc2_p[q // 2].source[z, x_lo, :, :, :, cols] = t[:, :, q]
        return carry

    lax.fori_loop(0, 8, fc2_tile, 0)
    first(fc2_p, 0)

    def hidden_grad(i, carry):
        cols = lanes_at(i * TILE, TILE)
        low = pl.ds(pl.multiple_of(i * TILE, TILE), TILE)
        grad = dot_nt(mlp_grad[...], fc2_w[low, :])
        grad = (grad * big[2 * ROWS : 4 * ROWS, cols].astype(F32)).astype(BF)
        big[2 * ROWS : 4 * ROWS, lanes_at(half_ff + i * TILE, TILE)] = grad
        total = jnp.sum(grad.astype(F32), axis=0, keepdims=True)
        row = 9 + 2 * core + i // 2
        vec[pl.ds(row, 1), lanes_at((i % 2) * TILE, TILE)] = total
        return carry

    lax.fori_loop(0, half_ff // TILE, hidden_grad, 0)
    low_rows, low_cols = pl.ds(2 * ROWS, 2 * ROWS), pl.ds(half_ff, half_ff)
    load_qkv = [
        load(
            7 + j,
            qkv_weight.at[:, lanes_at(j * WIDTH + own * MINE, MINE)],
            fc2_w.at[pl.ds(0, WIDTH), pl.ds(j * MINE, MINE)],
        )
        for j in range(3)
    ]
    load_heads.append(load(10, q_in, fc2_w.at[pl.ds(0, WIDTH), pl.ds(768, 256)]))
    load_heads.append(load(11, v_in, fc2_w.at[pl.ds(WIDTH, WIDTH), pl.ds(768, 256)]))

    def back(rows):
        low = pl.ds(pl.multiple_of(2 * ROWS + rows.start, ROWS), ROWS)
        return dot_nt(big[low, low_cols], fc1_w[...])

    part_send[1] = back(there).astype(BF)
    got_back = mail.send(part_send.at[1], part_recv.at[1], "pair")
    normed_two_grad = back(here)
    second(fc2_p, 0)
    load_normed = load(13, normed_in, fc1_w.at[:, pl.ds(0, WIDTH)])
    got_back.wait_recv()
    normed_two_grad = normed_two_grad + part_recv[1].astype(F32)
    normed_mid, rate = norm_parts(middle[...])
    vec[3:4, :] = jnp.sum(normed_two_grad, axis=0, keepdims=True)
    vec[4:5, :] = jnp.sum(normed_two_grad * normed_mid, axis=0, keepdims=True)
    mid_grad = upstream + norm_back(normed_mid, rate, normed_two_grad * scale_two)
    middle[...] = mid_grad
    vec[2:3, :] = jnp.sum(valid * branch[...].astype(F32) * mid_grad, axis=0, keepdims=True)
    branch_grad = (valid * gate_one * mid_grad).astype(BF)
    vec[8:9, :] = jnp.sum(branch_grad.astype(F32), axis=0, keepdims=True)
    mail.sent(got_back)
    part_send[1] = branch_grad
    branch_cols[here, :] = part_send[1, :, half_cols]
    other_cols = lanes_at((1 - core) * 512, 512)
    got_cols = mail.send(part_send.at[1, :, other_cols], branch_cols.at[here], "pair")
    context_grad = dot_nt(branch_grad, proj_w[...]).astype(BF)
    mail.sent(got_part)
    part_send[0] = context_grad
    got_do = [
        mail.send(
            part_send.at[0, :, lanes_at(block * MINE, MINE)], do_recv.at[own], which
        )
        for block, which in ((cross, "cross"), (far, "far"), (pair, "pair"))
    ]
    do_recv[own] = part_send[0, :, lanes_at(own * MINE, MINE)]

    start = half_ff
    for piece in fc1_p:
        width = piece.columns

        def fc1_tile(i, carry, start=start, width=width, piece=piece):
            t = dot_tn(
                normed_two[:, lanes_at(i * 512, 512)],
                big[2 * ROWS : 4 * ROWS, start : start + width],
            )
            piece.source[pl.ds(i * 2, 2)] = t.astype(BF).reshape(2, 2, 4, 2, 16, width)
            return carry

        lax.fori_loop(0, 2, fc1_tile, 0)
        piece.first(0)
        start += width

    for copy in got_act:
        mail.sent(copy)
    load_e = load(12, e_in, big)

    got_att.wait_recv()
    got_cols.wait_recv()

    def proj_tile(i, carry):
        t = dot_tn(att[:, lanes_at(i * 512, 512)], branch_cols[...])
        t = t.astype(BF).reshape(2, 2, 4, 2, 16, 512)
        proj_p[0].source[pl.ds(i * 2, 2)] = t[..., 0:256]
        proj_p[1].source[pl.ds(i * 2, 2)] = t[..., 256:512]
        return carry

    lax.fori_loop(0, 2, proj_tile, 0)
    first(proj_p, 0)
    third(fc2_p, 0)

    mail.sent(got_att)
    mail.sent(got_cols)
    load_plain = [
        load(14, plain_in.at[block_rows(cross)], att.at[pl.ds(0, ROWS)]),
        load(16, plain_in.at[block_rows(pair)], part_send.at[1]),
    ]
    load_heads.append(load(4, kt_in, att.at[pl.ds(ROWS, ROWS)]))
    for copy in out_copies:
        copy.wait()
    q_wide, do_wide = proj_w.at[:, 0:MINE], proj_w.at[:, MINE : 2 * MINE]
    for copy in load_heads:
        copy.wait()
    load_e.wait()
    load_normed.wait()
    for copy in load_qkv:
        copy.wait()
    for n, block in enumerate((own, pair, far, cross)):
        if n > 0:
            got_do[3 - n].wait_recv()
        rows = block_rows(block)
        lane = lax.broadcasted_iota(jnp.int32, (ROWS, MINE), 1)
        grad_t = do_recv[block].astype(F32).T
        parts, rests = [], []
        for h in range(4):
            factor = inv[h, :, rows] * head_mask[0, own * 4 + h].astype(F32)
            part = (grad_t[h * HEAD : (h + 1) * HEAD] * factor).astype(BF)
            parts.append(part)
            rests.append(
                jnp.sum(
                    part.astype(F32) * ot[h * HEAD : (h + 1) * HEAD, rows].astype(F32),
                    axis=0,
                    keepdims=True,
                )
            )
        grad_low = jnp.concatenate(parts, axis=0)
        grad_rows = grad_low.astype(F32).T.astype(BF)
        queries = fc2_w[rows, 768:1024]
        zero = jnp.zeros((), BF)
        for h in range(4):
            keep = lane // HEAD == h
            q_wide[h * ROWS : (h + 1) * ROWS, :] = jnp.where(keep, queries, zero)
            do_wide[h * ROWS : (h + 1) * ROWS, :] = jnp.where(keep, grad_rows, zero)
        for h in range(4):
            below = lax.broadcasted_iota(jnp.int32, (MINE, ROWS), 0) // HEAD == h
            masked = jnp.where(below, grad_low, zero)
            prob_grad = dot(fc2_w[WIDTH : 2 * WIDTH, 768:1024], masked)
            powers = big[:, lanes_at((block * 4 + h) * ROWS, ROWS)].astype(F32)
            score_grad = (powers * (prob_grad - rests[h])).astype(BF)
            fc1_w[:, WIDTH + h * ROWS : WIDTH + (h + 1) * ROWS] = score_grad
            dq_t[h * HEAD : (h + 1) * HEAD, :] = dot(
                att[ROWS + h * HEAD : ROWS + (h + 1) * HEAD, :], score_grad
            )
        more_k = dot(fc1_w[:, WIDTH : 2 * WIDTH], q_wide[...])
        more_v = dot(big[:, lanes_at(block * 4 * ROWS, 4 * ROWS)], do_wide[...])
        if n == 0:
            dk[...] = more_k
            dv[...] = more_v
        else:
            dk[...] += more_k
            dv[...] += more_v
        row_of = pl.ds(pl.multiple_of(WIDTH + block * ROWS, ROWS), ROWS)
        fc2_w[row_of, 0:MINE] = (dq_t[...].T * 0.125).astype(BF)
        if n == 1:
            for copy in got_do:
                mail.sent(copy)
            load_plain.append(load(15, plain_in.at[block_rows(far)], part_send.at[0]))
            second(fc2_p, 1)
        elif n == 2:
            second(fc1_p, 0)
            second(proj_p, 0)
        elif n == 3:
            third(fc2_p, 1)
    low = slice(WIDTH, 2 * WIDTH)
    fc2_w[low, MINE : 2 * MINE] = dk[...].astype(BF)
    fc2_w[low, 2 * MINE : 3 * MINE] = dv[...].astype(BF)
    for j, row in ((0, 6), (2, 7)):
        total = jnp.sum(fc2_w[low, j * MINE : (j + 1) * MINE].astype(F32), axis=0, keepdims=True)
        vec[row : row + 1, lanes_at(own * MINE, MINE)] = total

    places = [big.at[:, pl.ds(j * WIDTH, WIDTH)] for j in range(4)]
    places += [proj_w, fc1_w.at[:, pl.ds(WIDTH, WIDTH)]]
    load_ada = [
        load(17 + j, ada_weight.at[:, pl.ds(j * WIDTH, WIDTH)], places[j]) for j in range(6)
    ]
    for copy in load_plain:
        copy.wait()

    def normed_back(block, plain):
        row_of = pl.ds(pl.multiple_of(WIDTH + block * ROWS, ROWS), ROWS)
        grad = dot_nt(fc2_w[row_of, 0:768], fc2_w[0:WIDTH, 0:768])
        vec[0:1, :] += jnp.sum(grad, axis=0, keepdims=True)
        vec[1:2, :] += jnp.sum(grad * plain.astype(F32), axis=0, keepdims=True)
        return grad

    mail.sent(got_normed)
    normed_two[0:ROWS, :] = normed_back(cross, att[0:ROWS, :]).astype(BF)
    got_cross = mail.send(normed_two.at[pl.ds(0, ROWS)], part_recv.at[0], "pair")
    far_part = normed_back(far, part_send[0])
    second(fc2_p, 2)
    mail.sent(got_grad)
    mlp_grad[0:ROWS, :] = normed_back(pair, part_send[1]).astype(BF)
    third(proj_p, 0)
    got_pair = mail.send(mlp_grad.at[pl.ds(0, ROWS)], part_recv.at[1], "pair")
    own_part = normed_back(own, norm_parts(tokens[...].astype(F32))[0])
    for s in range(4):
        dv[s * ROWS : (s + 1) * ROWS, :] = own_part[:, s * MINE : (s + 1) * MINE]
    got_vec = mail.send(vec, share.at[0], "pair")
    third(fc1_p, 0)
    got_cross.wait_recv()
    normed_two[ROWS : 2 * ROWS, :] = (far_part + part_recv[0].astype(F32)).astype(BF)
    got_vec.wait_recv()
    share[1] = vec[...] + share[0]
    got_vec = mail.send(share.at[1], share.at[2], "far")
    got_far = mail.send(normed_two.at[pl.ds(ROWS, ROWS)], n_recv, "far")

    fc2_p[0].sent(0)

    def qkv_tile(i, carry):
        t = dot_tn(fc1_w[:, lanes_at(i * 512, 512)], fc2_w[WIDTH : 2 * WIDTH, 0:768])
        t = t.astype(BF).reshape(2, 2, 4, 2, 16, 768)
        qkv_p[0].source[pl.ds(i * 2, 2)] = t[..., 0:384]
        qkv_p[1].source[pl.ds(i * 2, 2)] = t[..., 384:768]
        return carry

    lax.fori_loop(0, 2, qkv_tile, 0)
    first(qkv_p, 0)
    second(proj_p, 1)
    second(fc1_p, 1)
    third(fc2_p, 2)
    got_vec.wait_recv()
    total = share[1] + share[2]
    value = condition[...].astype(F32)
    sigma = 1.0 / (1.0 + jnp.exp(-value))
    row = lax.broadcasted_iota(jnp.int32, (16, WIDTH), 0)
    low = jnp.where(row == 14, value * sigma, total).astype(BF)
    low_vec[...] = low
    x, y, z = spot[0], spot[1], spot[2]
    x_lo = x % 2
    ring_cols = lanes_at(core * 512, 512)
    everyone[z, x_lo, y, :, ring_cols] = low_vec[:, ring_cols]
    mine = everyone.at[z, x_lo, y, :, ring_cols]
    got_y = [mail.send_ring(mine, mine, "y", step) for step in (1, -1, 2)]
    second(qkv_p, 0)
    third(proj_p, 1)
    third(fc1_p, 1)
    for copy in load_ada:
        copy.wait()
    back_cond = jnp.zeros((1, WIDTH), F32)
    for j in range(6):
        back_cond = back_cond + dot_nt(low, places[j][...])[j : j + 1]
    cond_grad[...] = back_cond * (sigma * (1.0 + value * (1.0 - sigma)))
    for copy in got_y:
        copy.wait_recv()
    mine = everyone.at[z, x_lo, :, :, ring_cols]
    got_l = mail.send_ring(mine, mine, "l", 0)
    second(proj_p, 2)
    second(fc1_p, 2)
    third(qkv_p, 0)
    got_l.wait_recv()
    mine = everyone.at[z, :, :, :, ring_cols]
    got_z = [mail.send_ring(mine, mine, "z", step) for step in (1, -1, 2)]
    got_near = [mail.send(mine, mine, "pair")]
    third(proj_p, 2)
    third(fc1_p, 2)

    start = 0
    for piece in pieces[:FC_PIECES]:
        width = piece.columns // 2
        for half in range(2):
            fin[high, core, :, start : start + width] = piece.result(half)[...]
            start += width
    to_far = mail.send(fin.at[high, core], fin.at[high, core], "far")
    to_pair = mail.send(fin.at[high, core], fin.at[high, core], "pair")
    second(qkv_p, 1)
    got_pair.wait_recv()
    got_far.wait_recv()
    own_part = jnp.concatenate([dv[s * ROWS : (s + 1) * ROWS, :] for s in range(4)], axis=1)
    normed_grad = own_part + n_recv[...].astype(F32) + part_recv[1].astype(F32)
    normed_one, rate_one = norm_parts(tokens[...].astype(F32))
    result = middle[...] + norm_back(normed_one, rate_one, normed_grad * (1.0 + mods[1:2, :]))
    out_copies = stage(result, input_grad)
    third(qkv_p, 1)
    for step, copy in zip((1, -1, 2), got_z, strict=True):
        copy.wait_recv()
        mine = everyone.at[(z + 4 - step) % 4, :, :, :, ring_cols]
        got_near.append(mail.send(mine, mine, "pair"))
    third(qkv_p, 2)
    for k, piece in enumerate(qkv_p):
        for half in range(2):
            fin_q[own, half, :, k * 384 : (k + 1) * 384] = piece.result(half)[...]
    q_far = mail.send(fin_q.at[own], fin_q.at[own], "far")
    q_pair = mail.send(fin_q.at[own], fin_q.at[own], "pair")
    to_far.wait_recv()
    to_pair_two = mail.send(fin.at[1 - high, core], fin.at[1 - high, core], "pair")
    q_far.wait_recv()
    q_pair_two = mail.send(fin_q.at[far], fin_q.at[far], "pair")
    for copy in got_near:
        copy.wait_recv()

    bucket = lax.axis_index("bucket")
    window = everyone[:, :, :, :, lanes_at((bucket // 4) * 128, 128)]
    turned = window.reshape(512, 128).astype(F32).T
    quarter = pl.multiple_of((bucket % 4) * 32, 32)
    dv[0:128, :] = turned[:, 0:256]
    dv[128:256, :] = turned[:, 256:512]
    silu = jnp.concatenate([dv[pl.ds(quarter, 32), :], dv[pl.ds(quarter + 128, 32), :]], axis=1)
    lane = lax.broadcasted_iota(jnp.int32, (32, 512), 1)
    silu = jnp.where(lane % 16 == 14, silu, 0.0)
    left = [pltpu.roll(silu, 512 + j - 14, 1) for j in range(6)]
    pick = lax.broadcasted_iota(jnp.int32, (16, 512), 0)
    lane = lax.broadcasted_iota(jnp.int32, (16, 512), 1)
    left.append(jnp.where(lane % 16 == pick, 1.0, 0.0))
    product = dot(jnp.concatenate(left, axis=0).astype(BF), everyone[...].reshape(512, WIDTH))
    ada_copies = []
    for j in range(6):
        middle[j * 32 : (j + 1) * 32, :] = product[j * 32 : (j + 1) * 32]
        ada_copies.append(
            pltpu.make_async_copy(
                middle.at[pl.ds(j * 32, 32)],
                ada_out.at[:, pl.ds(j * WIDTH, WIDTH)],
                out_sem.at[7 + j],
            )
        )
        ada_copies[j].start()
    sums_out[...] = product[192:208]
    for copy in (to_pair, q_pair, to_pair_two, q_pair_two):
        copy.wait_recv()
    last_copies = [
        pltpu.make_async_copy(fin, fin_out, out_sem.at[5]),
        pltpu.make_async_copy(fin_q, fin_q_out, out_sem.at[6]),
    ]
    for copy in last_copies:
        copy.start()
    for copy in last_copies + out_copies + ada_copies:
        copy.wait()
    mail.finish()
    for piece in pieces:
        piece.finish()


def middle_call(*args):
    shape = jax.ShapeDtypeStruct
    row = 4 * ROWS
    piece_scratch = []
    for k in range(PIECES):
        for phase in range(3):
            dims = Piece.dims(ROUTE_OF[k], phase, COLUMNS_OF[k])
            slots = 4 if ROUTE_OF[k][phase] == "l" else 6
            piece_scratch.append(pltpu.VMEM((slots,) + dims, BF))
    for k in range(FC_PIECES):
        piece_scratch.append(pltpu.VMEM((4, 2, 4, 2, 16, COLUMNS_OF[k]), BF))
    scratch = [
        pltpu.VMEM((WIDTH, WIDTH), BF),
        pltpu.VMEM((WIDTH, 2 * WIDTH), BF),
        pltpu.VMEM((2 * WIDTH, WIDTH), BF),
        pltpu.VMEM((2 * ROWS, WIDTH), BF),
        pltpu.VMEM((2 * ROWS, WIDTH), BF),
        pltpu.VMEM((row, 4 * row), BF),
        pltpu.VMEM((2 * ROWS, WIDTH), BF),
        pltpu.VMEM((2 * ROWS, WIDTH // 2), BF),
        pltpu.VMEM((ROWS, WIDTH), F32),
        pltpu.VMEM((ROWS, WIDTH), BF),
        pltpu.VMEM((2, ROWS, WIDTH), BF),
        pltpu.VMEM((2, ROWS, WIDTH), BF),
        pltpu.VMEM((1, 2 * WIDTH), F32),
        pltpu.VMEM((MINE, row), BF),
        pltpu.VMEM((4, 1, row), F32),
        pltpu.VMEM((4, ROWS, MINE), BF),
        pltpu.VMEM((MINE, ROWS), F32),
        pltpu.VMEM((row, MINE), F32),
        pltpu.VMEM((row, MINE), F32),
        pltpu.VMEM((ROWS, WIDTH), BF),
        pltpu.VMEM((2, 2, 16, FC_COLUMNS), BF),
        pltpu.VMEM((4, 2, 16, 768), BF),
        pltpu.VMEM((16, WIDTH), F32),
        pltpu.VMEM((3, 16, WIDTH), F32),
        pltpu.VMEM((16, WIDTH), BF),
        pltpu.VMEM((4, 2, 4, 16, WIDTH), BF),
        pltpu.SemaphoreType.DMA((23,)),
        pltpu.SemaphoreType.DMA((13,)),
        pltpu.SemaphoreType.DMA((40,)),
        pltpu.SemaphoreType.DMA((40,)),
        pltpu.SemaphoreType.DMA((PIECES, 3, 6)),
        pltpu.SemaphoreType.DMA((PIECES, 3, 6)),
    ] + piece_scratch
    return pl.pallas_call(
        middle_kernel,
        out_shape=[
            shape((ROWS, WIDTH), F32),
            shape((ROWS, WIDTH), F32),
            shape((1, WIDTH), F32),
            shape((32, 6 * WIDTH), F32),
            shape((16, WIDTH), F32),
            shape((2, 2, 16, FC_COLUMNS), BF),
            shape((4, 2, 16, 768), BF),
        ],
        in_specs=[VMEM] * 4 + [SMEM] * 3 + [VMEM] * 4 + [ANY] * 14,
        out_specs=[ANY, ANY, VMEM, ANY, VMEM, ANY, ANY],
        scratch_shapes=scratch,
        compiler_params=pltpu.CompilerParams(
            collective_id=3, has_side_effects=True, vmem_limit_bytes=63 << 20
        ),
        name="middle",
    )(*args)


def finish_kernel(
    block_in,
    input_in,
    cond_in,
    ada_in,
    sums,
    fin,
    fin_q,
    block_out,
    input_out,
    cond_out,
    ada_out,
    ada_b_out,
    qkv_out,
    qv_out,
    proj_out,
    proj_b_out,
    fc1_out,
    fc1_b_out,
    fc2_out,
    fc2_b_out,
    block_mid,
    input_mid,
    ada_mid,
    sem,
):
    passing = (
        (block_in, block_mid, block_out),
        (input_in, input_mid, input_out),
        (ada_in, ada_mid, ada_out),
    )
    arriving = [
        pltpu.make_async_copy(src, mid, sem.at[k]) for k, (src, mid, _) in enumerate(passing)
    ]
    copies = [
        pltpu.make_async_copy(mid, dst, sem.at[3 + k]) for k, (_, mid, dst) in enumerate(passing)
    ]
    for copy in arriving:
        copy.start()
    cond_out[...] = cond_in[...]
    for h in range(2):
        rows = slice(h * 16, (h + 1) * 16)
        for c in range(2):
            start = 0
            for q, half in FC2_UNITS:
                row = h * 64 + q * 16
                col = c * 512 + half * 256
                fc2_out[row : row + 16, col : col + 256] = fin[h, c, :, start : start + 256].astype(
                    F32
                )
                start += 256
            fc1_out[rows, c * 2 * WIDTH : (c + 1) * 2 * WIDTH] = fin[
                h, c, :, start : start + 2 * WIDTH
            ].astype(F32)
            start += 2 * WIDTH
            proj_out[rows, c * 512 : (c + 1) * 512] = fin[h, c, :, start : start + 512].astype(F32)
        for s in range(4):
            for j in range(3):
                col = j * WIDTH + s * MINE
                qkv_out[rows, col : col + MINE] = fin_q[s, h, :, j * MINE : (j + 1) * MINE].astype(
                    F32
                )
    for here, there in zip(arriving, copies, strict=True):
        here.wait()
        there.start()
    bucket = lax.axis_index("bucket")
    for row, size, dst in (
        (0, 6 * WIDTH, ada_b_out),
        (6, 2 * WIDTH, qv_out),
        (8, WIDTH, proj_b_out),
        (9, 4 * WIDTH, fc1_b_out),
        (13, WIDTH, fc2_b_out),
    ):
        width = size // 32
        line = jnp.concatenate([sums[row + r : row + r + 1, :] for r in range(size // WIDTH)], 1)
        line = jnp.broadcast_to(line, (8, size))
        line = pltpu.roll(line, (size - bucket * width) % size, 1)
        dst[...] = line[0, 0:width]
    for copy in copies:
        copy.wait()


def finish_call(*args):
    shape = jax.ShapeDtypeStruct
    sizes = [
        (ROWS, WIDTH),
        (ROWS, WIDTH),
        (1, WIDTH),
        (32, 6 * WIDTH),
        (6 * WIDTH // 32,),
        (32, 3 * WIDTH),
        (2 * WIDTH // 32,),
        (32, WIDTH),
        (WIDTH // 32,),
        (32, 4 * WIDTH),
        (4 * WIDTH // 32,),
        (128, WIDTH),
        (WIDTH // 32,),
    ]
    spread = (0, 1, 3)
    return pl.pallas_call(
        finish_kernel,
        out_shape=[shape(size, F32) for size in sizes],
        in_specs=[ANY, ANY, VMEM, ANY] + [VMEM] * 3,
        out_specs=[ANY if k in spread else VMEM for k in range(len(sizes))],
        scratch_shapes=[
            pltpu.VMEM((ROWS, WIDTH), F32),
            pltpu.VMEM((ROWS, WIDTH), F32),
            pltpu.VMEM((32, 6 * WIDTH), F32),
            pltpu.SemaphoreType.DMA((6,)),
        ],
        compiler_params=pltpu.CompilerParams(vmem_limit_bytes=62 << 20),
        name="finish",
    )(*args)


def run_attend(tokens, condition, lengths, head_mask, ada_weight, ada_bias, qkv_weight, qv_bias):
    return attend(
        tokens[0],
        condition,
        lengths,
        head_mask,
        ada_weight,
        ada_bias,
        qkv_weight,
        qv_bias,
    )


def local(
    tokens,
    condition,
    lengths,
    head_mask,
    group_mask,
    token_mask,
    ada_weight,
    ada_bias,
    qkv_weight,
    qv_bias,
    proj_weight,
    proj_bias,
    fc1_weight,
    fc1_bias,
    fc2_weight,
    fc2_bias,
    out_grad,
):
    mods, attended, queries, values, kt, ot, inv, normed, plain, powers = run_attend(
        tokens, condition, lengths, head_mask, ada_weight, ada_bias, qkv_weight, qv_bias
    )
    block_out, input_grad, cond, ada, sums, fin, fin_q = middle_call(
        tokens[0],
        out_grad[0],
        condition,
        mods,
        lengths,
        head_mask,
        group_mask,
        token_mask,
        proj_bias,
        fc1_bias,
        fc2_bias,
        attended,
        proj_weight,
        fc1_weight,
        fc2_weight,
        qkv_weight,
        queries,
        values,
        kt,
        ot,
        inv,
        normed,
        plain,
        ada_weight,
        powers,
    )
    results = finish_call(block_out, input_grad, cond, ada, sums, fin, fin_q)
    return (results[0][None], results[1][None]) + tuple(results[2:])


def solution(mesh):
    return jax.shard_map(
        local,
        mesh=mesh,
        in_specs=(
            P("bucket", "seq", None),
            P("bucket", None),
            P("bucket", None),
            P("bucket", None),
            P("bucket", None),
            P("bucket", "seq"),
            P(),
            P(),
            P(),
            P(),
            P(),
            P(),
            P(),
            P(),
            P(),
            P(),
            P("bucket", "seq", None),
        ),
        out_specs=(
            P("bucket", "seq", None),
            P("bucket", "seq", None),
            P("bucket", None),
            P("bucket", None),
            P("bucket"),
            P("bucket", None),
            P("bucket"),
            P("bucket", None),
            P("bucket"),
            P("bucket", None),
            P("bucket"),
            P("bucket", None),
            P("bucket"),
        ),
        check_vma=False,
    )
```

```python
import functools

import jax
import jax.numpy as jnp
from jax import lax
from jax.experimental import pallas as pl
from jax.experimental.pallas import tpu as pltpu
from jax.sharding import PartitionSpec as P


MESH_IDS = pl.DeviceIdType.MESH
AXES = {"x": 0, "y": 1, "z": 2}


def place():
    bucket = lax.axis_index("bucket")
    seq = lax.axis_index("seq")
    return (
        (seq // 2) * 2 + (bucket // 4) % 2,
        bucket % 4,
        bucket // 8,
        seq % 2,
    )


def device(x, y, z, core):
    return (z * 8 + (x % 2) * 4 + y, (x // 2) * 2 + core)


def shifted(spot, axis, step):
    x, y, z, core = spot
    if axis == "x":
        x = (x + step) % 4
    elif axis == "y":
        y = (y + step) % 4
    elif axis == "z":
        z = (z + step) % 4
    elif axis == "l":
        x = (x // 2) * 2 + 1 - x % 2
    elif axis == "ly":
        x = (x // 2) * 2 + 1 - x % 2
        y = (y + step) % 4
    return device(x, y, z, core)


TORUS = [(axis, step) for axis in "xyz" for step in (1, -1)]


def add_into(target, others):
    total = target[...].astype(jnp.float32)
    for other in others:
        total = total + other[...].astype(jnp.float32)
    target[...] = total.astype(jnp.bfloat16)


class Piece:
    def __init__(self, source, columns, route, landing, send_sem, recv_sem, spot):
        self.source, self.columns, self.route = source, columns, route
        self.landing = landing
        self.send_sem, self.recv_sem, self.spot = send_sem, recv_sem, spot
        self.copies, self.done = {}, []

    @staticmethod
    def dims(route, phase, columns):
        done = route[: phase + 1]
        out = []
        if "z" not in done:
            out.append(4)
        if "x" not in done and "l" not in done:
            out.append(2)
        if "y" not in done:
            out.append(4)
        if "l" in route:
            return tuple(out) + (16, columns)
        if "x" not in done:
            out.append(2)
        return tuple(out) + (16, columns // 2)

    def block(self, phase, target, half):
        done, axis = self.route[:phase], self.route[phase]
        split = "l" in self.route
        index = []
        if "z" not in done:
            index.append(target if axis == "z" else slice(None))
        if "x" not in done and "l" not in done:
            index.append(
                target % 2 if axis == "x" else target if axis == "l" else slice(None)
            )
        if "y" not in done:
            index.append(target if axis == "y" else slice(None))
        if phase == 0:
            if split:
                return self.source.at[tuple(index) + (half,)]
            index.append(target // 2 if axis == "x" else slice(None))
            width = self.columns // 2
            lanes = pl.ds(half * width, width)
            return self.source.at[tuple(index) + (slice(None), lanes)]
        if not split and "x" not in done:
            index.append(target // 2 if axis == "x" else slice(None))
        return self.landing[phase - 1].at[(3 - half,) + tuple(index)]

    def here(self, phase):
        if self.route[phase] == "l":
            return self.spot[0] % 2
        return self.spot[AXES[self.route[phase]]]

    def send(self, phase, slot, ref, step):
        copy = pltpu.make_async_remote_copy(
            src_ref=ref,
            dst_ref=self.landing[phase].at[slot],
            send_sem=self.send_sem.at[phase, slot],
            recv_sem=self.recv_sem.at[phase, slot],
            device_id=shifted(self.spot, self.route[phase], step),
            device_id_type=MESH_IDS,
        )
        copy.start()
        self.copies[phase, slot] = copy

    def first(self, phase):
        a = self.here(phase)
        if self.route[phase] == "l":
            self.send(phase, 2, self.block(phase, 1 - a, 1), 1)
            self.send(phase, 3, self.block(phase, 1 - a, 0), 1)
            return
        if phase > 0:
            for step, slots in ((1, (0, 1)), (-1, (3, 2)), (2, (4, 5))):
                for half in range(2):
                    self.send(phase, slots[half], self.block(phase, (a + step) % 4, half), step)
            return
        self.send(phase, 0, self.block(phase, (a + 2) % 4, 0), 1)
        self.send(phase, 1, self.block(phase, (a + 2) % 4, 1), -1)
        self.send(phase, 2, self.block(phase, (a + 1) % 4, 1), 1)
        self.send(phase, 3, self.block(phase, (a + 3) % 4, 0), -1)

    def second(self, phase):
        if phase > 0:
            return
        a = self.here(phase)
        landing = self.landing[phase]
        for slot, step, half in ((0, 1, 0), (1, -1, 1)):
            self.copies[phase, slot].wait_recv()
            add_into(landing.at[slot], [self.block(phase, (a + step) % 4, half)])
            self.send(phase, slot + 4, landing.at[slot], step)

    def third(self, phase):
        a = self.here(phase)
        landing = self.landing[phase]
        for half, slot, others in ((0, 3, (4, 0)), (1, 2, (5, 1))):
            self.copies[phase, slot].wait_recv()
            terms = [self.block(phase, a, half)]
            if self.route[phase] == "l":
                others = ()
            elif phase == 0:
                others = others[:1]
            for other in others:
                self.copies[phase, other].wait_recv()
                terms.append(landing.at[other])
            add_into(landing.at[slot], terms)

    def result(self, half):
        return self.landing[-1].at[3 - half]

    def sent(self, phase):
        for slot in range(4):
            self.copies[phase, slot].wait_send()
            self.done.append((phase, slot))

    def finish(self):
        for key, copy in self.copies.items():
            if key not in self.done:
                copy.wait_send()


BF = jnp.bfloat16
F32 = jnp.float32
VMEM = pl.BlockSpec(memory_space=pltpu.VMEM)
SMEM = pl.BlockSpec(memory_space=pltpu.SMEM)
ANY = pl.BlockSpec(memory_space=pl.ANY)
NT = (((1,), (1,)), ((), ()))
TN = (((0,), (0,)), ((), ()))
WIDTH = 1024
ROWS = 256
HEAD = 64
MINE = 256


def dot(a, b):
    return jnp.dot(a, b, preferred_element_type=F32)


def dot_nt(a, b):
    return lax.dot_general(a, b, NT, preferred_element_type=F32)


def dot_tn(a, b):
    return lax.dot_general(a, b, TN, preferred_element_type=F32)


def down(op, values):
    while values.shape[0] > 8:
        size = values.shape[0] // 2
        values = op(values[:size], values[size:])
    return values


def lanes_at(start, size):
    return pl.ds(pl.multiple_of(start, 128), size)


def block_rows(index):
    return pl.ds(pl.multiple_of(index * ROWS, ROWS), ROWS)


def norm_parts(values):
    centred = values - jnp.mean(values, axis=-1, keepdims=True)
    rate = lax.rsqrt(jnp.mean(centred * centred, axis=-1, keepdims=True) + 1e-06)
    return centred * rate, rate


def norm_back(normed, rate, grad):
    inner = jnp.mean(grad * normed, axis=-1, keepdims=True)
    return (grad - jnp.mean(grad, axis=-1, keepdims=True) - normed * inner) * rate


def segment(positions, lengths):
    first = lengths[0, 0]
    both = lengths[0, 0] + lengths[0, 1]
    return (positions >= first).astype(jnp.int32) + (positions >= both).astype(jnp.int32)


def quad(spot):
    x, _, _, core = spot
    high = x // 2
    own = high * 2 + core
    pair = high * 2 + (1 - core)
    far = (1 - high) * 2 + core
    cross = (1 - high) * 2 + (1 - core)
    return own, pair, far, cross


def partner(spot, which):
    x, y, z, core = spot
    if which == "pair":
        return device(x, y, z, 1 - core)
    if which == "far":
        return device((x + 2) % 4, y, z, core)
    return device((x + 2) % 4, y, z, 1 - core)


def greet_all(spot, moves, partners):
    barrier = pltpu.get_barrier_semaphore()
    for axis, step in moves:
        pl.semaphore_signal(
            barrier, inc=1, device_id=shifted(spot, axis, step), device_id_type=MESH_IDS
        )
    for which in partners:
        pl.semaphore_signal(barrier, inc=1, device_id=partner(spot, which), device_id_type=MESH_IDS)
    pl.semaphore_wait(barrier, len(moves) + len(partners))


class Mail:
    def __init__(self, spot, send_sem, recv_sem):
        self.spot, self.send_sem, self.recv_sem = spot, send_sem, recv_sem
        self.copies, self.done = [], []

    def send(self, src, dst, which):
        return self.send_to(src, dst, partner(self.spot, which))

    def send_ring(self, src, dst, axis, step):
        return self.send_to(src, dst, shifted(self.spot, axis, step))

    def send_to(self, src, dst, target):
        k = len(self.copies)
        copy = pltpu.make_async_remote_copy(
            src_ref=src,
            dst_ref=dst,
            send_sem=self.send_sem.at[k],
            recv_sem=self.recv_sem.at[k],
            device_id=target,
            device_id_type=MESH_IDS,
        )
        copy.start()
        self.copies.append(copy)
        return copy

    def sent(self, copy):
        copy.wait_send()
        self.done.append(copy)

    def finish(self):
        for copy in self.copies:
            if not any(copy is other for other in self.done):
                copy.wait_send()


def attend_kernel(
    tokens,
    condition,
    lengths,
    head_mask,
    ada_weight,
    ada_bias,
    qkv_weight,
    qv_bias,
    mods,
    attended,
    q_out,
    v_out,
    kt_out,
    ot_out,
    inv_out,
    normed_hbm,
    plain_hbm,
    e_out,
    ada,
    weight,
    everyone,
    k_aug,
    vt,
    ctx_t,
    ctx_send,
    ctx_recv,
    e_all,
    s_buf,
    normed_out,
    plain_out,
    load_sem,
    out_sem,
    send_sem,
    recv_sem,
):
    spot = place()
    own, pair, far, cross = quad(spot)
    loads = []
    for j in range(6):
        loads.append(
            pltpu.make_async_copy(
                ada_weight.at[:, pl.ds(j * WIDTH, WIDTH)], ada.at[j], load_sem.at[j]
            )
        )
    for j in range(3):
        start = pl.multiple_of(j * WIDTH + own * MINE, MINE)
        loads.append(
            pltpu.make_async_copy(
                qkv_weight.at[:, pl.ds(start, MINE)],
                weight.at[:, pl.ds(j * MINE, MINE)],
                load_sem.at[6 + j],
            )
        )
    for copy in loads:
        copy.start()
    greet_all(spot, [], ("pair", "far", "cross"))
    mail = Mail(spot, send_sem, recv_sem)
    half = ROWS // 2
    to_far = [
        mail.send(
            tokens.at[pl.ds(i * half, half)], everyone.at[own, pl.ds(i * half, half)], "far"
        )
        for i in range(2)
    ]
    to_pair = mail.send(tokens, everyone.at[own], "pair")

    value = condition[...].astype(F32)
    silu_low = (value / (1.0 + jnp.exp(-value))).astype(BF)
    silu_rows = jnp.broadcast_to(silu_low, (16, WIDTH))
    for j in range(6):
        loads[j].wait()
        row = dot(silu_rows, ada[j])[0:1]
        mods[pl.ds(j, 1), :] = row + ada_bias[pl.ds(j * WIDTH, WIDTH)].astype(F32).reshape(1, WIDTH)
    for copy in loads[6:]:
        copy.wait()

    shift, scale = mods[0:1, :], 1.0 + mods[1:2, :]
    mine = pl.multiple_of(own * MINE, MINE)
    q_bias = qv_bias[pl.ds(mine, MINE)].astype(F32).reshape(1, MINE)
    v_bias = qv_bias[pl.ds(WIDTH + mine, MINE)].astype(F32).reshape(1, MINE)
    lane = lax.broadcasted_iota(jnp.int32, (ROWS, 128), 1)

    def project(block, rows):
        plain = norm_parts(rows[...].astype(F32))[0]
        normed = (plain * scale + shift).astype(BF)
        here = pl.ds(pl.multiple_of(block * ROWS, ROWS), ROWS)
        plain_out[here, :] = plain.astype(BF)
        normed_out[here, :] = normed
        projected = dot(normed, weight[...])
        q_out[here, :] = ((projected[:, :MINE] + q_bias).astype(BF) * 0.125).astype(BF)
        keys = projected[:, MINE : 2 * MINE].astype(BF)
        values = (projected[:, 2 * MINE :] + v_bias).astype(BF)
        spots = segment(block * ROWS + lax.broadcasted_iota(jnp.int32, (ROWS, 128), 0), lengths)
        marks = jnp.where(spots == lane, 1.0, 0.0).astype(BF)
        for p in range(2):
            k_aug[p, here, pl.ds(0, 128)] = keys[:, p * 128 : (p + 1) * 128]
            k_aug[p, here, pl.ds(128, 128)] = marks
        v_out[here, :] = values
        kt_out[:, here] = keys.T
        vt[:, here] = values.T

    project(own, tokens)
    to_pair.wait_recv()
    project(pair, everyone.at[pair])
    forwards = []
    for i in range(2):
        to_far[i].wait_recv()
        piece = everyone.at[far, pl.ds(i * half, half)]
        forwards.append(mail.send(piece, piece, "pair"))
    project(far, everyone.at[far])
    for copy in forwards:
        copy.wait_recv()
    project(cross, everyone.at[cross])

    lanes = lax.broadcasted_iota(jnp.int32, (ROWS, 256), 1)
    order = ((cross, "cross"), (far, "far"), (pair, "pair"), (own, None))
    out_copies, sends, tops, inverses = [], [], {}, {}
    for k, (src, dst) in enumerate(((normed_out, normed_hbm), (plain_out, plain_hbm))):
        copy = pltpu.make_async_copy(src, dst, out_sem.at[4 + k])
        copy.start()
        out_copies.append(copy)

    def score(i):
        n, h = i // 4, i % 4
        block, p = order[n][0], h // 2
        spots = segment(block * ROWS + lax.broadcasted_iota(jnp.int32, (ROWS, 128), 0), lengths)
        marks = jnp.where((spots != lane) & (lane < 3), -1e30, 0.0).astype(BF)
        queries = q_out[block_rows(block), p * 128 : (p + 1) * 128]
        both = jnp.concatenate([queries, marks], axis=1)
        keep = (lanes // HEAD == h % 2) | (lanes >= 128)
        scores = dot_nt(k_aug[p], jnp.where(keep, both, jnp.zeros_like(both)))
        s_buf[i % 2] = scores
        tops[i] = jnp.max(down(jnp.maximum, scores), axis=0, keepdims=True)

    def soften(i):
        n, h = i // 4, i % 4
        powers = jnp.exp(s_buf[i % 2] - tops[i])
        e_all[:, i * ROWS : (i + 1) * ROWS] = powers.astype(BF)
        inverses[i] = 1.0 / jnp.sum(down(jnp.add, powers), axis=0, keepdims=True)
        inv_out[h, :, block_rows(order[n][0])] = inverses[i]

    def apply(i):
        n, h = i // 4, i % 4
        block, which = order[n]
        part = slice(h * HEAD, (h + 1) * HEAD)
        out = dot(vt[part, :], e_all[:, i * ROWS : (i + 1) * ROWS]) * inverses[i]
        ot_out[part, block_rows(block)] = out.astype(BF)
        ctx_t[n % 2, part, :] = out * head_mask[0, own * 4 + h].astype(F32)
        if h < 3:
            return
        ctx = ctx_t[n % 2].T.astype(BF)
        if which is None:
            ctx_recv[own] = ctx
        else:
            ctx_send[n] = ctx
            sends.append(mail.send(ctx_send.at[n], ctx_recv.at[own], which))
        wide = pl.ds(pl.multiple_of(block * 4 * ROWS, ROWS), 4 * ROWS)
        copy = pltpu.make_async_copy(
            e_all.at[:, pl.ds(n * 4 * ROWS, 4 * ROWS)], e_out.at[:, wide], out_sem.at[n]
        )
        copy.start()
        out_copies.append(copy)

    score(0)
    for i in range(16):
        if i > 0:
            apply(i - 1)
        if i < 15:
            score(i + 1)
        soften(i)
    apply(15)
    for copy in sends:
        copy.wait_recv()
    for s in range(4):
        attended[:, pl.ds(s * MINE, MINE)] = ctx_recv[s]
    for copy in out_copies:
        copy.wait()
    mail.finish()


def attend(
    tokens, condition, lengths, head_mask, ada_weight, ada_bias, qkv_weight, qv_bias
):
    shape = jax.ShapeDtypeStruct
    row = 4 * ROWS
    return pl.pallas_call(
        attend_kernel,
        out_shape=[
            shape((8, WIDTH), F32),
            shape((ROWS, WIDTH), BF),
            shape((row, MINE), BF),
            shape((row, MINE), BF),
            shape((MINE, row), BF),
            shape((MINE, row), BF),
            shape((4, 1, row), F32),
            shape((row, WIDTH), BF),
            shape((row, WIDTH), BF),
            shape((row, 4 * row), BF),
        ],
        in_specs=[VMEM, VMEM, SMEM, SMEM, ANY, VMEM, ANY, VMEM],
        out_specs=[VMEM] * 7 + [ANY] * 3,
        scratch_shapes=[
            pltpu.VMEM((6, WIDTH, WIDTH), BF),
            pltpu.VMEM((WIDTH, 3 * MINE), BF),
            pltpu.VMEM((4, ROWS, WIDTH), BF),
            pltpu.VMEM((2, row, 256), BF),
            pltpu.VMEM((MINE, row), BF),
            pltpu.VMEM((2, MINE, ROWS), F32),
            pltpu.VMEM((3, ROWS, MINE), BF),
            pltpu.VMEM((4, ROWS, MINE), BF),
            pltpu.VMEM((row, 4 * row), BF),
            pltpu.VMEM((2, row, ROWS), F32),
            pltpu.VMEM((row, WIDTH), BF),
            pltpu.VMEM((row, WIDTH), BF),
            pltpu.SemaphoreType.DMA((9,)),
            pltpu.SemaphoreType.DMA((6,)),
            pltpu.SemaphoreType.DMA((8,)),
            pltpu.SemaphoreType.DMA((8,)),
        ],
        compiler_params=pltpu.CompilerParams(
            collective_id=2, has_side_effects=True, vmem_limit_bytes=60 << 20
        ),
        name="attend",
    )(tokens, condition, lengths, head_mask, ada_weight, ada_bias, qkv_weight, qv_bias)


ROUTE_OF = ("zyx", "yxz", "xzy", "zyx", "yxz", "xzy", "zyx", "yxz", "zyl", "yzl")
COLUMNS_OF = (768, 768, 512, 512, 512, 1024, 256, 256, 384, 384)
PIECES = len(COLUMNS_OF)
FC_PIECES = PIECES - 2
FC_COLUMNS = sum(COLUMNS_OF[:FC_PIECES])
FC2_UNITS = ((0, 0), (0, 1), (1, 0), (1, 1), (2, 0), (2, 1), (3, 0), (3, 1))


def middle_kernel(
    tokens,
    out_grad,
    condition,
    mods,
    lengths,
    head_mask,
    group_mask,
    token_mask,
    proj_bias,
    fc1_bias,
    fc2_bias,
    attended,
    proj_weight,
    fc1_weight,
    fc2_weight,
    qkv_weight,
    q_in,
    v_in,
    kt_in,
    ot_in,
    inv_in,
    normed_in,
    plain_in,
    ada_weight,
    e_in,
    block_out,
    input_grad,
    cond_grad,
    ada_out,
    sums_out,
    fin_out,
    fin_q_out,
    proj_w,
    fc1_w,
    fc2_w,
    att,
    normed_two,
    big,
    mlp_grad,
    branch_cols,
    middle,
    branch,
    part_send,
    part_recv,
    channel,
    ot,
    inv,
    do_recv,
    dq_t,
    dk,
    dv,
    n_recv,
    fin,
    fin_q,
    vec,
    share,
    low_vec,
    everyone,
    load_sem,
    out_sem,
    mail_send,
    mail_recv,
    piece_send,
    piece_recv,
    *piece_refs,
):
    spot = place()
    core, high = spot[3], spot[0] // 2
    own, pair, far, cross = quad(spot)
    half_ff = 2 * WIDTH

    def load(k, src, dst):
        copy = pltpu.make_async_copy(src, dst, load_sem.at[k])
        copy.start()
        return copy

    here, there = block_rows(core), block_rows(1 - core)
    load_att = load(0, attended, att.at[here])
    load_proj = load(1, proj_weight, proj_w)
    load_fc1 = load(2, fc1_weight.at[:, lanes_at(core * half_ff, half_ff)], fc1_w)
    load_fc2 = load(
        3, fc2_weight.at[pl.ds(pl.multiple_of(core * half_ff, 256), half_ff), :], fc2_w
    )
    load_heads = [load(5, ot_in, ot), load(6, inv_in, inv)]
    greet_all(spot, TORUS + [("y", 2), ("z", 2), ("ly", 1), ("ly", -1), ("ly", 2)], ("pair", "far", "cross"))
    mail = Mail(spot, mail_send, mail_recv)
    pieces = []
    for k in range(PIECES):
        refs = piece_refs[3 * k : 3 * k + 3]
        if k < FC_PIECES:
            source = piece_refs[3 * PIECES + k]
        else:
            source = pieces[0].source.at[..., pl.ds((k - FC_PIECES) * 384, 384)]
        pieces.append(
            Piece(
                source,
                COLUMNS_OF[k],
                ROUTE_OF[k],
                refs,
                piece_send.at[k],
                piece_recv.at[k],
                spot,
            )
        )
    fc2_p, fc1_p, proj_p, qkv_p = pieces[0:3], pieces[3:6], pieces[6:8], pieces[8:10]

    def first(group, phase):
        for piece in group:
            piece.first(phase)

    def second(group, phase):
        for piece in group:
            piece.second(phase)

    def third(group, phase):
        for piece in group:
            piece.third(phase)
            if phase < 2:
                piece.first(phase + 1)

    shift_two, scale_two = mods[3:4, :], 1.0 + mods[4:5, :]
    gate_one, gate_two = mods[2:3, :], mods[5:6, :]
    position = own * ROWS + lax.broadcasted_iota(jnp.int32, (ROWS, 1), 0)
    valid = (position < lengths[0, 0] + lengths[0, 1]).astype(F32)
    kept = valid * jnp.broadcast_to(token_mask[...].astype(F32), (8, ROWS)).T[:, 0:1]
    for g in range(8):
        channel[:, pl.ds(g * 256, 256)] = jnp.full(
            (1, 256), group_mask[0, core * 8 + g].astype(F32), F32
        )
    vec[...] = jnp.zeros_like(vec)

    upstream = out_grad[...].astype(F32)
    low_grad = (kept * gate_two * upstream).astype(BF)
    mlp_grad[here, :] = low_grad
    vec[13:14, :] = jnp.sum(low_grad.astype(F32), axis=0, keepdims=True)
    got_grad = mail.send(mlp_grad.at[here], mlp_grad.at[here], "pair")
    load_att.wait()
    got_att = mail.send(att.at[here], att.at[here], "pair")
    load_proj.wait()
    fresh = dot(att[here, :], proj_w[...]) + proj_bias[...].astype(F32).reshape(1, WIDTH)
    branch[...] = fresh.astype(BF)
    mid = tokens[...].astype(F32) + valid * gate_one * fresh
    middle[...] = mid
    normed_two[here, :] = (norm_parts(mid)[0] * scale_two + shift_two).astype(BF)
    got_normed = mail.send(normed_two.at[here], normed_two.at[here], "pair")
    load_fc1.wait()
    mine = lanes_at(core * half_ff, half_ff)
    TILE = 512

    def hidden(rows):
        def body(i, carry):
            cols = lanes_at(i * TILE, TILE)
            wide = lanes_at(core * half_ff + i * TILE, TILE)
            u = dot(normed_two[rows, :], fc1_w[:, cols]) + fc1_bias[wide].astype(F32).reshape(1, TILE)
            square = u * u
            t = jnp.tanh(0.7978845608028654 * u * (1.0 + 0.044715 * square))
            up = 0.5 * (1.0 + t)
            mask = channel[:, cols]
            big[rows, wide] = (u * up * mask).astype(BF)
            slope = up + 0.5 * u * (1.0 - t * t) * (
                0.7978845608028654 + (3 * 0.7978845608028654 * 0.044715) * square
            )
            low = pl.ds(pl.multiple_of(2 * ROWS + rows.start, ROWS), ROWS)
            big[low, cols] = (slope * mask).astype(BF)
            return carry

        lax.fori_loop(0, half_ff // TILE, body, 0, unroll=True)

    hidden(here)
    got_act = [mail.send(big.at[here, mine], big.at[here, mine], "pair")]
    got_normed.wait_recv()
    hidden(there)
    got_act.append(mail.send(big.at[there, mine], big.at[there, mine], "pair"))
    load_fc2.wait()
    part_send[0] = dot(big[there, mine], fc2_w[...]).astype(BF)
    got_part = mail.send(part_send.at[0], part_recv.at[0], "pair")
    mlp_out = dot(big[here, mine], fc2_w[...]) + fc2_bias[...].astype(F32).reshape(1, WIDTH)
    got_part.wait_recv()
    mlp_out = mlp_out + part_recv[0].astype(F32)

    def stage(result, target):
        copies = []
        for s in range(4):
            cols = pl.ds(s * MINE, MINE)
            dk[s * ROWS : (s + 1) * ROWS, :] = result[:, s * MINE : (s + 1) * MINE]
            copies.append(
                pltpu.make_async_copy(
                    dk.at[pl.ds(s * ROWS, ROWS)], target.at[:, cols], out_sem.at[s]
                )
            )
            copies[s].start()
        return copies

    out_copies = stage(middle[...] + kept * gate_two * mlp_out, block_out)
    vec[5:6, :] = jnp.sum(kept * mlp_out * upstream, axis=0, keepdims=True)

    got_grad.wait_recv()
    for copy in got_act:
        copy.wait_recv()
    half_cols = lanes_at(core * 512, 512)

    def fc2_tile(i, carry):
        t = dot_tn(big[0 : 2 * ROWS, lanes_at(i * 512, 512)], mlp_grad[:, half_cols])
        t = t.astype(BF).reshape(4, 2, 4, 16, 512)
        z, x_lo = i // 2, i % 2
        fc2_p[0].source[z, x_lo, :, :, :, 0:512] = t[:, :, 0]
        fc2_p[0].source[z, x_lo, :, :, :, 512:768] = t[:, :, 1, :, 0:256]
        fc2_p[1].source[z, x_lo, :, :, :, 0:256] = t[:, :, 1, :, 256:512]
        fc2_p[1].source[z, x_lo, :, :, :, 256:768] = t[:, :, 2]
        fc2_p[2].source[z, x_lo] = t[:, :, 3]
        return carry

    lax.fori_loop(0, 8, fc2_tile, 0)
    first(fc2_p, 0)

    def hidden_grad(i, carry):
        cols = lanes_at(i * TILE, TILE)
        low = pl.ds(pl.multiple_of(i * TILE, TILE), TILE)
        grad = dot_nt(mlp_grad[...], fc2_w[low, :])
        grad = (grad * big[2 * ROWS : 4 * ROWS, cols].astype(F32)).astype(BF)
        big[2 * ROWS : 4 * ROWS, lanes_at(half_ff + i * TILE, TILE)] = grad
        total = jnp.sum(grad.astype(F32), axis=0, keepdims=True)
        row = 9 + 2 * core + i // 2
        vec[pl.ds(row, 1), lanes_at((i % 2) * TILE, TILE)] = total
        return carry

    lax.fori_loop(0, half_ff // TILE, hidden_grad, 0, unroll=True)
    low_rows, low_cols = pl.ds(2 * ROWS, 2 * ROWS), pl.ds(half_ff, half_ff)
    load_qkv = [
        load(
            7 + j,
            qkv_weight.at[:, lanes_at(j * WIDTH + own * MINE, MINE)],
            fc2_w.at[pl.ds(0, WIDTH), pl.ds(j * MINE, MINE)],
        )
        for j in range(3)
    ]
    load_heads.append(load(10, q_in, fc2_w.at[pl.ds(0, WIDTH), pl.ds(768, 256)]))
    load_heads.append(load(11, v_in, fc2_w.at[pl.ds(WIDTH, WIDTH), pl.ds(768, 256)]))

    def back(rows):
        low = pl.ds(pl.multiple_of(2 * ROWS + rows.start, ROWS), ROWS)
        return dot_nt(big[low, low_cols], fc1_w[...])

    part_send[1] = back(there).astype(BF)
    got_back = mail.send(part_send.at[1], part_recv.at[1], "pair")
    normed_two_grad = back(here)
    second(fc2_p, 0)
    load_normed = load(13, normed_in, fc1_w.at[:, pl.ds(0, WIDTH)])
    got_back.wait_recv()
    normed_two_grad = normed_two_grad + part_recv[1].astype(F32)
    normed_mid, rate = norm_parts(middle[...])
    vec[3:4, :] = jnp.sum(normed_two_grad, axis=0, keepdims=True)
    vec[4:5, :] = jnp.sum(normed_two_grad * normed_mid, axis=0, keepdims=True)
    mid_grad = upstream + norm_back(normed_mid, rate, normed_two_grad * scale_two)
    middle[...] = mid_grad
    vec[2:3, :] = jnp.sum(valid * branch[...].astype(F32) * mid_grad, axis=0, keepdims=True)
    branch_grad = (valid * gate_one * mid_grad).astype(BF)
    vec[8:9, :] = jnp.sum(branch_grad.astype(F32), axis=0, keepdims=True)
    mail.sent(got_back)
    part_send[1] = branch_grad
    branch_cols[here, :] = part_send[1, :, half_cols]
    other_cols = lanes_at((1 - core) * 512, 512)
    got_cols = mail.send(part_send.at[1, :, other_cols], branch_cols.at[here], "pair")
    context_grad = dot_nt(branch_grad, proj_w[...]).astype(BF)
    mail.sent(got_part)
    part_send[0] = context_grad
    got_do = [
        mail.send(
            part_send.at[0, :, lanes_at(block * MINE, MINE)], do_recv.at[own], which
        )
        for block, which in ((cross, "cross"), (far, "far"), (pair, "pair"))
    ]
    do_recv[own] = part_send[0, :, lanes_at(own * MINE, MINE)]

    start = half_ff
    for piece in fc1_p:
        width = piece.columns

        def fc1_tile(i, carry, start=start, width=width, piece=piece):
            t = dot_tn(
                normed_two[:, lanes_at(i * 512, 512)],
                big[2 * ROWS : 4 * ROWS, start : start + width],
            )
            piece.source[pl.ds(i * 2, 2)] = t.astype(BF).reshape(2, 2, 4, 2, 16, width)
            return carry

        lax.fori_loop(0, 2, fc1_tile, 0)
        piece.first(0)
        start += width

    for copy in got_act:
        mail.sent(copy)
    load_e = load(12, e_in, big)

    got_att.wait_recv()
    got_cols.wait_recv()

    def proj_tile(i, carry):
        t = dot_tn(att[:, lanes_at(i * 512, 512)], branch_cols[...])
        t = t.astype(BF).reshape(2, 2, 4, 2, 16, 512)
        proj_p[0].source[pl.ds(i * 2, 2)] = t[..., 0:256]
        proj_p[1].source[pl.ds(i * 2, 2)] = t[..., 256:512]
        return carry

    lax.fori_loop(0, 2, proj_tile, 0)
    first(proj_p, 0)
    third(fc2_p, 0)

    mail.sent(got_att)
    mail.sent(got_cols)
    load_plain = [
        load(14, plain_in.at[block_rows(cross)], att.at[pl.ds(0, ROWS)]),
        load(16, plain_in.at[block_rows(pair)], part_send.at[1]),
    ]
    load_heads.append(load(4, kt_in, att.at[pl.ds(ROWS, ROWS)]))
    for copy in out_copies:
        copy.wait()
    q_wide, do_wide = proj_w.at[:, 0:MINE], proj_w.at[:, MINE : 2 * MINE]
    for copy in load_heads:
        copy.wait()
    load_e.wait()
    load_normed.wait()
    for copy in load_qkv:
        copy.wait()
    for n, block in enumerate((own, pair, far, cross)):
        if n > 0:
            got_do[3 - n].wait_recv()
        rows = block_rows(block)
        lane = lax.broadcasted_iota(jnp.int32, (ROWS, MINE), 1)
        grad_t = do_recv[block].astype(F32).T
        parts, rests = [], []
        for h in range(4):
            factor = inv[h, :, rows] * head_mask[0, own * 4 + h].astype(F32)
            part = (grad_t[h * HEAD : (h + 1) * HEAD] * factor).astype(BF)
            parts.append(part)
            rests.append(
                jnp.sum(
                    part.astype(F32) * ot[h * HEAD : (h + 1) * HEAD, rows].astype(F32),
                    axis=0,
                    keepdims=True,
                )
            )
        grad_low = jnp.concatenate(parts, axis=0)
        grad_rows = grad_low.astype(F32).T.astype(BF)
        queries = fc2_w[rows, 768:1024]
        zero = jnp.zeros((), BF)
        for h in range(4):
            keep = lane // HEAD == h
            q_wide[h * ROWS : (h + 1) * ROWS, :] = jnp.where(keep, queries, zero)
            do_wide[h * ROWS : (h + 1) * ROWS, :] = jnp.where(keep, grad_rows, zero)
        for h in range(4):
            below = lax.broadcasted_iota(jnp.int32, (MINE, ROWS), 0) // HEAD == h
            masked = jnp.where(below, grad_low, zero)
            prob_grad = dot(fc2_w[WIDTH : 2 * WIDTH, 768:1024], masked)
            powers = big[:, lanes_at((block * 4 + h) * ROWS, ROWS)].astype(F32)
            score_grad = (powers * (prob_grad - rests[h])).astype(BF)
            fc1_w[:, WIDTH + h * ROWS : WIDTH + (h + 1) * ROWS] = score_grad
            dq_t[h * HEAD : (h + 1) * HEAD, :] = dot(
                att[ROWS + h * HEAD : ROWS + (h + 1) * HEAD, :], score_grad
            )
        more_k = dot(fc1_w[:, WIDTH : 2 * WIDTH], q_wide[...])
        more_v = dot(big[:, lanes_at(block * 4 * ROWS, 4 * ROWS)], do_wide[...])
        if n == 0:
            dk[...] = more_k
            dv[...] = more_v
        else:
            dk[...] += more_k
            dv[...] += more_v
        row_of = pl.ds(pl.multiple_of(WIDTH + block * ROWS, ROWS), ROWS)
        fc2_w[row_of, 0:MINE] = (dq_t[...].T * 0.125).astype(BF)
        if n == 1:
            for copy in got_do:
                mail.sent(copy)
            load_plain.append(load(15, plain_in.at[block_rows(far)], part_send.at[0]))
            third(fc2_p, 1)
        elif n == 2:
            second(fc1_p, 0)
            second(proj_p, 0)
        elif n == 3:
            third(fc2_p, 2)
    low = slice(WIDTH, 2 * WIDTH)
    fc2_w[low, MINE : 2 * MINE] = dk[...].astype(BF)
    fc2_w[low, 2 * MINE : 3 * MINE] = dv[...].astype(BF)
    for j, row in ((0, 6), (2, 7)):
        total = jnp.sum(fc2_w[low, j * MINE : (j + 1) * MINE].astype(F32), axis=0, keepdims=True)
        vec[row : row + 1, lanes_at(own * MINE, MINE)] = total

    places = [big.at[:, pl.ds(j * WIDTH, WIDTH)] for j in range(4)]
    places += [proj_w, fc1_w.at[:, pl.ds(WIDTH, WIDTH)]]
    load_ada = [
        load(17 + j, ada_weight.at[:, pl.ds(j * WIDTH, WIDTH)], places[j]) for j in range(6)
    ]
    for copy in load_plain:
        copy.wait()

    def normed_back(block, plain):
        row_of = pl.ds(pl.multiple_of(WIDTH + block * ROWS, ROWS), ROWS)
        grad = dot_nt(fc2_w[row_of, 0:768], fc2_w[0:WIDTH, 0:768])
        vec[0:1, :] += jnp.sum(grad, axis=0, keepdims=True)
        vec[1:2, :] += jnp.sum(grad * plain.astype(F32), axis=0, keepdims=True)
        return grad

    mail.sent(got_normed)
    normed_two[0:ROWS, :] = normed_back(cross, att[0:ROWS, :]).astype(BF)
    got_cross = mail.send(normed_two.at[pl.ds(0, ROWS)], part_recv.at[0], "pair")
    far_part = normed_back(far, part_send[0])
    mail.sent(got_grad)
    mlp_grad[0:ROWS, :] = normed_back(pair, part_send[1]).astype(BF)
    got_pair = mail.send(mlp_grad.at[pl.ds(0, ROWS)], part_recv.at[1], "pair")
    own_part = normed_back(own, norm_parts(tokens[...].astype(F32))[0])
    for s in range(4):
        dv[s * ROWS : (s + 1) * ROWS, :] = own_part[:, s * MINE : (s + 1) * MINE]
    share[own] = vec[...]
    got_vec = [
        mail.send(share.at[own], share.at[own], which) for which in ("pair", "far", "cross")
    ]

    fc2_p[0].sent(0)

    def qkv_tile(i, carry):
        t = dot_tn(fc1_w[:, lanes_at(i * 512, 512)], fc2_w[WIDTH : 2 * WIDTH, 0:768])
        t = t.astype(BF).reshape(2, 2, 4, 2, 16, 768)
        qkv_p[0].source[pl.ds(i * 2, 2)] = t[..., 0:384]
        qkv_p[1].source[pl.ds(i * 2, 2)] = t[..., 384:768]
        return carry

    lax.fori_loop(0, 2, qkv_tile, 0)
    first(qkv_p, 0)
    got_cross.wait_recv()
    normed_two[ROWS : 2 * ROWS, :] = (far_part + part_recv[0].astype(F32)).astype(BF)
    got_far = mail.send(normed_two.at[pl.ds(ROWS, ROWS)], n_recv, "far")
    third(fc1_p, 0)
    third(proj_p, 0)
    for copy in got_vec:
        copy.wait_recv()
    total = (share[0] + share[1]) + (share[2] + share[3])
    value = condition[...].astype(F32)
    sigma = 1.0 / (1.0 + jnp.exp(-value))
    row = lax.broadcasted_iota(jnp.int32, (16, WIDTH), 0)
    low = jnp.where(row == 14, value * sigma, total).astype(BF)
    low_vec[...] = low
    x, y, z = spot[0], spot[1], spot[2]
    x_lo = x % 2
    ring_cols = lanes_at(core * 512, 512)
    everyone[z, x_lo, y, :, ring_cols] = low_vec[:, ring_cols]
    mine = everyone.at[z, x_lo, y, :, ring_cols]
    got_near = [
        mail.send_ring(mine, mine, axis, step)
        for axis, step in (("y", 1), ("y", -1), ("y", 2), ("l", 0), ("ly", 1), ("ly", -1), ("ly", 2))
    ]
    second(qkv_p, 0)
    for copy in load_ada:
        copy.wait()
    back_cond = jnp.zeros((1, WIDTH), F32)
    for j in range(6):
        back_cond = back_cond + dot_nt(low, places[j][...])[j : j + 1]
    cond_grad[...] = back_cond * (sigma * (1.0 + value * (1.0 - sigma)))
    third(fc1_p, 1)
    third(proj_p, 1)
    for copy in got_near:
        copy.wait_recv()
    mine = everyone.at[z, :, :, :, ring_cols]
    got_z = [mail.send_ring(mine, mine, "z", step) for step in (1, -1, 2)]
    got_near = [mail.send(mine, mine, "pair")]
    third(qkv_p, 0)
    third(fc1_p, 2)
    third(proj_p, 2)

    start = 0
    for piece in pieces[:FC_PIECES]:
        width = piece.columns // 2
        for half in range(2):
            fin[high, core, :, start : start + width] = piece.result(half)[...]
            start += width
    to_far = mail.send(fin.at[high, core], fin.at[high, core], "far")
    to_pair = mail.send(fin.at[high, core], fin.at[high, core], "pair")
    third(qkv_p, 1)
    for step, copy in zip((1, -1, 2), got_z, strict=True):
        copy.wait_recv()
        mine = everyone.at[(z + 4 - step) % 4, :, :, :, ring_cols]
        got_near.append(mail.send(mine, mine, "pair"))
    third(qkv_p, 2)
    for k, piece in enumerate(qkv_p):
        for half in range(2):
            fin_q[own, half, :, k * 384 : (k + 1) * 384] = piece.result(half)[...]
    got_q = [mail.send(fin_q.at[own], fin_q.at[own], which) for which in ("far", "cross", "pair")]
    to_far.wait_recv()
    to_pair_two = mail.send(fin.at[1 - high, core], fin.at[1 - high, core], "pair")
    got_pair.wait_recv()
    got_far.wait_recv()
    own_part = jnp.concatenate([dv[s * ROWS : (s + 1) * ROWS, :] for s in range(4)], axis=1)
    normed_grad = own_part + n_recv[...].astype(F32) + part_recv[1].astype(F32)
    normed_one, rate_one = norm_parts(tokens[...].astype(F32))
    result = middle[...] + norm_back(normed_one, rate_one, normed_grad * (1.0 + mods[1:2, :]))
    out_copies = stage(result, input_grad)
    for copy in got_near:
        copy.wait_recv()

    bucket = lax.axis_index("bucket")
    window = everyone[:, :, :, :, lanes_at((bucket // 4) * 128, 128)]
    turned = window.reshape(512, 128).astype(F32).T
    quarter = pl.multiple_of((bucket % 4) * 32, 32)
    dv[0:128, :] = turned[:, 0:256]
    dv[128:256, :] = turned[:, 256:512]
    silu = jnp.concatenate([dv[pl.ds(quarter, 32), :], dv[pl.ds(quarter + 128, 32), :]], axis=1)
    lane = lax.broadcasted_iota(jnp.int32, (32, 512), 1)
    silu = jnp.where(lane % 16 == 14, silu, 0.0)
    left = [pltpu.roll(silu, 512 + j - 14, 1) for j in range(6)]
    pick = lax.broadcasted_iota(jnp.int32, (16, 512), 0)
    lane = lax.broadcasted_iota(jnp.int32, (16, 512), 1)
    left.append(jnp.where(lane % 16 == pick, 1.0, 0.0))
    product = dot(jnp.concatenate(left, axis=0).astype(BF), everyone[...].reshape(512, WIDTH))
    ada_copies = []
    for j in range(6):
        middle[j * 32 : (j + 1) * 32, :] = product[j * 32 : (j + 1) * 32]
        ada_copies.append(
            pltpu.make_async_copy(
                middle.at[pl.ds(j * 32, 32)],
                ada_out.at[:, pl.ds(j * WIDTH, WIDTH)],
                out_sem.at[7 + j],
            )
        )
        ada_copies[j].start()
    sums_out[...] = product[192:208]
    for copy in [to_pair, to_pair_two] + got_q:
        copy.wait_recv()
    last_copies = [
        pltpu.make_async_copy(fin, fin_out, out_sem.at[5]),
        pltpu.make_async_copy(fin_q, fin_q_out, out_sem.at[6]),
    ]
    for copy in last_copies:
        copy.start()
    for copy in last_copies + out_copies + ada_copies:
        copy.wait()
    mail.finish()
    for piece in pieces:
        piece.finish()


def middle_call(*args):
    shape = jax.ShapeDtypeStruct
    row = 4 * ROWS
    piece_scratch = []
    for k in range(PIECES):
        for phase in range(3):
            dims = Piece.dims(ROUTE_OF[k], phase, COLUMNS_OF[k])
            slots = 4 if ROUTE_OF[k][phase] == "l" else 6
            piece_scratch.append(pltpu.VMEM((slots,) + dims, BF))
    for k in range(FC_PIECES):
        piece_scratch.append(pltpu.VMEM((4, 2, 4, 2, 16, COLUMNS_OF[k]), BF))
    scratch = [
        pltpu.VMEM((WIDTH, WIDTH), BF),
        pltpu.VMEM((WIDTH, 2 * WIDTH), BF),
        pltpu.VMEM((2 * WIDTH, WIDTH), BF),
        pltpu.VMEM((2 * ROWS, WIDTH), BF),
        pltpu.VMEM((2 * ROWS, WIDTH), BF),
        pltpu.VMEM((row, 4 * row), BF),
        pltpu.VMEM((2 * ROWS, WIDTH), BF),
        pltpu.VMEM((2 * ROWS, WIDTH // 2), BF),
        pltpu.VMEM((ROWS, WIDTH), F32),
        pltpu.VMEM((ROWS, WIDTH), BF),
        pltpu.VMEM((2, ROWS, WIDTH), BF),
        pltpu.VMEM((2, ROWS, WIDTH), BF),
        pltpu.VMEM((1, 2 * WIDTH), F32),
        pltpu.VMEM((MINE, row), BF),
        pltpu.VMEM((4, 1, row), F32),
        pltpu.VMEM((4, ROWS, MINE), BF),
        pltpu.VMEM((MINE, ROWS), F32),
        pltpu.VMEM((row, MINE), F32),
        pltpu.VMEM((row, MINE), F32),
        pltpu.VMEM((ROWS, WIDTH), BF),
        pltpu.VMEM((2, 2, 16, FC_COLUMNS), BF),
        pltpu.VMEM((4, 2, 16, 768), BF),
        pltpu.VMEM((16, WIDTH), F32),
        pltpu.VMEM((4, 16, WIDTH), F32),
        pltpu.VMEM((16, WIDTH), BF),
        pltpu.VMEM((4, 2, 4, 16, WIDTH), BF),
        pltpu.SemaphoreType.DMA((23,)),
        pltpu.SemaphoreType.DMA((13,)),
        pltpu.SemaphoreType.DMA((40,)),
        pltpu.SemaphoreType.DMA((40,)),
        pltpu.SemaphoreType.DMA((PIECES, 3, 6)),
        pltpu.SemaphoreType.DMA((PIECES, 3, 6)),
    ] + piece_scratch
    return pl.pallas_call(
        middle_kernel,
        out_shape=[
            shape((ROWS, WIDTH), F32),
            shape((ROWS, WIDTH), F32),
            shape((1, WIDTH), F32),
            shape((32, 6 * WIDTH), F32),
            shape((16, WIDTH), F32),
            shape((2, 2, 16, FC_COLUMNS), BF),
            shape((4, 2, 16, 768), BF),
        ],
        in_specs=[VMEM] * 4 + [SMEM] * 3 + [VMEM] * 4 + [ANY] * 14,
        out_specs=[ANY, ANY, VMEM, ANY, VMEM, ANY, ANY],
        scratch_shapes=scratch,
        compiler_params=pltpu.CompilerParams(
            collective_id=3, has_side_effects=True, vmem_limit_bytes=63 << 20
        ),
        name="middle",
    )(*args)


def finish_kernel(
    block_in,
    input_in,
    cond_in,
    ada_in,
    sums,
    fin,
    fin_q,
    block_out,
    input_out,
    cond_out,
    ada_out,
    ada_b_out,
    qkv_out,
    qv_out,
    proj_out,
    proj_b_out,
    fc1_out,
    fc1_b_out,
    fc2_out,
    fc2_b_out,
    block_mid,
    input_mid,
    ada_mid,
    sem,
):
    passing = (
        (block_in, block_mid, block_out),
        (input_in, input_mid, input_out),
        (ada_in, ada_mid, ada_out),
    )
    arriving = [
        pltpu.make_async_copy(src, mid, sem.at[k]) for k, (src, mid, _) in enumerate(passing)
    ]
    copies = [
        pltpu.make_async_copy(mid, dst, sem.at[3 + k]) for k, (_, mid, dst) in enumerate(passing)
    ]
    for copy in arriving:
        copy.start()
    cond_out[...] = cond_in[...]
    for h in range(2):
        rows = slice(h * 16, (h + 1) * 16)
        for c in range(2):
            start = 0
            for q, half in FC2_UNITS:
                row = h * 64 + q * 16
                col = c * 512 + half * 256
                fc2_out[row : row + 16, col : col + 256] = fin[h, c, :, start : start + 256].astype(
                    F32
                )
                start += 256
            fc1_out[rows, c * 2 * WIDTH : (c + 1) * 2 * WIDTH] = fin[
                h, c, :, start : start + 2 * WIDTH
            ].astype(F32)
            start += 2 * WIDTH
            proj_out[rows, c * 512 : (c + 1) * 512] = fin[h, c, :, start : start + 512].astype(F32)
        for s in range(4):
            for j in range(3):
                col = j * WIDTH + s * MINE
                qkv_out[rows, col : col + MINE] = fin_q[s, h, :, j * MINE : (j + 1) * MINE].astype(
                    F32
                )
    for here, there in zip(arriving, copies, strict=True):
        here.wait()
        there.start()
    bucket = lax.axis_index("bucket")
    for row, size, dst in (
        (0, 6 * WIDTH, ada_b_out),
        (6, 2 * WIDTH, qv_out),
        (8, WIDTH, proj_b_out),
        (9, 4 * WIDTH, fc1_b_out),
        (13, WIDTH, fc2_b_out),
    ):
        width = size // 32
        line = jnp.concatenate([sums[row + r : row + r + 1, :] for r in range(size // WIDTH)], 1)
        line = jnp.broadcast_to(line, (8, size))
        line = pltpu.roll(line, (size - bucket * width) % size, 1)
        dst[...] = line[0, 0:width]
    for copy in copies:
        copy.wait()


def finish_call(*args):
    shape = jax.ShapeDtypeStruct
    sizes = [
        (ROWS, WIDTH),
        (ROWS, WIDTH),
        (1, WIDTH),
        (32, 6 * WIDTH),
        (6 * WIDTH // 32,),
        (32, 3 * WIDTH),
        (2 * WIDTH // 32,),
        (32, WIDTH),
        (WIDTH // 32,),
        (32, 4 * WIDTH),
        (4 * WIDTH // 32,),
        (128, WIDTH),
        (WIDTH // 32,),
    ]
    spread = (0, 1, 3)
    return pl.pallas_call(
        finish_kernel,
        out_shape=[shape(size, F32) for size in sizes],
        in_specs=[ANY, ANY, VMEM, ANY] + [VMEM] * 3,
        out_specs=[ANY if k in spread else VMEM for k in range(len(sizes))],
        scratch_shapes=[
            pltpu.VMEM((ROWS, WIDTH), F32),
            pltpu.VMEM((ROWS, WIDTH), F32),
            pltpu.VMEM((32, 6 * WIDTH), F32),
            pltpu.SemaphoreType.DMA((6,)),
        ],
        compiler_params=pltpu.CompilerParams(vmem_limit_bytes=62 << 20),
        name="finish",
    )(*args)


def run_attend(tokens, condition, lengths, head_mask, ada_weight, ada_bias, qkv_weight, qv_bias):
    return attend(
        tokens[0],
        condition,
        lengths,
        head_mask,
        ada_weight,
        ada_bias,
        qkv_weight,
        qv_bias,
    )


def local(
    tokens,
    condition,
    lengths,
    head_mask,
    group_mask,
    token_mask,
    ada_weight,
    ada_bias,
    qkv_weight,
    qv_bias,
    proj_weight,
    proj_bias,
    fc1_weight,
    fc1_bias,
    fc2_weight,
    fc2_bias,
    out_grad,
):
    mods, attended, queries, values, kt, ot, inv, normed, plain, powers = run_attend(
        tokens, condition, lengths, head_mask, ada_weight, ada_bias, qkv_weight, qv_bias
    )
    block_out, input_grad, cond, ada, sums, fin, fin_q = middle_call(
        tokens[0],
        out_grad[0],
        condition,
        mods,
        lengths,
        head_mask,
        group_mask,
        token_mask,
        proj_bias,
        fc1_bias,
        fc2_bias,
        attended,
        proj_weight,
        fc1_weight,
        fc2_weight,
        qkv_weight,
        queries,
        values,
        kt,
        ot,
        inv,
        normed,
        plain,
        ada_weight,
        powers,
    )
    results = finish_call(block_out, input_grad, cond, ada, sums, fin, fin_q)
    return (results[0][None], results[1][None]) + tuple(results[2:])


def solution(mesh):
    return jax.shard_map(
        local,
        mesh=mesh,
        in_specs=(
            P("bucket", "seq", None),
            P("bucket", None),
            P("bucket", None),
            P("bucket", None),
            P("bucket", None),
            P("bucket", "seq"),
            P(),
            P(),
            P(),
            P(),
            P(),
            P(),
            P(),
            P(),
            P(),
            P(),
            P("bucket", "seq", None),
        ),
        out_specs=(
            P("bucket", "seq", None),
            P("bucket", "seq", None),
            P("bucket", None),
            P("bucket", None),
            P("bucket"),
            P("bucket", None),
            P("bucket"),
            P("bucket", None),
            P("bucket"),
            P("bucket", None),
            P("bucket"),
            P("bucket", None),
            P("bucket"),
        ),
        check_vma=False,
    )
```

```python
import functools

import jax
import jax.numpy as jnp
from jax import lax
from jax.experimental import pallas as pl
from jax.experimental.pallas import tpu as pltpu
from jax.sharding import PartitionSpec as P


MESH_IDS = pl.DeviceIdType.MESH
AXES = {"x": 0, "y": 1, "z": 2}


def place():
    bucket = lax.axis_index("bucket")
    seq = lax.axis_index("seq")
    return (
        (seq // 2) * 2 + (bucket // 4) % 2,
        bucket % 4,
        bucket // 8,
        seq % 2,
    )


def device(x, y, z, core):
    return (z * 8 + (x % 2) * 4 + y, (x // 2) * 2 + core)


def shifted(spot, axis, step):
    x, y, z, core = spot
    if axis == "x":
        x = (x + step) % 4
    elif axis == "y":
        y = (y + step) % 4
    elif axis == "z":
        z = (z + step) % 4
    elif axis == "l":
        x = (x // 2) * 2 + 1 - x % 2
    elif axis == "ly":
        x = (x // 2) * 2 + 1 - x % 2
        y = (y + step) % 4
    return device(x, y, z, core)


TORUS = [(axis, step) for axis in "xyz" for step in (1, -1)]


def add_into(target, others):
    total = target[...].astype(jnp.float32)
    for other in others:
        total = total + other[...].astype(jnp.float32)
    target[...] = total.astype(jnp.bfloat16)


class Piece:
    def __init__(self, source, columns, route, landing, send_sem, recv_sem, spot):
        self.source, self.columns, self.route = source, columns, route
        self.landing = landing
        self.send_sem, self.recv_sem, self.spot = send_sem, recv_sem, spot
        self.copies, self.done = {}, []

    @staticmethod
    def dims(route, phase, columns):
        done = route[: phase + 1]
        out = []
        if "z" not in done:
            out.append(4)
        if "x" not in done and "l" not in done:
            out.append(2)
        if "y" not in done:
            out.append(4)
        if "l" in route:
            return tuple(out) + (16, columns)
        if "x" not in done:
            out.append(2)
        return tuple(out) + (16, columns // 2)

    def block(self, phase, target, half):
        done, axis = self.route[:phase], self.route[phase]
        split = "l" in self.route
        index = []
        if "z" not in done:
            index.append(target if axis == "z" else slice(None))
        if "x" not in done and "l" not in done:
            index.append(
                target % 2 if axis == "x" else target if axis == "l" else slice(None)
            )
        if "y" not in done:
            index.append(target if axis == "y" else slice(None))
        if phase == 0:
            if split:
                return self.source.at[tuple(index) + (half,)]
            index.append(target // 2 if axis == "x" else slice(None))
            width = self.columns // 2
            lanes = pl.ds(half * width, width)
            return self.source.at[tuple(index) + (slice(None), lanes)]
        if not split and "x" not in done:
            index.append(target // 2 if axis == "x" else slice(None))
        return self.landing[phase - 1].at[(3 - half,) + tuple(index)]

    def here(self, phase):
        if self.route[phase] == "l":
            return self.spot[0] % 2
        return self.spot[AXES[self.route[phase]]]

    def send(self, phase, slot, ref, step):
        copy = pltpu.make_async_remote_copy(
            src_ref=ref,
            dst_ref=self.landing[phase].at[slot],
            send_sem=self.send_sem.at[phase, slot],
            recv_sem=self.recv_sem.at[phase, slot],
            device_id=shifted(self.spot, self.route[phase], step),
            device_id_type=MESH_IDS,
        )
        copy.start()
        self.copies[phase, slot] = copy

    def first(self, phase):
        a = self.here(phase)
        if self.route[phase] == "l":
            self.send(phase, 2, self.block(phase, 1 - a, 1), 1)
            self.send(phase, 3, self.block(phase, 1 - a, 0), 1)
            return
        if phase > 0:
            for step, slots in ((1, (0, 1)), (-1, (3, 2)), (2, (4, 5))):
                for half in range(2):
                    self.send(phase, slots[half], self.block(phase, (a + step) % 4, half), step)
            return
        self.send(phase, 0, self.block(phase, (a + 2) % 4, 0), 1)
        self.send(phase, 1, self.block(phase, (a + 2) % 4, 1), -1)
        self.send(phase, 2, self.block(phase, (a + 1) % 4, 1), 1)
        self.send(phase, 3, self.block(phase, (a + 3) % 4, 0), -1)

    def second(self, phase):
        if phase > 0:
            return
        a = self.here(phase)
        landing = self.landing[phase]
        for slot, step, half in ((0, 1, 0), (1, -1, 1)):
            self.copies[phase, slot].wait_recv()
            add_into(landing.at[slot], [self.block(phase, (a + step) % 4, half)])
            self.send(phase, slot + 4, landing.at[slot], step)

    def third(self, phase):
        a = self.here(phase)
        landing = self.landing[phase]
        for half, slot, others in ((0, 3, (4, 0)), (1, 2, (5, 1))):
            self.copies[phase, slot].wait_recv()
            terms = [self.block(phase, a, half)]
            if self.route[phase] == "l":
                others = ()
            elif phase == 0:
                others = others[:1]
            for other in others:
                self.copies[phase, other].wait_recv()
                terms.append(landing.at[other])
            add_into(landing.at[slot], terms)

    def result(self, half):
        return self.landing[-1].at[3 - half]

    def sent(self, phase):
        for slot in range(4):
            self.copies[phase, slot].wait_send()
            self.done.append((phase, slot))

    def finish(self):
        for key, copy in self.copies.items():
            if key not in self.done:
                copy.wait_send()


BF = jnp.bfloat16
F32 = jnp.float32
VMEM = pl.BlockSpec(memory_space=pltpu.VMEM)
SMEM = pl.BlockSpec(memory_space=pltpu.SMEM)
ANY = pl.BlockSpec(memory_space=pl.ANY)
NT = (((1,), (1,)), ((), ()))
TN = (((0,), (0,)), ((), ()))
WIDTH = 1024
ROWS = 256
HEAD = 64
MINE = 256


def dot(a, b):
    return jnp.dot(a, b, preferred_element_type=F32)


def dot_nt(a, b):
    return lax.dot_general(a, b, NT, preferred_element_type=F32)


def dot_tn(a, b):
    return lax.dot_general(a, b, TN, preferred_element_type=F32)


def down(op, values):
    while values.shape[0] > 8:
        size = values.shape[0] // 2
        values = op(values[:size], values[size:])
    return values


def lanes_at(start, size):
    return pl.ds(pl.multiple_of(start, 128), size)


def block_rows(index):
    return pl.ds(pl.multiple_of(index * ROWS, ROWS), ROWS)


def norm_parts(values):
    centred = values - jnp.mean(values, axis=-1, keepdims=True)
    rate = lax.rsqrt(jnp.mean(centred * centred, axis=-1, keepdims=True) + 1e-06)
    return centred * rate, rate


def norm_back(normed, rate, grad):
    inner = jnp.mean(grad * normed, axis=-1, keepdims=True)
    return (grad - jnp.mean(grad, axis=-1, keepdims=True) - normed * inner) * rate


def segment(positions, lengths):
    first = lengths[0, 0]
    both = lengths[0, 0] + lengths[0, 1]
    return (positions >= first).astype(jnp.int32) + (positions >= both).astype(jnp.int32)


def quad(spot):
    x, _, _, core = spot
    high = x // 2
    own = high * 2 + core
    pair = high * 2 + (1 - core)
    far = (1 - high) * 2 + core
    cross = (1 - high) * 2 + (1 - core)
    return own, pair, far, cross


def partner(spot, which):
    x, y, z, core = spot
    if which == "pair":
        return device(x, y, z, 1 - core)
    if which == "far":
        return device((x + 2) % 4, y, z, core)
    return device((x + 2) % 4, y, z, 1 - core)


def greet_all(spot, moves, partners):
    barrier = pltpu.get_barrier_semaphore()
    for axis, step in moves:
        pl.semaphore_signal(
            barrier, inc=1, device_id=shifted(spot, axis, step), device_id_type=MESH_IDS
        )
    for which in partners:
        pl.semaphore_signal(barrier, inc=1, device_id=partner(spot, which), device_id_type=MESH_IDS)
    pl.semaphore_wait(barrier, len(moves) + len(partners))


class Mail:
    def __init__(self, spot, send_sem, recv_sem):
        self.spot, self.send_sem, self.recv_sem = spot, send_sem, recv_sem
        self.copies, self.done = [], []

    def send(self, src, dst, which):
        return self.send_to(src, dst, partner(self.spot, which))

    def send_ring(self, src, dst, axis, step):
        return self.send_to(src, dst, shifted(self.spot, axis, step))

    def send_to(self, src, dst, target):
        k = len(self.copies)
        copy = pltpu.make_async_remote_copy(
            src_ref=src,
            dst_ref=dst,
            send_sem=self.send_sem.at[k],
            recv_sem=self.recv_sem.at[k],
            device_id=target,
            device_id_type=MESH_IDS,
        )
        copy.start()
        self.copies.append(copy)
        return copy

    def sent(self, copy):
        copy.wait_send()
        self.done.append(copy)

    def finish(self):
        for copy in self.copies:
            if not any(copy is other for other in self.done):
                copy.wait_send()


def attend_kernel(
    tokens,
    condition,
    lengths,
    head_mask,
    ada_weight,
    ada_bias,
    qkv_weight,
    qv_bias,
    mods,
    attended,
    q_out,
    v_out,
    kt_out,
    ot_out,
    inv_out,
    normed_hbm,
    plain_hbm,
    e_out,
    ada,
    weight,
    everyone,
    k_aug,
    vt,
    ctx_t,
    ctx_send,
    ctx_recv,
    e_all,
    s_buf,
    normed_out,
    plain_out,
    load_sem,
    out_sem,
    send_sem,
    recv_sem,
):
    spot = place()
    own, pair, far, cross = quad(spot)
    loads = []
    for j in range(6):
        loads.append(
            pltpu.make_async_copy(
                ada_weight.at[:, pl.ds(j * WIDTH, WIDTH)], ada.at[j], load_sem.at[j]
            )
        )
    for j in range(3):
        start = pl.multiple_of(j * WIDTH + own * MINE, MINE)
        loads.append(
            pltpu.make_async_copy(
                qkv_weight.at[:, pl.ds(start, MINE)],
                weight.at[:, pl.ds(j * MINE, MINE)],
                load_sem.at[6 + j],
            )
        )
    for copy in loads:
        copy.start()
    greet_all(spot, [], ("pair", "far", "cross"))
    mail = Mail(spot, send_sem, recv_sem)
    half = ROWS // 2
    to_far = [
        mail.send(
            tokens.at[pl.ds(i * half, half)], everyone.at[own, pl.ds(i * half, half)], "far"
        )
        for i in range(2)
    ]
    to_pair = mail.send(tokens, everyone.at[own], "pair")

    value = condition[...].astype(F32)
    silu_low = (value / (1.0 + jnp.exp(-value))).astype(BF)
    silu_rows = jnp.broadcast_to(silu_low, (16, WIDTH))
    for j in range(6):
        loads[j].wait()
        row = dot(silu_rows, ada[j])[0:1]
        mods[pl.ds(j, 1), :] = row + ada_bias[pl.ds(j * WIDTH, WIDTH)].astype(F32).reshape(1, WIDTH)
    for copy in loads[6:]:
        copy.wait()

    shift, scale = mods[0:1, :], 1.0 + mods[1:2, :]
    mine = pl.multiple_of(own * MINE, MINE)
    q_bias = qv_bias[pl.ds(mine, MINE)].astype(F32).reshape(1, MINE)
    v_bias = qv_bias[pl.ds(WIDTH + mine, MINE)].astype(F32).reshape(1, MINE)
    lane = lax.broadcasted_iota(jnp.int32, (ROWS, 128), 1)

    def project(block, rows):
        plain = norm_parts(rows[...].astype(F32))[0]
        normed = (plain * scale + shift).astype(BF)
        here = pl.ds(pl.multiple_of(block * ROWS, ROWS), ROWS)
        plain_out[here, :] = plain.astype(BF)
        normed_out[here, :] = normed
        projected = dot(normed, weight[...])
        q_out[here, :] = ((projected[:, :MINE] + q_bias).astype(BF) * 0.125).astype(BF)
        keys = projected[:, MINE : 2 * MINE].astype(BF)
        values = (projected[:, 2 * MINE :] + v_bias).astype(BF)
        spots = segment(block * ROWS + lax.broadcasted_iota(jnp.int32, (ROWS, 128), 0), lengths)
        marks = jnp.where(spots == lane, 1.0, 0.0).astype(BF)
        for p in range(2):
            k_aug[p, here, pl.ds(0, 128)] = keys[:, p * 128 : (p + 1) * 128]
            k_aug[p, here, pl.ds(128, 128)] = marks
        v_out[here, :] = values
        kt_out[:, here] = keys.T
        vt[:, here] = values.T

    project(own, tokens)
    to_pair.wait_recv()
    project(pair, everyone.at[pair])
    forwards = []
    for i in range(2):
        to_far[i].wait_recv()
        piece = everyone.at[far, pl.ds(i * half, half)]
        forwards.append(mail.send(piece, piece, "pair"))
    project(far, everyone.at[far])
    for copy in forwards:
        copy.wait_recv()
    project(cross, everyone.at[cross])

    lanes = lax.broadcasted_iota(jnp.int32, (ROWS, 256), 1)
    order = ((cross, "cross"), (far, "far"), (pair, "pair"), (own, None))
    out_copies, sends, tops, inverses = [], [], {}, {}
    for k, (src, dst) in enumerate(((normed_out, normed_hbm), (plain_out, plain_hbm))):
        copy = pltpu.make_async_copy(src, dst, out_sem.at[4 + k])
        copy.start()
        out_copies.append(copy)

    def score(i):
        n, h = i // 4, i % 4
        block, p = order[n][0], h // 2
        spots = segment(block * ROWS + lax.broadcasted_iota(jnp.int32, (ROWS, 128), 0), lengths)
        marks = jnp.where((spots != lane) & (lane < 3), -1e30, 0.0).astype(BF)
        queries = q_out[block_rows(block), p * 128 : (p + 1) * 128]
        both = jnp.concatenate([queries, marks], axis=1)
        keep = (lanes // HEAD == h % 2) | (lanes >= 128)
        scores = dot_nt(k_aug[p], jnp.where(keep, both, jnp.zeros_like(both)))
        s_buf[i % 2] = scores
        tops[i] = jnp.max(down(jnp.maximum, scores), axis=0, keepdims=True)

    def soften(i):
        n, h = i // 4, i % 4
        powers = jnp.exp(s_buf[i % 2] - tops[i])
        e_all[:, i * ROWS : (i + 1) * ROWS] = powers.astype(BF)
        inverses[i] = 1.0 / jnp.sum(down(jnp.add, powers), axis=0, keepdims=True)
        inv_out[h, :, block_rows(order[n][0])] = inverses[i]

    def apply(i):
        n, h = i // 4, i % 4
        block, which = order[n]
        part = slice(h * HEAD, (h + 1) * HEAD)
        out = dot(vt[part, :], e_all[:, i * ROWS : (i + 1) * ROWS]) * inverses[i]
        ot_out[part, block_rows(block)] = out.astype(BF)
        ctx_t[n % 2, part, :] = out * head_mask[0, own * 4 + h].astype(F32)
        if h < 3:
            return
        ctx = ctx_t[n % 2].T.astype(BF)
        if which is None:
            ctx_recv[own] = ctx
        else:
            ctx_send[n] = ctx
            sends.append(mail.send(ctx_send.at[n], ctx_recv.at[own], which))
        wide = pl.ds(pl.multiple_of(block * 4 * ROWS, ROWS), 4 * ROWS)
        copy = pltpu.make_async_copy(
            e_all.at[:, pl.ds(n * 4 * ROWS, 4 * ROWS)], e_out.at[:, wide], out_sem.at[n]
        )
        copy.start()
        out_copies.append(copy)

    score(0)
    for i in range(16):
        if i > 0:
            apply(i - 1)
        if i < 15:
            score(i + 1)
        soften(i)
    apply(15)
    for copy in sends:
        copy.wait_recv()
    for s in range(4):
        attended[:, pl.ds(s * MINE, MINE)] = ctx_recv[s]
    for copy in out_copies:
        copy.wait()
    mail.finish()


def attend(
    tokens, condition, lengths, head_mask, ada_weight, ada_bias, qkv_weight, qv_bias
):
    shape = jax.ShapeDtypeStruct
    row = 4 * ROWS
    return pl.pallas_call(
        attend_kernel,
        out_shape=[
            shape((8, WIDTH), F32),
            shape((ROWS, WIDTH), BF),
            shape((row, MINE), BF),
            shape((row, MINE), BF),
            shape((MINE, row), BF),
            shape((MINE, row), BF),
            shape((4, 1, row), F32),
            shape((row, WIDTH), BF),
            shape((row, WIDTH), BF),
            shape((row, 4 * row), BF),
        ],
        in_specs=[VMEM, VMEM, SMEM, SMEM, ANY, VMEM, ANY, VMEM],
        out_specs=[VMEM] * 7 + [ANY] * 3,
        scratch_shapes=[
            pltpu.VMEM((6, WIDTH, WIDTH), BF),
            pltpu.VMEM((WIDTH, 3 * MINE), BF),
            pltpu.VMEM((4, ROWS, WIDTH), BF),
            pltpu.VMEM((2, row, 256), BF),
            pltpu.VMEM((MINE, row), BF),
            pltpu.VMEM((2, MINE, ROWS), F32),
            pltpu.VMEM((3, ROWS, MINE), BF),
            pltpu.VMEM((4, ROWS, MINE), BF),
            pltpu.VMEM((row, 4 * row), BF),
            pltpu.VMEM((2, row, ROWS), F32),
            pltpu.VMEM((row, WIDTH), BF),
            pltpu.VMEM((row, WIDTH), BF),
            pltpu.SemaphoreType.DMA((9,)),
            pltpu.SemaphoreType.DMA((6,)),
            pltpu.SemaphoreType.DMA((8,)),
            pltpu.SemaphoreType.DMA((8,)),
        ],
        compiler_params=pltpu.CompilerParams(
            collective_id=2, has_side_effects=True, vmem_limit_bytes=60 << 20
        ),
        name="attend",
    )(tokens, condition, lengths, head_mask, ada_weight, ada_bias, qkv_weight, qv_bias)


ROUTE_OF = ("zyx", "yxz", "xzy", "zyx", "yxz", "xzy", "zyx", "yxz", "zyl", "yzl")
COLUMNS_OF = (768, 768, 512, 768, 768, 512, 256, 256, 384, 384)
PIECES = len(COLUMNS_OF)
FC_PIECES = PIECES - 2
FC_COLUMNS = sum(COLUMNS_OF[:FC_PIECES])
FC2_UNITS = ((0, 0), (0, 1), (1, 0), (1, 1), (2, 0), (2, 1), (3, 0), (3, 1))


def middle_kernel(
    tokens,
    out_grad,
    condition,
    mods,
    lengths,
    head_mask,
    group_mask,
    token_mask,
    proj_bias,
    fc1_bias,
    fc2_bias,
    attended,
    proj_weight,
    fc1_weight,
    fc2_weight,
    qkv_weight,
    q_in,
    v_in,
    kt_in,
    ot_in,
    inv_in,
    normed_in,
    plain_in,
    ada_weight,
    e_in,
    block_out,
    input_grad,
    cond_grad,
    ada_out,
    sums_out,
    fin_out,
    fin_q_out,
    proj_w,
    fc1_w,
    fc2_w,
    att,
    normed_two,
    big,
    mlp_grad,
    branch_cols,
    middle,
    branch,
    part_send,
    part_recv,
    channel,
    ot,
    inv,
    do_recv,
    dq_t,
    dk,
    dv,
    n_recv,
    fin,
    fin_q,
    vec,
    share,
    low_vec,
    everyone,
    load_sem,
    out_sem,
    mail_send,
    mail_recv,
    piece_send,
    piece_recv,
    *piece_refs,
):
    spot = place()
    core, high = spot[3], spot[0] // 2
    own, pair, far, cross = quad(spot)
    half_ff = 2 * WIDTH

    def load(k, src, dst):
        copy = pltpu.make_async_copy(src, dst, load_sem.at[k])
        copy.start()
        return copy

    here, there = block_rows(core), block_rows(1 - core)
    load_att = load(0, attended, att.at[here])
    load_proj = load(1, proj_weight, proj_w)
    load_fc1 = load(2, fc1_weight.at[:, lanes_at(core * half_ff, half_ff)], fc1_w)
    load_fc2 = load(
        3, fc2_weight.at[pl.ds(pl.multiple_of(core * half_ff, 256), half_ff), :], fc2_w
    )
    load_heads = [load(5, ot_in, ot), load(6, inv_in, inv)]
    greet_all(spot, TORUS + [("y", 2), ("z", 2), ("ly", 1), ("ly", -1), ("ly", 2)], ("pair", "far", "cross"))
    mail = Mail(spot, mail_send, mail_recv)
    pieces = []
    for k in range(PIECES):
        refs = piece_refs[3 * k : 3 * k + 3]
        if k < FC_PIECES:
            source = piece_refs[3 * PIECES + k]
        else:
            source = pieces[0].source.at[..., pl.ds((k - FC_PIECES) * 384, 384)]
        pieces.append(
            Piece(
                source,
                COLUMNS_OF[k],
                ROUTE_OF[k],
                refs,
                piece_send.at[k],
                piece_recv.at[k],
                spot,
            )
        )
    fc2_p, fc1_p, proj_p, qkv_p = pieces[0:3], pieces[3:6], pieces[6:8], pieces[8:10]

    def first(group, phase):
        for piece in group:
            piece.first(phase)

    def second(group, phase):
        for piece in group:
            piece.second(phase)

    def third(group, phase):
        for piece in group:
            piece.third(phase)
            if phase < 2:
                piece.first(phase + 1)

    shift_two, scale_two = mods[3:4, :], 1.0 + mods[4:5, :]
    gate_one, gate_two = mods[2:3, :], mods[5:6, :]
    position = own * ROWS + lax.broadcasted_iota(jnp.int32, (ROWS, 1), 0)
    valid = (position < lengths[0, 0] + lengths[0, 1]).astype(F32)
    kept = valid * jnp.broadcast_to(token_mask[...].astype(F32), (8, ROWS)).T[:, 0:1]
    for g in range(8):
        channel[:, pl.ds(g * 256, 256)] = jnp.full(
            (1, 256), group_mask[0, core * 8 + g].astype(F32), F32
        )
    vec[...] = jnp.zeros_like(vec)

    upstream = out_grad[...].astype(F32)
    low_grad = (kept * gate_two * upstream).astype(BF)
    mlp_grad[here, :] = low_grad
    vec[13:14, :] = jnp.sum(low_grad.astype(F32), axis=0, keepdims=True)
    got_grad = mail.send(mlp_grad.at[here], mlp_grad.at[here], "pair")
    load_att.wait()
    got_att = mail.send(att.at[here], att.at[here], "pair")
    load_proj.wait()
    fresh = dot(att[here, :], proj_w[...]) + proj_bias[...].astype(F32).reshape(1, WIDTH)
    branch[...] = fresh.astype(BF)
    mid = tokens[...].astype(F32) + valid * gate_one * fresh
    middle[...] = mid
    normed_two[here, :] = (norm_parts(mid)[0] * scale_two + shift_two).astype(BF)
    got_normed = mail.send(normed_two.at[here], normed_two.at[here], "pair")
    load_fc1.wait()
    mine = lanes_at(core * half_ff, half_ff)
    TILE = 512

    def hidden(rows):
        def body(i, carry):
            cols = lanes_at(i * TILE, TILE)
            wide = lanes_at(core * half_ff + i * TILE, TILE)
            u = dot(normed_two[rows, :], fc1_w[:, cols]) + fc1_bias[wide].astype(F32).reshape(1, TILE)
            square = u * u
            t = jnp.tanh(0.7978845608028654 * u * (1.0 + 0.044715 * square))
            up = 0.5 * (1.0 + t)
            mask = channel[:, cols]
            big[rows, wide] = (u * up * mask).astype(BF)
            slope = up + 0.5 * u * (1.0 - t * t) * (
                0.7978845608028654 + (3 * 0.7978845608028654 * 0.044715) * square
            )
            low = pl.ds(pl.multiple_of(2 * ROWS + rows.start, ROWS), ROWS)
            big[low, cols] = (slope * mask).astype(BF)
            return carry

        lax.fori_loop(0, half_ff // TILE, body, 0, unroll=True)

    hidden(here)
    got_act = [mail.send(big.at[here, mine], big.at[here, mine], "pair")]
    got_normed.wait_recv()
    hidden(there)
    got_act.append(mail.send(big.at[there, mine], big.at[there, mine], "pair"))
    load_fc2.wait()
    part_send[0] = dot(big[there, mine], fc2_w[...]).astype(BF)
    got_part = mail.send(part_send.at[0], part_recv.at[0], "pair")
    mlp_out = dot(big[here, mine], fc2_w[...]) + fc2_bias[...].astype(F32).reshape(1, WIDTH)
    got_part.wait_recv()
    mlp_out = mlp_out + part_recv[0].astype(F32)

    def stage(result, target):
        copies = []
        for s in range(4):
            cols = pl.ds(s * MINE, MINE)
            dk[s * ROWS : (s + 1) * ROWS, :] = result[:, s * MINE : (s + 1) * MINE]
            copies.append(
                pltpu.make_async_copy(
                    dk.at[pl.ds(s * ROWS, ROWS)], target.at[:, cols], out_sem.at[s]
                )
            )
            copies[s].start()
        return copies

    out_copies = stage(middle[...] + kept * gate_two * mlp_out, block_out)
    vec[5:6, :] = jnp.sum(kept * mlp_out * upstream, axis=0, keepdims=True)

    got_grad.wait_recv()
    for copy in got_act:
        copy.wait_recv()
    half_cols = lanes_at(core * 512, 512)

    def fc2_tile(i, carry):
        t = dot_tn(big[0 : 2 * ROWS, lanes_at(i * 512, 512)], mlp_grad[:, half_cols])
        t = t.astype(BF).reshape(4, 2, 4, 16, 512)
        z, x_lo = i // 2, i % 2
        fc2_p[0].source[z, x_lo, :, :, :, 0:512] = t[:, :, 0]
        fc2_p[0].source[z, x_lo, :, :, :, 512:768] = t[:, :, 1, :, 0:256]
        fc2_p[1].source[z, x_lo, :, :, :, 0:256] = t[:, :, 1, :, 256:512]
        fc2_p[1].source[z, x_lo, :, :, :, 256:768] = t[:, :, 2]
        fc2_p[2].source[z, x_lo] = t[:, :, 3]
        return carry

    lax.fori_loop(0, 8, fc2_tile, 0)
    first(fc2_p, 0)

    def hidden_grad(i, carry):
        cols = lanes_at(i * TILE, TILE)
        low = pl.ds(pl.multiple_of(i * TILE, TILE), TILE)
        grad = dot_nt(mlp_grad[...], fc2_w[low, :])
        grad = (grad * big[2 * ROWS : 4 * ROWS, cols].astype(F32)).astype(BF)
        big[2 * ROWS : 4 * ROWS, lanes_at(half_ff + i * TILE, TILE)] = grad
        total = jnp.sum(grad.astype(F32), axis=0, keepdims=True)
        row = 9 + 2 * core + i // 2
        vec[pl.ds(row, 1), lanes_at((i % 2) * TILE, TILE)] = total
        return carry

    lax.fori_loop(0, half_ff // TILE, hidden_grad, 0, unroll=True)
    low_rows, low_cols = pl.ds(2 * ROWS, 2 * ROWS), pl.ds(half_ff, half_ff)
    load_qkv = [
        load(
            7 + j,
            qkv_weight.at[:, lanes_at(j * WIDTH + own * MINE, MINE)],
            fc2_w.at[pl.ds(0, WIDTH), pl.ds(j * MINE, MINE)],
        )
        for j in range(3)
    ]
    load_heads.append(load(10, q_in, fc2_w.at[pl.ds(0, WIDTH), pl.ds(768, 256)]))
    load_heads.append(load(11, v_in, fc2_w.at[pl.ds(WIDTH, WIDTH), pl.ds(768, 256)]))

    def back(rows):
        low = pl.ds(pl.multiple_of(2 * ROWS + rows.start, ROWS), ROWS)
        return dot_nt(big[low, low_cols], fc1_w[...])

    part_send[1] = back(there).astype(BF)
    got_back = mail.send(part_send.at[1], part_recv.at[1], "pair")
    normed_two_grad = back(here)
    second(fc2_p, 0)
    load_normed = load(13, normed_in, fc1_w.at[:, pl.ds(0, WIDTH)])
    got_back.wait_recv()
    normed_two_grad = normed_two_grad + part_recv[1].astype(F32)
    normed_mid, rate = norm_parts(middle[...])
    vec[3:4, :] = jnp.sum(normed_two_grad, axis=0, keepdims=True)
    vec[4:5, :] = jnp.sum(normed_two_grad * normed_mid, axis=0, keepdims=True)
    mid_grad = upstream + norm_back(normed_mid, rate, normed_two_grad * scale_two)
    middle[...] = mid_grad
    vec[2:3, :] = jnp.sum(valid * branch[...].astype(F32) * mid_grad, axis=0, keepdims=True)
    branch_grad = (valid * gate_one * mid_grad).astype(BF)
    vec[8:9, :] = jnp.sum(branch_grad.astype(F32), axis=0, keepdims=True)
    mail.sent(got_back)
    part_send[1] = branch_grad
    branch_cols[here, :] = part_send[1, :, half_cols]
    other_cols = lanes_at((1 - core) * 512, 512)
    got_cols = mail.send(part_send.at[1, :, other_cols], branch_cols.at[here], "pair")
    context_grad = dot_nt(branch_grad, proj_w[...]).astype(BF)
    mail.sent(got_part)
    part_send[0] = context_grad
    got_do = [
        mail.send(
            part_send.at[0, :, lanes_at(block * MINE, MINE)], do_recv.at[own], which
        )
        for block, which in ((cross, "cross"), (far, "far"), (pair, "pair"))
    ]
    do_recv[own] = part_send[0, :, lanes_at(own * MINE, MINE)]

    start = half_ff
    for piece in fc1_p:
        width = piece.columns

        def fc1_tile(i, carry, start=start, width=width, piece=piece):
            t = dot_tn(
                normed_two[:, lanes_at(i * 512, 512)],
                big[2 * ROWS : 4 * ROWS, start : start + width],
            )
            piece.source[pl.ds(i * 2, 2)] = t.astype(BF).reshape(2, 2, 4, 2, 16, width)
            return carry

        lax.fori_loop(0, 2, fc1_tile, 0)
        piece.first(0)
        start += width

    for copy in got_act:
        mail.sent(copy)
    load_e = load(12, e_in, big)

    got_att.wait_recv()
    got_cols.wait_recv()

    def proj_tile(i, carry):
        t = dot_tn(att[:, lanes_at(i * 512, 512)], branch_cols[...])
        t = t.astype(BF).reshape(2, 2, 4, 2, 16, 512)
        proj_p[0].source[pl.ds(i * 2, 2)] = t[..., 0:256]
        proj_p[1].source[pl.ds(i * 2, 2)] = t[..., 256:512]
        return carry

    lax.fori_loop(0, 2, proj_tile, 0)
    first(proj_p, 0)
    third(fc2_p, 0)

    mail.sent(got_att)
    mail.sent(got_cols)
    load_plain = [
        load(14, plain_in.at[block_rows(cross)], att.at[pl.ds(0, ROWS)]),
        load(16, plain_in.at[block_rows(pair)], part_send.at[1]),
    ]
    load_heads.append(load(4, kt_in, att.at[pl.ds(ROWS, ROWS)]))
    for copy in out_copies:
        copy.wait()
    q_wide, do_wide = proj_w.at[:, 0:MINE], proj_w.at[:, MINE : 2 * MINE]
    for copy in load_heads:
        copy.wait()
    load_e.wait()
    load_normed.wait()
    for copy in load_qkv:
        copy.wait()
    for n, block in enumerate((own, pair, far, cross)):
        if n > 0:
            got_do[3 - n].wait_recv()
        rows = block_rows(block)
        lane = lax.broadcasted_iota(jnp.int32, (ROWS, MINE), 1)
        grad_t = do_recv[block].astype(F32).T
        parts, rests = [], []
        for h in range(4):
            factor = inv[h, :, rows] * head_mask[0, own * 4 + h].astype(F32)
            part = (grad_t[h * HEAD : (h + 1) * HEAD] * factor).astype(BF)
            parts.append(part)
            rests.append(
                jnp.sum(
                    part.astype(F32) * ot[h * HEAD : (h + 1) * HEAD, rows].astype(F32),
                    axis=0,
                    keepdims=True,
                )
            )
        grad_low = jnp.concatenate(parts, axis=0)
        grad_rows = grad_low.astype(F32).T.astype(BF)
        queries = fc2_w[rows, 768:1024]
        zero = jnp.zeros((), BF)
        for h in range(4):
            keep = lane // HEAD == h
            q_wide[h * ROWS : (h + 1) * ROWS, :] = jnp.where(keep, queries, zero)
            do_wide[h * ROWS : (h + 1) * ROWS, :] = jnp.where(keep, grad_rows, zero)
        for h in range(4):
            below = lax.broadcasted_iota(jnp.int32, (MINE, ROWS), 0) // HEAD == h
            masked = jnp.where(below, grad_low, zero)
            prob_grad = dot(fc2_w[WIDTH : 2 * WIDTH, 768:1024], masked)
            powers = big[:, lanes_at((block * 4 + h) * ROWS, ROWS)].astype(F32)
            score_grad = (powers * (prob_grad - rests[h])).astype(BF)
            fc1_w[:, WIDTH + h * ROWS : WIDTH + (h + 1) * ROWS] = score_grad
            dq_t[h * HEAD : (h + 1) * HEAD, :] = dot(
                att[ROWS + h * HEAD : ROWS + (h + 1) * HEAD, :], score_grad
            )
        more_k = dot(fc1_w[:, WIDTH : 2 * WIDTH], q_wide[...])
        more_v = dot(big[:, lanes_at(block * 4 * ROWS, 4 * ROWS)], do_wide[...])
        if n == 0:
            dk[...] = more_k
            dv[...] = more_v
        else:
            dk[...] += more_k
            dv[...] += more_v
        row_of = pl.ds(pl.multiple_of(WIDTH + block * ROWS, ROWS), ROWS)
        fc2_w[row_of, 0:MINE] = (dq_t[...].T * 0.125).astype(BF)
        if n == 1:
            for copy in got_do:
                mail.sent(copy)
            load_plain.append(load(15, plain_in.at[block_rows(far)], part_send.at[0]))
        elif n == 2:
            second(fc1_p, 0)
            second(proj_p, 0)
    low = slice(WIDTH, 2 * WIDTH)
    fc2_w[low, MINE : 2 * MINE] = dk[...].astype(BF)
    fc2_w[low, 2 * MINE : 3 * MINE] = dv[...].astype(BF)
    for j, row in ((0, 6), (2, 7)):
        total = jnp.sum(fc2_w[low, j * MINE : (j + 1) * MINE].astype(F32), axis=0, keepdims=True)
        vec[row : row + 1, lanes_at(own * MINE, MINE)] = total

    places = [big.at[:, pl.ds(j * WIDTH, WIDTH)] for j in range(4)]
    places += [proj_w, fc1_w.at[:, pl.ds(WIDTH, WIDTH)]]
    load_ada = [
        load(17 + j, ada_weight.at[:, pl.ds(j * WIDTH, WIDTH)], places[j]) for j in range(6)
    ]
    for copy in load_plain:
        copy.wait()

    def normed_back(block, plain):
        row_of = pl.ds(pl.multiple_of(WIDTH + block * ROWS, ROWS), ROWS)
        grad = dot_nt(fc2_w[row_of, 0:768], fc2_w[0:WIDTH, 0:768])
        vec[0:1, :] += jnp.sum(grad, axis=0, keepdims=True)
        vec[1:2, :] += jnp.sum(grad * plain.astype(F32), axis=0, keepdims=True)
        return grad

    mail.sent(got_normed)
    normed_two[0:ROWS, :] = normed_back(cross, att[0:ROWS, :]).astype(BF)
    got_cross = mail.send(normed_two.at[pl.ds(0, ROWS)], part_recv.at[0], "pair")
    far_part = normed_back(far, part_send[0])
    mail.sent(got_grad)
    mlp_grad[0:ROWS, :] = normed_back(pair, part_send[1]).astype(BF)
    got_pair = mail.send(mlp_grad.at[pl.ds(0, ROWS)], part_recv.at[1], "pair")
    own_part = normed_back(own, norm_parts(tokens[...].astype(F32))[0])
    for s in range(4):
        dv[s * ROWS : (s + 1) * ROWS, :] = own_part[:, s * MINE : (s + 1) * MINE]
    share[own] = vec[...]
    got_vec = [
        mail.send(share.at[own], share.at[own], which) for which in ("pair", "far", "cross")
    ]

    fc2_p[0].sent(0)

    def qkv_tile(i, carry):
        t = dot_tn(fc1_w[:, lanes_at(i * 512, 512)], fc2_w[WIDTH : 2 * WIDTH, 0:768])
        t = t.astype(BF).reshape(2, 2, 4, 2, 16, 768)
        qkv_p[0].source[pl.ds(i * 2, 2)] = t[..., 0:384]
        qkv_p[1].source[pl.ds(i * 2, 2)] = t[..., 384:768]
        return carry

    lax.fori_loop(0, 2, qkv_tile, 0)
    first(qkv_p, 0)
    got_cross.wait_recv()
    normed_two[ROWS : 2 * ROWS, :] = (far_part + part_recv[0].astype(F32)).astype(BF)
    got_far = mail.send(normed_two.at[pl.ds(ROWS, ROWS)], n_recv, "far")
    for copy in got_vec:
        copy.wait_recv()
    total = (share[0] + share[1]) + (share[2] + share[3])
    value = condition[...].astype(F32)
    sigma = 1.0 / (1.0 + jnp.exp(-value))
    row = lax.broadcasted_iota(jnp.int32, (16, WIDTH), 0)
    low = jnp.where(row == 14, value * sigma, total).astype(BF)
    low_vec[...] = low
    x, y, z = spot[0], spot[1], spot[2]
    x_lo = x % 2
    ring_cols = lanes_at(core * 512, 512)
    everyone[z, x_lo, y, :, ring_cols] = low_vec[:, ring_cols]
    mine = everyone.at[z, x_lo, y, :, ring_cols]
    got_near = [
        mail.send_ring(mine, mine, axis, step)
        for axis, step in (("y", 1), ("y", -1), ("y", 2), ("l", 0), ("ly", 1), ("ly", -1), ("ly", 2))
    ]
    third(fc2_p, 1)
    second(qkv_p, 0)
    third(proj_p, 0)
    third(fc1_p, 0)
    for copy in load_ada:
        copy.wait()
    back_cond = jnp.zeros((1, WIDTH), F32)
    for j in range(6):
        back_cond = back_cond + dot_nt(low, places[j][...])[j : j + 1]
    cond_grad[...] = back_cond * (sigma * (1.0 + value * (1.0 - sigma)))
    for copy in got_near:
        copy.wait_recv()
    mine = everyone.at[z, :, :, :, ring_cols]
    got_z = [mail.send_ring(mine, mine, "z", step) for step in (1, -1, 2)]
    got_near = [mail.send(mine, mine, "pair")]
    third(qkv_p, 0)
    third(fc2_p, 2)
    third(proj_p, 1)
    third(fc1_p, 1)

    third(qkv_p, 1)
    third(proj_p, 2)
    third(fc1_p, 2)

    start = 0
    for piece in pieces[:FC_PIECES]:
        width = piece.columns // 2
        for half in range(2):
            fin[high, core, :, start : start + width] = piece.result(half)[...]
            start += width
    to_far = mail.send(fin.at[high, core], fin.at[high, core], "far")
    to_pair = mail.send(fin.at[high, core], fin.at[high, core], "pair")
    for step, copy in zip((1, -1, 2), got_z, strict=True):
        copy.wait_recv()
        mine = everyone.at[(z + 4 - step) % 4, :, :, :, ring_cols]
        got_near.append(mail.send(mine, mine, "pair"))
    third(qkv_p, 2)
    for k, piece in enumerate(qkv_p):
        for half in range(2):
            fin_q[own, half, :, k * 384 : (k + 1) * 384] = piece.result(half)[...]
    got_q = [mail.send(fin_q.at[own], fin_q.at[own], which) for which in ("far", "cross", "pair")]
    to_far.wait_recv()
    to_pair_two = mail.send(fin.at[1 - high, core], fin.at[1 - high, core], "pair")
    got_pair.wait_recv()
    got_far.wait_recv()
    own_part = jnp.concatenate([dv[s * ROWS : (s + 1) * ROWS, :] for s in range(4)], axis=1)
    normed_grad = own_part + n_recv[...].astype(F32) + part_recv[1].astype(F32)
    normed_one, rate_one = norm_parts(tokens[...].astype(F32))
    result = middle[...] + norm_back(normed_one, rate_one, normed_grad * (1.0 + mods[1:2, :]))
    out_copies = stage(result, input_grad)
    for copy in got_near:
        copy.wait_recv()

    bucket = lax.axis_index("bucket")
    window = everyone[:, :, :, :, lanes_at((bucket // 4) * 128, 128)]
    turned = window.reshape(512, 128).astype(F32).T
    quarter = pl.multiple_of((bucket % 4) * 32, 32)
    dv[0:128, :] = turned[:, 0:256]
    dv[128:256, :] = turned[:, 256:512]
    silu = jnp.concatenate([dv[pl.ds(quarter, 32), :], dv[pl.ds(quarter + 128, 32), :]], axis=1)
    lane = lax.broadcasted_iota(jnp.int32, (32, 512), 1)
    silu = jnp.where(lane % 16 == 14, silu, 0.0)
    left = [pltpu.roll(silu, 512 + j - 14, 1) for j in range(6)]
    pick = lax.broadcasted_iota(jnp.int32, (16, 512), 0)
    lane = lax.broadcasted_iota(jnp.int32, (16, 512), 1)
    left.append(jnp.where(lane % 16 == pick, 1.0, 0.0))
    product = dot(jnp.concatenate(left, axis=0).astype(BF), everyone[...].reshape(512, WIDTH))
    ada_copies = []
    for j in range(6):
        middle[j * 32 : (j + 1) * 32, :] = product[j * 32 : (j + 1) * 32]
        ada_copies.append(
            pltpu.make_async_copy(
                middle.at[pl.ds(j * 32, 32)],
                ada_out.at[:, pl.ds(j * WIDTH, WIDTH)],
                out_sem.at[7 + j],
            )
        )
        ada_copies[j].start()
    sums_out[...] = product[192:208]
    for copy in [to_pair, to_pair_two] + got_q:
        copy.wait_recv()
    last_copies = [
        pltpu.make_async_copy(fin, fin_out, out_sem.at[5]),
        pltpu.make_async_copy(fin_q, fin_q_out, out_sem.at[6]),
    ]
    for copy in last_copies:
        copy.start()
    for copy in last_copies + out_copies + ada_copies:
        copy.wait()
    mail.finish()
    for piece in pieces:
        piece.finish()


def middle_call(*args):
    shape = jax.ShapeDtypeStruct
    row = 4 * ROWS
    piece_scratch = []
    for k in range(PIECES):
        for phase in range(3):
            dims = Piece.dims(ROUTE_OF[k], phase, COLUMNS_OF[k])
            slots = 4 if ROUTE_OF[k][phase] == "l" else 6
            piece_scratch.append(pltpu.VMEM((slots,) + dims, BF))
    for k in range(FC_PIECES):
        piece_scratch.append(pltpu.VMEM((4, 2, 4, 2, 16, COLUMNS_OF[k]), BF))
    scratch = [
        pltpu.VMEM((WIDTH, WIDTH), BF),
        pltpu.VMEM((WIDTH, 2 * WIDTH), BF),
        pltpu.VMEM((2 * WIDTH, WIDTH), BF),
        pltpu.VMEM((2 * ROWS, WIDTH), BF),
        pltpu.VMEM((2 * ROWS, WIDTH), BF),
        pltpu.VMEM((row, 4 * row), BF),
        pltpu.VMEM((2 * ROWS, WIDTH), BF),
        pltpu.VMEM((2 * ROWS, WIDTH // 2), BF),
        pltpu.VMEM((ROWS, WIDTH), F32),
        pltpu.VMEM((ROWS, WIDTH), BF),
        pltpu.VMEM((2, ROWS, WIDTH), BF),
        pltpu.VMEM((2, ROWS, WIDTH), BF),
        pltpu.VMEM((1, 2 * WIDTH), F32),
        pltpu.VMEM((MINE, row), BF),
        pltpu.VMEM((4, 1, row), F32),
        pltpu.VMEM((4, ROWS, MINE), BF),
        pltpu.VMEM((MINE, ROWS), F32),
        pltpu.VMEM((row, MINE), F32),
        pltpu.VMEM((row, MINE), F32),
        pltpu.VMEM((ROWS, WIDTH), BF),
        pltpu.VMEM((2, 2, 16, FC_COLUMNS), BF),
        pltpu.VMEM((4, 2, 16, 768), BF),
        pltpu.VMEM((16, WIDTH), F32),
        pltpu.VMEM((4, 16, WIDTH), F32),
        pltpu.VMEM((16, WIDTH), BF),
        pltpu.VMEM((4, 2, 4, 16, WIDTH), BF),
        pltpu.SemaphoreType.DMA((23,)),
        pltpu.SemaphoreType.DMA((13,)),
        pltpu.SemaphoreType.DMA((40,)),
        pltpu.SemaphoreType.DMA((40,)),
        pltpu.SemaphoreType.DMA((PIECES, 3, 6)),
        pltpu.SemaphoreType.DMA((PIECES, 3, 6)),
    ] + piece_scratch
    return pl.pallas_call(
        middle_kernel,
        out_shape=[
            shape((ROWS, WIDTH), F32),
            shape((ROWS, WIDTH), F32),
            shape((1, WIDTH), F32),
            shape((32, 6 * WIDTH), F32),
            shape((16, WIDTH), F32),
            shape((2, 2, 16, FC_COLUMNS), BF),
            shape((4, 2, 16, 768), BF),
        ],
        in_specs=[VMEM] * 4 + [SMEM] * 3 + [VMEM] * 4 + [ANY] * 14,
        out_specs=[ANY, ANY, VMEM, ANY, VMEM, ANY, ANY],
        scratch_shapes=scratch,
        compiler_params=pltpu.CompilerParams(
            collective_id=3, has_side_effects=True, vmem_limit_bytes=63 << 20
        ),
        name="middle",
    )(*args)


def finish_kernel(
    block_in,
    input_in,
    cond_in,
    ada_in,
    sums,
    fin,
    fin_q,
    block_out,
    input_out,
    cond_out,
    ada_out,
    ada_b_out,
    qkv_out,
    qv_out,
    proj_out,
    proj_b_out,
    fc1_out,
    fc1_b_out,
    fc2_out,
    fc2_b_out,
    block_mid,
    input_mid,
    ada_mid,
    sem,
):
    passing = (
        (block_in, block_mid, block_out),
        (input_in, input_mid, input_out),
        (ada_in, ada_mid, ada_out),
    )
    arriving = [
        pltpu.make_async_copy(src, mid, sem.at[k]) for k, (src, mid, _) in enumerate(passing)
    ]
    copies = [
        pltpu.make_async_copy(mid, dst, sem.at[3 + k]) for k, (_, mid, dst) in enumerate(passing)
    ]
    for copy in arriving:
        copy.start()
    cond_out[...] = cond_in[...]
    for h in range(2):
        rows = slice(h * 16, (h + 1) * 16)
        for c in range(2):
            start = 0
            for q, half in FC2_UNITS:
                row = h * 64 + q * 16
                col = c * 512 + half * 256
                fc2_out[row : row + 16, col : col + 256] = fin[h, c, :, start : start + 256].astype(
                    F32
                )
                start += 256
            fc1_out[rows, c * 2 * WIDTH : (c + 1) * 2 * WIDTH] = fin[
                h, c, :, start : start + 2 * WIDTH
            ].astype(F32)
            start += 2 * WIDTH
            proj_out[rows, c * 512 : (c + 1) * 512] = fin[h, c, :, start : start + 512].astype(F32)
        for s in range(4):
            for j in range(3):
                col = j * WIDTH + s * MINE
                qkv_out[rows, col : col + MINE] = fin_q[s, h, :, j * MINE : (j + 1) * MINE].astype(
                    F32
                )
    for here, there in zip(arriving, copies, strict=True):
        here.wait()
        there.start()
    bucket = lax.axis_index("bucket")
    for row, size, dst in (
        (0, 6 * WIDTH, ada_b_out),
        (6, 2 * WIDTH, qv_out),
        (8, WIDTH, proj_b_out),
        (9, 4 * WIDTH, fc1_b_out),
        (13, WIDTH, fc2_b_out),
    ):
        width = size // 32
        line = jnp.concatenate([sums[row + r : row + r + 1, :] for r in range(size // WIDTH)], 1)
        line = jnp.broadcast_to(line, (8, size))
        line = pltpu.roll(line, (size - bucket * width) % size, 1)
        dst[...] = line[0, 0:width]
    for copy in copies:
        copy.wait()


def finish_call(*args):
    shape = jax.ShapeDtypeStruct
    sizes = [
        (ROWS, WIDTH),
        (ROWS, WIDTH),
        (1, WIDTH),
        (32, 6 * WIDTH),
        (6 * WIDTH // 32,),
        (32, 3 * WIDTH),
        (2 * WIDTH // 32,),
        (32, WIDTH),
        (WIDTH // 32,),
        (32, 4 * WIDTH),
        (4 * WIDTH // 32,),
        (128, WIDTH),
        (WIDTH // 32,),
    ]
    spread = (0, 1, 3)
    return pl.pallas_call(
        finish_kernel,
        out_shape=[shape(size, F32) for size in sizes],
        in_specs=[ANY, ANY, VMEM, ANY] + [VMEM] * 3,
        out_specs=[ANY if k in spread else VMEM for k in range(len(sizes))],
        scratch_shapes=[
            pltpu.VMEM((ROWS, WIDTH), F32),
            pltpu.VMEM((ROWS, WIDTH), F32),
            pltpu.VMEM((32, 6 * WIDTH), F32),
            pltpu.SemaphoreType.DMA((6,)),
        ],
        compiler_params=pltpu.CompilerParams(vmem_limit_bytes=62 << 20),
        name="finish",
    )(*args)


def run_attend(tokens, condition, lengths, head_mask, ada_weight, ada_bias, qkv_weight, qv_bias):
    return attend(
        tokens[0],
        condition,
        lengths,
        head_mask,
        ada_weight,
        ada_bias,
        qkv_weight,
        qv_bias,
    )


def local(
    tokens,
    condition,
    lengths,
    head_mask,
    group_mask,
    token_mask,
    ada_weight,
    ada_bias,
    qkv_weight,
    qv_bias,
    proj_weight,
    proj_bias,
    fc1_weight,
    fc1_bias,
    fc2_weight,
    fc2_bias,
    out_grad,
):
    mods, attended, queries, values, kt, ot, inv, normed, plain, powers = run_attend(
        tokens, condition, lengths, head_mask, ada_weight, ada_bias, qkv_weight, qv_bias
    )
    block_out, input_grad, cond, ada, sums, fin, fin_q = middle_call(
        tokens[0],
        out_grad[0],
        condition,
        mods,
        lengths,
        head_mask,
        group_mask,
        token_mask,
        proj_bias,
        fc1_bias,
        fc2_bias,
        attended,
        proj_weight,
        fc1_weight,
        fc2_weight,
        qkv_weight,
        queries,
        values,
        kt,
        ot,
        inv,
        normed,
        plain,
        ada_weight,
        powers,
    )
    results = finish_call(block_out, input_grad, cond, ada, sums, fin, fin_q)
    return (results[0][None], results[1][None]) + tuple(results[2:])


def solution(mesh):
    return jax.shard_map(
        local,
        mesh=mesh,
        in_specs=(
            P("bucket", "seq", None),
            P("bucket", None),
            P("bucket", None),
            P("bucket", None),
            P("bucket", None),
            P("bucket", "seq"),
            P(),
            P(),
            P(),
            P(),
            P(),
            P(),
            P(),
            P(),
            P(),
            P(),
            P("bucket", "seq", None),
        ),
        out_specs=(
            P("bucket", "seq", None),
            P("bucket", "seq", None),
            P("bucket", None),
            P("bucket", None),
            P("bucket"),
            P("bucket", None),
            P("bucket"),
            P("bucket", None),
            P("bucket"),
            P("bucket", None),
            P("bucket"),
            P("bucket", None),
            P("bucket"),
        ),
        check_vma=False,
    )
```

```python
import functools

import jax
import jax.numpy as jnp
from jax import lax
from jax.experimental import pallas as pl
from jax.experimental.pallas import tpu as pltpu
from jax.sharding import PartitionSpec as P


MESH_IDS = pl.DeviceIdType.MESH
AXES = {"x": 0, "y": 1, "z": 2}


def place():
    bucket = lax.axis_index("bucket")
    seq = lax.axis_index("seq")
    return (
        (seq // 2) * 2 + (bucket // 4) % 2,
        bucket % 4,
        bucket // 8,
        seq % 2,
    )


def device(x, y, z, core):
    return (z * 8 + (x % 2) * 4 + y, (x // 2) * 2 + core)


def shifted(spot, axis, step):
    x, y, z, core = spot
    if axis == "x":
        x = (x + step) % 4
    elif axis == "y":
        y = (y + step) % 4
    elif axis == "z":
        z = (z + step) % 4
    elif axis == "l":
        x = (x // 2) * 2 + 1 - x % 2
    elif axis == "ly":
        x = (x // 2) * 2 + 1 - x % 2
        y = (y + step) % 4
    return device(x, y, z, core)


TORUS = [(axis, step) for axis in "xyz" for step in (1, -1)]


def add_into(target, others):
    total = target[...].astype(jnp.float32)
    for other in others:
        total = total + other[...].astype(jnp.float32)
    target[...] = total.astype(jnp.bfloat16)


class Piece:
    def __init__(self, source, columns, route, landing, send_sem, recv_sem, spot):
        self.source, self.columns, self.route = source, columns, route
        self.landing = landing
        self.send_sem, self.recv_sem, self.spot = send_sem, recv_sem, spot
        self.copies, self.done = {}, []

    @staticmethod
    def dims(route, phase, columns):
        done = route[: phase + 1]
        out = []
        if "z" not in done:
            out.append(4)
        if "x" not in done and "l" not in done:
            out.append(2)
        if "y" not in done:
            out.append(4)
        if "l" in route:
            return tuple(out) + (16, columns)
        if "x" not in done:
            out.append(2)
        return tuple(out) + (16, columns // 2)

    def block(self, phase, target, half):
        done, axis = self.route[:phase], self.route[phase]
        split = "l" in self.route
        index = []
        if "z" not in done:
            index.append(target if axis == "z" else slice(None))
        if "x" not in done and "l" not in done:
            index.append(
                target % 2 if axis == "x" else target if axis == "l" else slice(None)
            )
        if "y" not in done:
            index.append(target if axis == "y" else slice(None))
        if phase == 0:
            if split:
                return self.source.at[tuple(index) + (half,)]
            index.append(target // 2 if axis == "x" else slice(None))
            width = self.columns // 2
            lanes = pl.ds(half * width, width)
            return self.source.at[tuple(index) + (slice(None), lanes)]
        if not split and "x" not in done:
            index.append(target // 2 if axis == "x" else slice(None))
        return self.landing[phase - 1].at[(3 - half,) + tuple(index)]

    def here(self, phase):
        if self.route[phase] == "l":
            return self.spot[0] % 2
        return self.spot[AXES[self.route[phase]]]

    def send(self, phase, slot, ref, step):
        copy = pltpu.make_async_remote_copy(
            src_ref=ref,
            dst_ref=self.landing[phase].at[slot],
            send_sem=self.send_sem.at[phase, slot],
            recv_sem=self.recv_sem.at[phase, slot],
            device_id=shifted(self.spot, self.route[phase], step),
            device_id_type=MESH_IDS,
        )
        copy.start()
        self.copies[phase, slot] = copy

    def first(self, phase):
        a = self.here(phase)
        if self.route[phase] == "l":
            self.send(phase, 2, self.block(phase, 1 - a, 1), 1)
            self.send(phase, 3, self.block(phase, 1 - a, 0), 1)
            return
        if phase > 0:
            for step, slots in ((1, (0, 1)), (-1, (3, 2)), (2, (4, 5))):
                for half in range(2):
                    self.send(phase, slots[half], self.block(phase, (a + step) % 4, half), step)
            return
        self.send(phase, 0, self.block(phase, (a + 2) % 4, 0), 1)
        self.send(phase, 1, self.block(phase, (a + 2) % 4, 1), -1)
        self.send(phase, 2, self.block(phase, (a + 1) % 4, 1), 1)
        self.send(phase, 3, self.block(phase, (a + 3) % 4, 0), -1)

    def second(self, phase):
        if phase > 0:
            return
        a = self.here(phase)
        landing = self.landing[phase]
        for slot, step, half in ((0, 1, 0), (1, -1, 1)):
            self.copies[phase, slot].wait_recv()
            add_into(landing.at[slot], [self.block(phase, (a + step) % 4, half)])
            self.send(phase, slot + 4, landing.at[slot], step)

    def third(self, phase):
        a = self.here(phase)
        landing = self.landing[phase]
        for half, slot, others in ((0, 3, (4, 0)), (1, 2, (5, 1))):
            self.copies[phase, slot].wait_recv()
            terms = [self.block(phase, a, half)]
            if self.route[phase] == "l":
                others = ()
            elif phase == 0:
                others = others[:1]
            for other in others:
                self.copies[phase, other].wait_recv()
                terms.append(landing.at[other])
            add_into(landing.at[slot], terms)

    def result(self, half):
        return self.landing[-1].at[3 - half]

    def sent(self, phase):
        for slot in range(4):
            self.copies[phase, slot].wait_send()
            self.done.append((phase, slot))

    def finish(self):
        for key, copy in self.copies.items():
            if key not in self.done:
                copy.wait_send()


BF = jnp.bfloat16
F32 = jnp.float32
VMEM = pl.BlockSpec(memory_space=pltpu.VMEM)
SMEM = pl.BlockSpec(memory_space=pltpu.SMEM)
ANY = pl.BlockSpec(memory_space=pl.ANY)
NT = (((1,), (1,)), ((), ()))
TN = (((0,), (0,)), ((), ()))
WIDTH = 1024
ROWS = 256
HEAD = 64
MINE = 256


def dot(a, b):
    return jnp.dot(a, b, preferred_element_type=F32)


def dot_nt(a, b):
    return lax.dot_general(a, b, NT, preferred_element_type=F32)


def dot_tn(a, b):
    return lax.dot_general(a, b, TN, preferred_element_type=F32)


def down(op, values):
    while values.shape[0] > 8:
        size = values.shape[0] // 2
        values = op(values[:size], values[size:])
    return values


def lanes_at(start, size):
    return pl.ds(pl.multiple_of(start, 128), size)


def block_rows(index):
    return pl.ds(pl.multiple_of(index * ROWS, ROWS), ROWS)


def norm_parts(values):
    centred = values - jnp.mean(values, axis=-1, keepdims=True)
    rate = lax.rsqrt(jnp.mean(centred * centred, axis=-1, keepdims=True) + 1e-06)
    return centred * rate, rate


def norm_back(normed, rate, grad):
    inner = jnp.mean(grad * normed, axis=-1, keepdims=True)
    return (grad - jnp.mean(grad, axis=-1, keepdims=True) - normed * inner) * rate


def segment(positions, lengths):
    first = lengths[0, 0]
    both = lengths[0, 0] + lengths[0, 1]
    return (positions >= first).astype(jnp.int32) + (positions >= both).astype(jnp.int32)


def quad(spot):
    x, _, _, core = spot
    high = x // 2
    own = high * 2 + core
    pair = high * 2 + (1 - core)
    far = (1 - high) * 2 + core
    cross = (1 - high) * 2 + (1 - core)
    return own, pair, far, cross


def partner(spot, which):
    x, y, z, core = spot
    if which == "pair":
        return device(x, y, z, 1 - core)
    if which == "far":
        return device((x + 2) % 4, y, z, core)
    return device((x + 2) % 4, y, z, 1 - core)


def greet_all(spot, moves, partners):
    barrier = pltpu.get_barrier_semaphore()
    for axis, step in moves:
        pl.semaphore_signal(
            barrier, inc=1, device_id=shifted(spot, axis, step), device_id_type=MESH_IDS
        )
    for which in partners:
        pl.semaphore_signal(barrier, inc=1, device_id=partner(spot, which), device_id_type=MESH_IDS)
    pl.semaphore_wait(barrier, len(moves) + len(partners))


class Mail:
    def __init__(self, spot, send_sem, recv_sem):
        self.spot, self.send_sem, self.recv_sem = spot, send_sem, recv_sem
        self.copies, self.done = [], []

    def send(self, src, dst, which):
        return self.send_to(src, dst, partner(self.spot, which))

    def send_ring(self, src, dst, axis, step):
        return self.send_to(src, dst, shifted(self.spot, axis, step))

    def send_to(self, src, dst, target):
        k = len(self.copies)
        copy = pltpu.make_async_remote_copy(
            src_ref=src,
            dst_ref=dst,
            send_sem=self.send_sem.at[k],
            recv_sem=self.recv_sem.at[k],
            device_id=target,
            device_id_type=MESH_IDS,
        )
        copy.start()
        self.copies.append(copy)
        return copy

    def sent(self, copy):
        copy.wait_send()
        self.done.append(copy)

    def finish(self):
        for copy in self.copies:
            if not any(copy is other for other in self.done):
                copy.wait_send()


def attend_kernel(
    tokens,
    condition,
    lengths,
    head_mask,
    ada_weight,
    ada_bias,
    qkv_weight,
    qv_bias,
    mods,
    attended,
    q_out,
    v_out,
    kt_out,
    ot_out,
    inv_out,
    normed_hbm,
    plain_hbm,
    e_out,
    ada,
    weight,
    everyone,
    k_aug,
    vt,
    ctx_t,
    ctx_send,
    ctx_recv,
    e_all,
    s_buf,
    normed_out,
    plain_out,
    load_sem,
    out_sem,
    send_sem,
    recv_sem,
):
    spot = place()
    own, pair, far, cross = quad(spot)
    loads = []
    for j in range(6):
        loads.append(
            pltpu.make_async_copy(
                ada_weight.at[:, pl.ds(j * WIDTH, WIDTH)], ada.at[j], load_sem.at[j]
            )
        )
    for j in range(3):
        start = pl.multiple_of(j * WIDTH + own * MINE, MINE)
        loads.append(
            pltpu.make_async_copy(
                qkv_weight.at[:, pl.ds(start, MINE)],
                weight.at[:, pl.ds(j * MINE, MINE)],
                load_sem.at[6 + j],
            )
        )
    for copy in loads:
        copy.start()
    greet_all(spot, [], ("pair", "far", "cross"))
    mail = Mail(spot, send_sem, recv_sem)
    half = ROWS // 2
    to_far = [
        mail.send(
            tokens.at[pl.ds(i * half, half)], everyone.at[own, pl.ds(i * half, half)], "far"
        )
        for i in range(2)
    ]
    to_pair = mail.send(tokens, everyone.at[own], "pair")

    value = condition[...].astype(F32)
    silu_low = (value / (1.0 + jnp.exp(-value))).astype(BF)
    silu_rows = jnp.broadcast_to(silu_low, (16, WIDTH))
    for j in range(6):
        loads[j].wait()
        row = dot(silu_rows, ada[j])[0:1]
        mods[pl.ds(j, 1), :] = row + ada_bias[pl.ds(j * WIDTH, WIDTH)].astype(F32).reshape(1, WIDTH)
    for copy in loads[6:]:
        copy.wait()

    shift, scale = mods[0:1, :], 1.0 + mods[1:2, :]
    mine = pl.multiple_of(own * MINE, MINE)
    q_bias = qv_bias[pl.ds(mine, MINE)].astype(F32).reshape(1, MINE)
    v_bias = qv_bias[pl.ds(WIDTH + mine, MINE)].astype(F32).reshape(1, MINE)
    lane = lax.broadcasted_iota(jnp.int32, (ROWS, 128), 1)

    def project(block, rows):
        plain = norm_parts(rows[...].astype(F32))[0]
        normed = (plain * scale + shift).astype(BF)
        here = pl.ds(pl.multiple_of(block * ROWS, ROWS), ROWS)
        plain_out[here, :] = plain.astype(BF)
        normed_out[here, :] = normed
        projected = dot(normed, weight[...])
        q_out[here, :] = ((projected[:, :MINE] + q_bias).astype(BF) * 0.125).astype(BF)
        keys = projected[:, MINE : 2 * MINE].astype(BF)
        values = (projected[:, 2 * MINE :] + v_bias).astype(BF)
        spots = segment(block * ROWS + lax.broadcasted_iota(jnp.int32, (ROWS, 128), 0), lengths)
        marks = jnp.where(spots == lane, 1.0, 0.0).astype(BF)
        for p in range(2):
            k_aug[p, here, pl.ds(0, 128)] = keys[:, p * 128 : (p + 1) * 128]
            k_aug[p, here, pl.ds(128, 128)] = marks
        v_out[here, :] = values
        kt_out[:, here] = keys.T
        vt[:, here] = values.T

    project(own, tokens)
    to_pair.wait_recv()
    project(pair, everyone.at[pair])
    forwards = []
    for i in range(2):
        to_far[i].wait_recv()
        piece = everyone.at[far, pl.ds(i * half, half)]
        forwards.append(mail.send(piece, piece, "pair"))
    project(far, everyone.at[far])
    for copy in forwards:
        copy.wait_recv()
    project(cross, everyone.at[cross])

    lanes = lax.broadcasted_iota(jnp.int32, (ROWS, 256), 1)
    order = ((cross, "cross"), (far, "far"), (pair, "pair"), (own, None))
    out_copies, sends, tops, inverses = [], [], {}, {}
    for k, (src, dst) in enumerate(((normed_out, normed_hbm), (plain_out, plain_hbm))):
        copy = pltpu.make_async_copy(src, dst, out_sem.at[4 + k])
        copy.start()
        out_copies.append(copy)

    def score(i):
        n, h = i // 4, i % 4
        block, p = order[n][0], h // 2
        spots = segment(block * ROWS + lax.broadcasted_iota(jnp.int32, (ROWS, 128), 0), lengths)
        marks = jnp.where((spots != lane) & (lane < 3), -1e30, 0.0).astype(BF)
        queries = q_out[block_rows(block), p * 128 : (p + 1) * 128]
        both = jnp.concatenate([queries, marks], axis=1)
        keep = (lanes // HEAD == h % 2) | (lanes >= 128)
        scores = dot_nt(k_aug[p], jnp.where(keep, both, jnp.zeros_like(both)))
        s_buf[i % 2] = scores
        tops[i] = jnp.max(down(jnp.maximum, scores), axis=0, keepdims=True)

    def soften(i):
        n, h = i // 4, i % 4
        powers = jnp.exp(s_buf[i % 2] - tops[i])
        e_all[:, i * ROWS : (i + 1) * ROWS] = powers.astype(BF)
        inverses[i] = 1.0 / jnp.sum(down(jnp.add, powers), axis=0, keepdims=True)
        inv_out[h, :, block_rows(order[n][0])] = inverses[i]

    def apply(i):
        n, h = i // 4, i % 4
        block, which = order[n]
        part = slice(h * HEAD, (h + 1) * HEAD)
        out = dot(vt[part, :], e_all[:, i * ROWS : (i + 1) * ROWS]) * inverses[i]
        ot_out[part, block_rows(block)] = out.astype(BF)
        ctx_t[n % 2, part, :] = out * head_mask[0, own * 4 + h].astype(F32)
        if h < 3:
            return
        ctx = ctx_t[n % 2].T.astype(BF)
        if which is None:
            ctx_recv[own] = ctx
        else:
            ctx_send[n] = ctx
            sends.append(mail.send(ctx_send.at[n], ctx_recv.at[own], which))
        wide = pl.ds(pl.multiple_of(block * 4 * ROWS, ROWS), 4 * ROWS)
        copy = pltpu.make_async_copy(
            e_all.at[:, pl.ds(n * 4 * ROWS, 4 * ROWS)], e_out.at[:, wide], out_sem.at[n]
        )
        copy.start()
        out_copies.append(copy)

    score(0)
    for i in range(16):
        if i > 0:
            apply(i - 1)
        if i < 15:
            score(i + 1)
        soften(i)
    apply(15)
    for copy in sends:
        copy.wait_recv()
    for s in range(4):
        attended[:, pl.ds(s * MINE, MINE)] = ctx_recv[s]
    for copy in out_copies:
        copy.wait()
    mail.finish()


def attend(
    tokens, condition, lengths, head_mask, ada_weight, ada_bias, qkv_weight, qv_bias
):
    shape = jax.ShapeDtypeStruct
    row = 4 * ROWS
    return pl.pallas_call(
        attend_kernel,
        out_shape=[
            shape((8, WIDTH), F32),
            shape((ROWS, WIDTH), BF),
            shape((row, MINE), BF),
            shape((row, MINE), BF),
            shape((MINE, row), BF),
            shape((MINE, row), BF),
            shape((4, 1, row), F32),
            shape((row, WIDTH), BF),
            shape((row, WIDTH), BF),
            shape((row, 4 * row), BF),
        ],
        in_specs=[VMEM, VMEM, SMEM, SMEM, ANY, VMEM, ANY, VMEM],
        out_specs=[VMEM] * 7 + [ANY] * 3,
        scratch_shapes=[
            pltpu.VMEM((6, WIDTH, WIDTH), BF),
            pltpu.VMEM((WIDTH, 3 * MINE), BF),
            pltpu.VMEM((4, ROWS, WIDTH), BF),
            pltpu.VMEM((2, row, 256), BF),
            pltpu.VMEM((MINE, row), BF),
            pltpu.VMEM((2, MINE, ROWS), F32),
            pltpu.VMEM((3, ROWS, MINE), BF),
            pltpu.VMEM((4, ROWS, MINE), BF),
            pltpu.VMEM((row, 4 * row), BF),
            pltpu.VMEM((2, row, ROWS), F32),
            pltpu.VMEM((row, WIDTH), BF),
            pltpu.VMEM((row, WIDTH), BF),
            pltpu.SemaphoreType.DMA((9,)),
            pltpu.SemaphoreType.DMA((6,)),
            pltpu.SemaphoreType.DMA((8,)),
            pltpu.SemaphoreType.DMA((8,)),
        ],
        compiler_params=pltpu.CompilerParams(
            collective_id=2, has_side_effects=True, vmem_limit_bytes=60 << 20
        ),
        name="attend",
    )(tokens, condition, lengths, head_mask, ada_weight, ada_bias, qkv_weight, qv_bias)


ROUTE_OF = ("zyx", "yxz", "xzy", "zyx", "yxz", "xzy", "zyx", "yxz", "zyl", "yzl")
COLUMNS_OF = (768, 768, 512, 768, 768, 512, 256, 256, 384, 384)
PIECES = len(COLUMNS_OF)
FC_PIECES = PIECES - 2
FC_COLUMNS = sum(COLUMNS_OF[:FC_PIECES])
FC2_UNITS = ((0, 0), (0, 1), (1, 0), (1, 1), (2, 0), (2, 1), (3, 0), (3, 1))


def middle_kernel(
    tokens,
    out_grad,
    condition,
    mods,
    lengths,
    head_mask,
    group_mask,
    token_mask,
    proj_bias,
    fc1_bias,
    fc2_bias,
    attended,
    proj_weight,
    fc1_weight,
    fc2_weight,
    qkv_weight,
    q_in,
    v_in,
    kt_in,
    ot_in,
    inv_in,
    normed_in,
    plain_in,
    ada_weight,
    e_in,
    block_out,
    input_grad,
    cond_grad,
    ada_out,
    sums_out,
    fin_out,
    fin_q_out,
    proj_w,
    fc1_w,
    fc2_w,
    att,
    normed_two,
    big,
    mlp_grad,
    branch_cols,
    middle,
    branch,
    part_send,
    part_recv,
    channel,
    ot,
    inv,
    do_recv,
    dq_t,
    dk,
    dv,
    n_recv,
    fin,
    fin_q,
    vec,
    share,
    low_vec,
    everyone,
    load_sem,
    out_sem,
    mail_send,
    mail_recv,
    piece_send,
    piece_recv,
    *piece_refs,
):
    spot = place()
    core, high = spot[3], spot[0] // 2
    own, pair, far, cross = quad(spot)
    half_ff = 2 * WIDTH

    def load(k, src, dst):
        copy = pltpu.make_async_copy(src, dst, load_sem.at[k])
        copy.start()
        return copy

    here, there = block_rows(core), block_rows(1 - core)
    load_att = load(0, attended, att.at[here])
    load_proj = load(1, proj_weight, proj_w)
    load_fc1 = load(2, fc1_weight.at[:, lanes_at(core * half_ff, half_ff)], fc1_w)
    load_fc2 = load(
        3, fc2_weight.at[pl.ds(pl.multiple_of(core * half_ff, 256), half_ff), :], fc2_w
    )
    load_heads = [load(5, ot_in, ot), load(6, inv_in, inv)]
    greet_all(spot, TORUS + [("y", 2), ("z", 2), ("ly", 1), ("ly", -1), ("ly", 2)], ("pair", "far", "cross"))
    mail = Mail(spot, mail_send, mail_recv)
    pieces = []
    for k in range(PIECES):
        refs = piece_refs[3 * k : 3 * k + 3]
        if k < FC_PIECES:
            source = piece_refs[3 * PIECES + k]
        else:
            source = pieces[0].source.at[..., pl.ds((k - FC_PIECES) * 384, 384)]
        pieces.append(
            Piece(
                source,
                COLUMNS_OF[k],
                ROUTE_OF[k],
                refs,
                piece_send.at[k],
                piece_recv.at[k],
                spot,
            )
        )
    fc2_p, fc1_p, proj_p, qkv_p = pieces[0:3], pieces[3:6], pieces[6:8], pieces[8:10]

    def first(group, phase):
        for piece in group:
            piece.first(phase)

    def second(group, phase):
        for piece in group:
            piece.second(phase)

    def third(group, phase):
        for piece in group:
            piece.third(phase)
            if phase < 2:
                piece.first(phase + 1)

    shift_two, scale_two = mods[3:4, :], 1.0 + mods[4:5, :]
    gate_one, gate_two = mods[2:3, :], mods[5:6, :]
    position = own * ROWS + lax.broadcasted_iota(jnp.int32, (ROWS, 1), 0)
    valid = (position < lengths[0, 0] + lengths[0, 1]).astype(F32)
    kept = valid * jnp.broadcast_to(token_mask[...].astype(F32), (8, ROWS)).T[:, 0:1]
    for g in range(8):
        channel[:, pl.ds(g * 256, 256)] = jnp.full(
            (1, 256), group_mask[0, core * 8 + g].astype(F32), F32
        )
    vec[...] = jnp.zeros_like(vec)

    upstream = out_grad[...].astype(F32)
    low_grad = (kept * gate_two * upstream).astype(BF)
    mlp_grad[here, :] = low_grad
    vec[13:14, :] = jnp.sum(low_grad.astype(F32), axis=0, keepdims=True)
    got_grad = mail.send(mlp_grad.at[here], mlp_grad.at[here], "pair")
    load_att.wait()
    got_att = mail.send(att.at[here], att.at[here], "pair")
    load_proj.wait()
    fresh = dot(att[here, :], proj_w[...]) + proj_bias[...].astype(F32).reshape(1, WIDTH)
    branch[...] = fresh.astype(BF)
    mid = tokens[...].astype(F32) + valid * gate_one * fresh
    middle[...] = mid
    normed_two[here, :] = (norm_parts(mid)[0] * scale_two + shift_two).astype(BF)
    got_normed = mail.send(normed_two.at[here], normed_two.at[here], "pair")
    load_fc1.wait()
    mine = lanes_at(core * half_ff, half_ff)
    TILE = 512

    def hidden(rows):
        def body(i, carry):
            cols = lanes_at(i * TILE, TILE)
            wide = lanes_at(core * half_ff + i * TILE, TILE)
            u = dot(normed_two[rows, :], fc1_w[:, cols]) + fc1_bias[wide].astype(F32).reshape(1, TILE)
            square = u * u
            t = jnp.tanh(0.7978845608028654 * u * (1.0 + 0.044715 * square))
            up = 0.5 * (1.0 + t)
            mask = channel[:, cols]
            big[rows, wide] = (u * up * mask).astype(BF)
            slope = up + 0.5 * u * (1.0 - t * t) * (
                0.7978845608028654 + (3 * 0.7978845608028654 * 0.044715) * square
            )
            low = pl.ds(pl.multiple_of(2 * ROWS + rows.start, ROWS), ROWS)
            big[low, cols] = (slope * mask).astype(BF)
            return carry

        lax.fori_loop(0, half_ff // TILE, body, 0, unroll=True)

    hidden(here)
    got_act = [mail.send(big.at[here, mine], big.at[here, mine], "pair")]
    got_normed.wait_recv()
    hidden(there)
    got_act.append(mail.send(big.at[there, mine], big.at[there, mine], "pair"))
    load_fc2.wait()
    part_send[0] = dot(big[there, mine], fc2_w[...]).astype(BF)
    got_part = mail.send(part_send.at[0], part_recv.at[0], "pair")
    mlp_out = dot(big[here, mine], fc2_w[...]) + fc2_bias[...].astype(F32).reshape(1, WIDTH)
    got_part.wait_recv()
    mlp_out = mlp_out + part_recv[0].astype(F32)

    def stage(result, target):
        copies = []
        for s in range(4):
            cols = pl.ds(s * MINE, MINE)
            dk[s * ROWS : (s + 1) * ROWS, :] = result[:, s * MINE : (s + 1) * MINE]
            copies.append(
                pltpu.make_async_copy(
                    dk.at[pl.ds(s * ROWS, ROWS)], target.at[:, cols], out_sem.at[s]
                )
            )
            copies[s].start()
        return copies

    out_copies = stage(middle[...] + kept * gate_two * mlp_out, block_out)
    vec[5:6, :] = jnp.sum(kept * mlp_out * upstream, axis=0, keepdims=True)

    got_grad.wait_recv()
    for copy in got_act:
        copy.wait_recv()
    half_cols = lanes_at(core * 512, 512)

    def fc2_tile(i, carry):
        t = dot_tn(big[0 : 2 * ROWS, lanes_at(i * 512, 512)], mlp_grad[:, half_cols])
        t = t.astype(BF).reshape(4, 2, 4, 16, 512)
        z, x_lo = i // 2, i % 2
        fc2_p[0].source[z, x_lo, :, :, :, 0:512] = t[:, :, 0]
        fc2_p[0].source[z, x_lo, :, :, :, 512:768] = t[:, :, 1, :, 0:256]
        fc2_p[1].source[z, x_lo, :, :, :, 0:256] = t[:, :, 1, :, 256:512]
        fc2_p[1].source[z, x_lo, :, :, :, 256:768] = t[:, :, 2]
        fc2_p[2].source[z, x_lo] = t[:, :, 3]
        return carry

    lax.fori_loop(0, 8, fc2_tile, 0)
    first(fc2_p, 0)

    def hidden_grad(i, carry):
        cols = lanes_at(i * TILE, TILE)
        low = pl.ds(pl.multiple_of(i * TILE, TILE), TILE)
        grad = dot_nt(mlp_grad[...], fc2_w[low, :])
        grad = (grad * big[2 * ROWS : 4 * ROWS, cols].astype(F32)).astype(BF)
        big[2 * ROWS : 4 * ROWS, lanes_at(half_ff + i * TILE, TILE)] = grad
        total = jnp.sum(grad.astype(F32), axis=0, keepdims=True)
        row = 9 + 2 * core + i // 2
        vec[pl.ds(row, 1), lanes_at((i % 2) * TILE, TILE)] = total
        return carry

    lax.fori_loop(0, half_ff // TILE, hidden_grad, 0, unroll=True)
    low_rows, low_cols = pl.ds(2 * ROWS, 2 * ROWS), pl.ds(half_ff, half_ff)
    load_qkv = [
        load(
            7 + j,
            qkv_weight.at[:, lanes_at(j * WIDTH + own * MINE, MINE)],
            fc2_w.at[pl.ds(0, WIDTH), pl.ds(j * MINE, MINE)],
        )
        for j in range(3)
    ]
    load_heads.append(load(10, q_in, fc2_w.at[pl.ds(0, WIDTH), pl.ds(768, 256)]))
    load_heads.append(load(11, v_in, fc2_w.at[pl.ds(WIDTH, WIDTH), pl.ds(768, 256)]))

    def back(rows):
        low = pl.ds(pl.multiple_of(2 * ROWS + rows.start, ROWS), ROWS)
        return dot_nt(big[low, low_cols], fc1_w[...])

    part_send[1] = back(there).astype(BF)
    got_back = mail.send(part_send.at[1], part_recv.at[1], "pair")
    normed_two_grad = back(here)
    second(fc2_p, 0)
    load_normed = load(13, normed_in, fc1_w.at[:, pl.ds(0, WIDTH)])
    got_back.wait_recv()
    normed_two_grad = normed_two_grad + part_recv[1].astype(F32)
    normed_mid, rate = norm_parts(middle[...])
    vec[3:4, :] = jnp.sum(normed_two_grad, axis=0, keepdims=True)
    vec[4:5, :] = jnp.sum(normed_two_grad * normed_mid, axis=0, keepdims=True)
    mid_grad = upstream + norm_back(normed_mid, rate, normed_two_grad * scale_two)
    middle[...] = mid_grad
    vec[2:3, :] = jnp.sum(valid * branch[...].astype(F32) * mid_grad, axis=0, keepdims=True)
    branch_grad = (valid * gate_one * mid_grad).astype(BF)
    vec[8:9, :] = jnp.sum(branch_grad.astype(F32), axis=0, keepdims=True)
    mail.sent(got_back)
    part_send[1] = branch_grad
    branch_cols[here, :] = part_send[1, :, half_cols]
    other_cols = lanes_at((1 - core) * 512, 512)
    got_cols = mail.send(part_send.at[1, :, other_cols], branch_cols.at[here], "pair")
    context_grad = dot_nt(branch_grad, proj_w[...]).astype(BF)
    mail.sent(got_part)
    part_send[0] = context_grad
    got_do = [
        mail.send(
            part_send.at[0, :, lanes_at(block * MINE, MINE)], do_recv.at[own], which
        )
        for block, which in ((cross, "cross"), (far, "far"), (pair, "pair"))
    ]
    do_recv[own] = part_send[0, :, lanes_at(own * MINE, MINE)]

    start = half_ff
    for piece in fc1_p:
        width = piece.columns

        def fc1_tile(i, carry, start=start, width=width, piece=piece):
            t = dot_tn(
                normed_two[:, lanes_at(i * 512, 512)],
                big[2 * ROWS : 4 * ROWS, start : start + width],
            )
            piece.source[pl.ds(i * 2, 2)] = t.astype(BF).reshape(2, 2, 4, 2, 16, width)
            return carry

        lax.fori_loop(0, 2, fc1_tile, 0)
        piece.first(0)
        start += width

    for copy in got_act:
        mail.sent(copy)
    load_e = load(12, e_in, big)

    got_att.wait_recv()
    got_cols.wait_recv()

    def proj_tile(i, carry):
        t = dot_tn(att[:, lanes_at(i * 512, 512)], branch_cols[...])
        t = t.astype(BF).reshape(2, 2, 4, 2, 16, 512)
        proj_p[0].source[pl.ds(i * 2, 2)] = t[..., 0:256]
        proj_p[1].source[pl.ds(i * 2, 2)] = t[..., 256:512]
        return carry

    lax.fori_loop(0, 2, proj_tile, 0)
    first(proj_p, 0)
    third(fc2_p, 0)

    mail.sent(got_att)
    mail.sent(got_cols)
    load_plain = [
        load(14, plain_in.at[block_rows(cross)], att.at[pl.ds(0, ROWS)]),
        load(16, plain_in.at[block_rows(pair)], part_send.at[1]),
    ]
    load_heads.append(load(4, kt_in, att.at[pl.ds(ROWS, ROWS)]))
    for copy in out_copies:
        copy.wait()
    q_wide, do_wide = proj_w.at[:, 0:MINE], proj_w.at[:, MINE : 2 * MINE]
    for copy in load_heads:
        copy.wait()
    load_e.wait()
    load_normed.wait()
    for copy in load_qkv:
        copy.wait()
    for n, block in enumerate((own, pair, far, cross)):
        if n > 0:
            got_do[3 - n].wait_recv()
        rows = block_rows(block)
        lane = lax.broadcasted_iota(jnp.int32, (ROWS, MINE), 1)
        grad_t = do_recv[block].astype(F32).T
        parts, rests = [], []
        for h in range(4):
            factor = inv[h, :, rows] * head_mask[0, own * 4 + h].astype(F32)
            part = (grad_t[h * HEAD : (h + 1) * HEAD] * factor).astype(BF)
            parts.append(part)
            rests.append(
                jnp.sum(
                    part.astype(F32) * ot[h * HEAD : (h + 1) * HEAD, rows].astype(F32),
                    axis=0,
                    keepdims=True,
                )
            )
        grad_low = jnp.concatenate(parts, axis=0)
        grad_rows = grad_low.astype(F32).T.astype(BF)
        queries = fc2_w[rows, 768:1024]
        zero = jnp.zeros((), BF)
        for h in range(4):
            keep = lane // HEAD == h
            q_wide[h * ROWS : (h + 1) * ROWS, :] = jnp.where(keep, queries, zero)
            do_wide[h * ROWS : (h + 1) * ROWS, :] = jnp.where(keep, grad_rows, zero)
        for h in range(4):
            below = lax.broadcasted_iota(jnp.int32, (MINE, ROWS), 0) // HEAD == h
            masked = jnp.where(below, grad_low, zero)
            prob_grad = dot(fc2_w[WIDTH : 2 * WIDTH, 768:1024], masked)
            powers = big[:, lanes_at((block * 4 + h) * ROWS, ROWS)].astype(F32)
            score_grad = (powers * (prob_grad - rests[h])).astype(BF)
            fc1_w[:, WIDTH + h * ROWS : WIDTH + (h + 1) * ROWS] = score_grad
            dq_t[h * HEAD : (h + 1) * HEAD, :] = dot(
                att[ROWS + h * HEAD : ROWS + (h + 1) * HEAD, :], score_grad
            )
        more_k = dot(fc1_w[:, WIDTH : 2 * WIDTH], q_wide[...])
        more_v = dot(big[:, lanes_at(block * 4 * ROWS, 4 * ROWS)], do_wide[...])
        if n == 0:
            dk[...] = more_k
            dv[...] = more_v
        else:
            dk[...] += more_k
            dv[...] += more_v
        row_of = pl.ds(pl.multiple_of(WIDTH + block * ROWS, ROWS), ROWS)
        fc2_w[row_of, 0:MINE] = (dq_t[...].T * 0.125).astype(BF)
        if n == 1:
            for copy in got_do:
                mail.sent(copy)
            load_plain.append(load(15, plain_in.at[block_rows(far)], part_send.at[0]))
        elif n == 2:
            second(fc1_p, 0)
            second(proj_p, 0)
    low = slice(WIDTH, 2 * WIDTH)
    fc2_w[low, MINE : 2 * MINE] = dk[...].astype(BF)
    fc2_w[low, 2 * MINE : 3 * MINE] = dv[...].astype(BF)
    for j, row in ((0, 6), (2, 7)):
        total = jnp.sum(fc2_w[low, j * MINE : (j + 1) * MINE].astype(F32), axis=0, keepdims=True)
        vec[row : row + 1, lanes_at(own * MINE, MINE)] = total

    places = [big.at[:, pl.ds(j * WIDTH, WIDTH)] for j in range(4)]
    places += [proj_w, fc1_w.at[:, pl.ds(WIDTH, WIDTH)]]
    load_ada = [
        load(17 + j, ada_weight.at[:, pl.ds(j * WIDTH, WIDTH)], places[j]) for j in range(6)
    ]
    for copy in load_plain:
        copy.wait()

    def normed_back(block, plain):
        row_of = pl.ds(pl.multiple_of(WIDTH + block * ROWS, ROWS), ROWS)
        grad = dot_nt(fc2_w[row_of, 0:768], fc2_w[0:WIDTH, 0:768])
        vec[0:1, :] += jnp.sum(grad, axis=0, keepdims=True)
        vec[1:2, :] += jnp.sum(grad * plain.astype(F32), axis=0, keepdims=True)
        return grad

    mail.sent(got_normed)
    normed_two[0:ROWS, :] = normed_back(cross, att[0:ROWS, :]).astype(BF)
    got_cross = mail.send(normed_two.at[pl.ds(0, ROWS)], part_recv.at[0], "pair")
    far_part = normed_back(far, part_send[0])
    mail.sent(got_grad)
    mlp_grad[0:ROWS, :] = normed_back(pair, part_send[1]).astype(BF)
    got_pair = mail.send(mlp_grad.at[pl.ds(0, ROWS)], part_recv.at[1], "pair")
    own_part = normed_back(own, norm_parts(tokens[...].astype(F32))[0])
    for s in range(4):
        dv[s * ROWS : (s + 1) * ROWS, :] = own_part[:, s * MINE : (s + 1) * MINE]
    share[own] = vec[...]
    got_vec = [
        mail.send(share.at[own], share.at[own], which) for which in ("pair", "far", "cross")
    ]

    fc2_p[0].sent(0)

    def qkv_tile(i, carry):
        t = dot_tn(fc1_w[:, lanes_at(i * 512, 512)], fc2_w[WIDTH : 2 * WIDTH, 0:768])
        t = t.astype(BF).reshape(2, 2, 4, 2, 16, 768)
        qkv_p[0].source[pl.ds(i * 2, 2)] = t[..., 0:384]
        qkv_p[1].source[pl.ds(i * 2, 2)] = t[..., 384:768]
        return carry

    lax.fori_loop(0, 2, qkv_tile, 0)
    first(qkv_p, 0)
    got_cross.wait_recv()
    normed_two[ROWS : 2 * ROWS, :] = (far_part + part_recv[0].astype(F32)).astype(BF)
    got_far = mail.send(normed_two.at[pl.ds(ROWS, ROWS)], n_recv, "far")
    for copy in got_vec:
        copy.wait_recv()
    total = (share[0] + share[1]) + (share[2] + share[3])
    value = condition[...].astype(F32)
    sigma = 1.0 / (1.0 + jnp.exp(-value))
    row = lax.broadcasted_iota(jnp.int32, (16, WIDTH), 0)
    low = jnp.where(row == 14, value * sigma, total).astype(BF)
    low_vec[...] = low
    x, y, z = spot[0], spot[1], spot[2]
    x_lo = x % 2
    ring_cols = lanes_at(core * 512, 512)
    everyone[z, x_lo, y, :, ring_cols] = low_vec[:, ring_cols]
    mine = everyone.at[z, x_lo, y, :, ring_cols]
    got_near = [
        mail.send_ring(mine, mine, axis, step)
        for axis, step in (("y", 1), ("y", -1), ("y", 2), ("l", 0), ("ly", 1), ("ly", -1), ("ly", 2))
    ]
    second(qkv_p, 0)
    third(fc2_p, 1)
    third(proj_p, 0)
    third(fc1_p, 0)
    for copy in load_ada:
        copy.wait()
    back_cond = jnp.zeros((1, WIDTH), F32)
    for j in range(6):
        back_cond = back_cond + dot_nt(low, places[j][...])[j : j + 1]
    cond_grad[...] = back_cond * (sigma * (1.0 + value * (1.0 - sigma)))
    for copy in got_near:
        copy.wait_recv()
    mine = everyone.at[z, :, :, :, ring_cols]
    got_z = [mail.send_ring(mine, mine, "z", step) for step in (1, -1, 2)]
    got_near = [mail.send(mine, mine, "pair")]
    third(qkv_p, 0)
    third(fc2_p, 2)
    third(proj_p, 1)
    third(fc1_p, 1)

    third(qkv_p, 1)
    third(proj_p, 2)
    third(fc1_p, 2)

    start = 0
    for piece in pieces[:FC_PIECES]:
        width = piece.columns // 2
        for half in range(2):
            fin[high, core, :, start : start + width] = piece.result(half)[...]
            start += width
    to_far = mail.send(fin.at[high, core], fin.at[high, core], "far")
    to_pair = mail.send(fin.at[high, core], fin.at[high, core], "pair")
    for step, copy in zip((1, -1, 2), got_z, strict=True):
        copy.wait_recv()
        mine = everyone.at[(z + 4 - step) % 4, :, :, :, ring_cols]
        got_near.append(mail.send(mine, mine, "pair"))
    third(qkv_p, 2)
    for k, piece in enumerate(qkv_p):
        for half in range(2):
            fin_q[own, half, :, k * 384 : (k + 1) * 384] = piece.result(half)[...]
    got_q = [mail.send(fin_q.at[own], fin_q.at[own], which) for which in ("far", "cross", "pair")]
    to_far.wait_recv()
    to_pair_two = mail.send(fin.at[1 - high, core], fin.at[1 - high, core], "pair")
    got_pair.wait_recv()
    got_far.wait_recv()
    own_part = jnp.concatenate([dv[s * ROWS : (s + 1) * ROWS, :] for s in range(4)], axis=1)
    normed_grad = own_part + n_recv[...].astype(F32) + part_recv[1].astype(F32)
    normed_one, rate_one = norm_parts(tokens[...].astype(F32))
    result = middle[...] + norm_back(normed_one, rate_one, normed_grad * (1.0 + mods[1:2, :]))
    out_copies = stage(result, input_grad)
    for copy in got_near:
        copy.wait_recv()

    bucket = lax.axis_index("bucket")
    window = everyone[:, :, :, :, lanes_at((bucket // 4) * 128, 128)]
    turned = window.reshape(512, 128).astype(F32).T
    quarter = pl.multiple_of((bucket % 4) * 32, 32)
    dv[0:128, :] = turned[:, 0:256]
    dv[128:256, :] = turned[:, 256:512]
    silu = jnp.concatenate([dv[pl.ds(quarter, 32), :], dv[pl.ds(quarter + 128, 32), :]], axis=1)
    lane = lax.broadcasted_iota(jnp.int32, (32, 512), 1)
    silu = jnp.where(lane % 16 == 14, silu, 0.0)
    left = [pltpu.roll(silu, 512 + j - 14, 1) for j in range(6)]
    pick = lax.broadcasted_iota(jnp.int32, (16, 512), 0)
    lane = lax.broadcasted_iota(jnp.int32, (16, 512), 1)
    left.append(jnp.where(lane % 16 == pick, 1.0, 0.0))
    product = dot(jnp.concatenate(left, axis=0).astype(BF), everyone[...].reshape(512, WIDTH))
    ada_copies = []
    for j in range(6):
        middle[j * 32 : (j + 1) * 32, :] = product[j * 32 : (j + 1) * 32]
        ada_copies.append(
            pltpu.make_async_copy(
                middle.at[pl.ds(j * 32, 32)],
                ada_out.at[:, pl.ds(j * WIDTH, WIDTH)],
                out_sem.at[7 + j],
            )
        )
        ada_copies[j].start()
    sums_out[...] = product[192:208]
    for copy in [to_pair, to_pair_two] + got_q:
        copy.wait_recv()
    last_copies = [
        pltpu.make_async_copy(fin, fin_out, out_sem.at[5]),
        pltpu.make_async_copy(fin_q, fin_q_out, out_sem.at[6]),
    ]
    for copy in last_copies:
        copy.start()
    for copy in last_copies + out_copies + ada_copies:
        copy.wait()
    mail.finish()
    for piece in pieces:
        piece.finish()


def middle_call(*args):
    shape = jax.ShapeDtypeStruct
    row = 4 * ROWS
    piece_scratch = []
    for k in range(PIECES):
        for phase in range(3):
            dims = Piece.dims(ROUTE_OF[k], phase, COLUMNS_OF[k])
            slots = 4 if ROUTE_OF[k][phase] == "l" else 6
            piece_scratch.append(pltpu.VMEM((slots,) + dims, BF))
    for k in range(FC_PIECES):
        piece_scratch.append(pltpu.VMEM((4, 2, 4, 2, 16, COLUMNS_OF[k]), BF))
    scratch = [
        pltpu.VMEM((WIDTH, WIDTH), BF),
        pltpu.VMEM((WIDTH, 2 * WIDTH), BF),
        pltpu.VMEM((2 * WIDTH, WIDTH), BF),
        pltpu.VMEM((2 * ROWS, WIDTH), BF),
        pltpu.VMEM((2 * ROWS, WIDTH), BF),
        pltpu.VMEM((row, 4 * row), BF),
        pltpu.VMEM((2 * ROWS, WIDTH), BF),
        pltpu.VMEM((2 * ROWS, WIDTH // 2), BF),
        pltpu.VMEM((ROWS, WIDTH), F32),
        pltpu.VMEM((ROWS, WIDTH), BF),
        pltpu.VMEM((2, ROWS, WIDTH), BF),
        pltpu.VMEM((2, ROWS, WIDTH), BF),
        pltpu.VMEM((1, 2 * WIDTH), F32),
        pltpu.VMEM((MINE, row), BF),
        pltpu.VMEM((4, 1, row), F32),
        pltpu.VMEM((4, ROWS, MINE), BF),
        pltpu.VMEM((MINE, ROWS), F32),
        pltpu.VMEM((row, MINE), F32),
        pltpu.VMEM((row, MINE), F32),
        pltpu.VMEM((ROWS, WIDTH), BF),
        pltpu.VMEM((2, 2, 16, FC_COLUMNS), BF),
        pltpu.VMEM((4, 2, 16, 768), BF),
        pltpu.VMEM((16, WIDTH), F32),
        pltpu.VMEM((4, 16, WIDTH), F32),
        pltpu.VMEM((16, WIDTH), BF),
        pltpu.VMEM((4, 2, 4, 16, WIDTH), BF),
        pltpu.SemaphoreType.DMA((23,)),
        pltpu.SemaphoreType.DMA((13,)),
        pltpu.SemaphoreType.DMA((40,)),
        pltpu.SemaphoreType.DMA((40,)),
        pltpu.SemaphoreType.DMA((PIECES, 3, 6)),
        pltpu.SemaphoreType.DMA((PIECES, 3, 6)),
    ] + piece_scratch
    return pl.pallas_call(
        middle_kernel,
        out_shape=[
            shape((ROWS, WIDTH), F32),
            shape((ROWS, WIDTH), F32),
            shape((1, WIDTH), F32),
            shape((32, 6 * WIDTH), F32),
            shape((16, WIDTH), F32),
            shape((2, 2, 16, FC_COLUMNS), BF),
            shape((4, 2, 16, 768), BF),
        ],
        in_specs=[VMEM] * 4 + [SMEM] * 3 + [VMEM] * 4 + [ANY] * 14,
        out_specs=[ANY, ANY, VMEM, ANY, VMEM, ANY, ANY],
        scratch_shapes=scratch,
        compiler_params=pltpu.CompilerParams(
            collective_id=3, has_side_effects=True, vmem_limit_bytes=63 << 20
        ),
        name="middle",
    )(*args)


def finish_kernel(
    block_in,
    input_in,
    cond_in,
    ada_in,
    sums,
    fin,
    fin_q,
    block_out,
    input_out,
    cond_out,
    ada_out,
    ada_b_out,
    qkv_out,
    qv_out,
    proj_out,
    proj_b_out,
    fc1_out,
    fc1_b_out,
    fc2_out,
    fc2_b_out,
    block_mid,
    input_mid,
    ada_mid,
    sem,
):
    passing = (
        (block_in, block_mid, block_out),
        (input_in, input_mid, input_out),
        (ada_in, ada_mid, ada_out),
    )
    arriving = [
        pltpu.make_async_copy(src, mid, sem.at[k]) for k, (src, mid, _) in enumerate(passing)
    ]
    copies = [
        pltpu.make_async_copy(mid, dst, sem.at[3 + k]) for k, (_, mid, dst) in enumerate(passing)
    ]
    for copy in arriving:
        copy.start()
    cond_out[...] = cond_in[...]
    for h in range(2):
        rows = slice(h * 16, (h + 1) * 16)
        for c in range(2):
            start = 0
            for q, half in FC2_UNITS:
                row = h * 64 + q * 16
                col = c * 512 + half * 256
                fc2_out[row : row + 16, col : col + 256] = fin[h, c, :, start : start + 256].astype(
                    F32
                )
                start += 256
            fc1_out[rows, c * 2 * WIDTH : (c + 1) * 2 * WIDTH] = fin[
                h, c, :, start : start + 2 * WIDTH
            ].astype(F32)
            start += 2 * WIDTH
            proj_out[rows, c * 512 : (c + 1) * 512] = fin[h, c, :, start : start + 512].astype(F32)
        for s in range(4):
            for j in range(3):
                col = j * WIDTH + s * MINE
                qkv_out[rows, col : col + MINE] = fin_q[s, h, :, j * MINE : (j + 1) * MINE].astype(
                    F32
                )
    for here, there in zip(arriving, copies, strict=True):
        here.wait()
        there.start()
    bucket = lax.axis_index("bucket")
    for row, size, dst in (
        (0, 6 * WIDTH, ada_b_out),
        (6, 2 * WIDTH, qv_out),
        (8, WIDTH, proj_b_out),
        (9, 4 * WIDTH, fc1_b_out),
        (13, WIDTH, fc2_b_out),
    ):
        width = size // 32
        line = jnp.concatenate([sums[row + r : row + r + 1, :] for r in range(size // WIDTH)], 1)
        line = jnp.broadcast_to(line, (8, size))
        line = pltpu.roll(line, (size - bucket * width) % size, 1)
        dst[...] = line[0, 0:width]
    for copy in copies:
        copy.wait()


def finish_call(*args):
    shape = jax.ShapeDtypeStruct
    sizes = [
        (ROWS, WIDTH),
        (ROWS, WIDTH),
        (1, WIDTH),
        (32, 6 * WIDTH),
        (6 * WIDTH // 32,),
        (32, 3 * WIDTH),
        (2 * WIDTH // 32,),
        (32, WIDTH),
        (WIDTH // 32,),
        (32, 4 * WIDTH),
        (4 * WIDTH // 32,),
        (128, WIDTH),
        (WIDTH // 32,),
    ]
    spread = (0, 1, 3)
    return pl.pallas_call(
        finish_kernel,
        out_shape=[shape(size, F32) for size in sizes],
        in_specs=[ANY, ANY, VMEM, ANY] + [VMEM] * 3,
        out_specs=[ANY if k in spread else VMEM for k in range(len(sizes))],
        scratch_shapes=[
            pltpu.VMEM((ROWS, WIDTH), F32),
            pltpu.VMEM((ROWS, WIDTH), F32),
            pltpu.VMEM((32, 6 * WIDTH), F32),
            pltpu.SemaphoreType.DMA((6,)),
        ],
        compiler_params=pltpu.CompilerParams(vmem_limit_bytes=62 << 20),
        name="finish",
    )(*args)


def run_attend(tokens, condition, lengths, head_mask, ada_weight, ada_bias, qkv_weight, qv_bias):
    return attend(
        tokens[0],
        condition,
        lengths,
        head_mask,
        ada_weight,
        ada_bias,
        qkv_weight,
        qv_bias,
    )


def local(
    tokens,
    condition,
    lengths,
    head_mask,
    group_mask,
    token_mask,
    ada_weight,
    ada_bias,
    qkv_weight,
    qv_bias,
    proj_weight,
    proj_bias,
    fc1_weight,
    fc1_bias,
    fc2_weight,
    fc2_bias,
    out_grad,
):
    mods, attended, queries, values, kt, ot, inv, normed, plain, powers = run_attend(
        tokens, condition, lengths, head_mask, ada_weight, ada_bias, qkv_weight, qv_bias
    )
    block_out, input_grad, cond, ada, sums, fin, fin_q = middle_call(
        tokens[0],
        out_grad[0],
        condition,
        mods,
        lengths,
        head_mask,
        group_mask,
        token_mask,
        proj_bias,
        fc1_bias,
        fc2_bias,
        attended,
        proj_weight,
        fc1_weight,
        fc2_weight,
        qkv_weight,
        queries,
        values,
        kt,
        ot,
        inv,
        normed,
        plain,
        ada_weight,
        powers,
    )
    results = finish_call(block_out, input_grad, cond, ada, sums, fin, fin_q)
    return (results[0][None], results[1][None]) + tuple(results[2:])


def solution(mesh):
    return jax.shard_map(
        local,
        mesh=mesh,
        in_specs=(
            P("bucket", "seq", None),
            P("bucket", None),
            P("bucket", None),
            P("bucket", None),
            P("bucket", None),
            P("bucket", "seq"),
            P(),
            P(),
            P(),
            P(),
            P(),
            P(),
            P(),
            P(),
            P(),
            P(),
            P("bucket", "seq", None),
        ),
        out_specs=(
            P("bucket", "seq", None),
            P("bucket", "seq", None),
            P("bucket", None),
            P("bucket", None),
            P("bucket"),
            P("bucket", None),
            P("bucket"),
            P("bucket", None),
            P("bucket"),
            P("bucket", None),
            P("bucket"),
            P("bucket", None),
            P("bucket"),
        ),
        check_vma=False,
    )
```
